128 devices in a mesh: dp: 4 (over y_hi, core), seq: 32 (over y_lo, x, z).
Axes of the slice: x: 4, y: 4 (y_hi: 2, y_lo: 2; y = y_hi * 2 + y_lo), z: 4, core: 2. Of those that a mesh axis runs over, the one named last changes fastest.
Arguments:
- conv_input: bfloat16 [4, 24576, 768], P('dp', 'seq'), may hold values from -6 to 6
- skip_grad: bfloat16 [4, 24576, 768], P('dp', 'seq'), may hold values from -3 to 3
- conv_weight: bfloat16 [5, 768, 768], replicated, may hold values from -0.09375 to 0.09375
- proj_weight: bfloat16 [768, 4608], replicated, may hold values from -1.75 to 1.75
- saved_query: bfloat16 [4, 1536, 1536], P('dp', 'seq'), may hold values from -6 to 6
- saved_key: bfloat16 [4, 1536, 1536], P('dp', 'seq'), may hold values from -6 to 6
- saved_value: bfloat16 [4, 1536, 1536], P('dp', 'seq'), may hold values from -6 to 6
- attn_grad: bfloat16 [4, 1536, 1536], P('dp', 'seq'), may hold values from -144 to 144
Outputs:
- input_grad: bfloat16 [4, 24576, 768], P('dp', 'seq')
- conv_grad: float32 [5, 768, 768], P(None, 'seq')
- proj_grad: float32 [768, 4608], P('seq')
The draws below stay inside these ranges and needn't reach their ends.
All inputs are finite; a program needn't handle non-finite values.
Results may differ from the reference program's by a relative error of at most 0.0084.
Values may be sent and summed in bfloat16 or wider, within the bound.
No kernel may reach another device: no remote copies, remote signals or barrier semaphores. Data moves between devices by JAX's collectives and lax.ppermute only.
A program may use at most 192 MiB of HBM per device.

```python
import jax
import jax.numpy as jnp
from jax import lax

C = 768
HEADS = 8
HD = 192
TAPS = 5
UP = 16
LOSS_SCALE = 32
D = 1536
L = 1536
POS = 24576
BATCH = 4


def base_draw(key, salt):
    sub_key = jax.random.fold_in(key, salt)
    return jnp.clip(jax.random.normal(sub_key, (BATCH, L, D), jnp.float32), -4.5, 4.5)


def draw_saved_query(key, part):
    values = base_draw(key, 1)
    return values.astype(jnp.bfloat16)


def draw_saved_key(key, part):
    values = base_draw(key, 2)
    return values.astype(jnp.bfloat16)


def raised(values, stream_key, source, target, shards_of, factor):
    def block_of(axis_at):
        return (jnp.arange(values.shape[axis_at]) // (values.shape[axis_at] // shards_of)).reshape((-1,) + (1,) * (values.ndim - 1 - axis_at))

    first = jax.random.permutation(stream_key, shards_of)[block_of(target)]
    far = (block_of(target) + shards_of // 2) % shards_of
    return jnp.where((block_of(source) == first) | (block_of(source) == far), factor * values, values)


def level_of(key, dims, shards, smallest, largest):
    gain, own = 1.0, jax.random.fold_in(key, 6)
    for dim, parts in shards:
        heights = jnp.exp(jax.random.uniform(jax.random.fold_in(own, dim), (parts,), jnp.float32, smallest / len(shards), largest / len(shards)))
        gain = gain * jnp.repeat(heights, dims[dim] // parts).reshape([-1 if axis == dim else 1 for axis in range(len(dims))])
    return gain


def centred(key, dims, deviation, limit, split=(), held_as=jnp.bfloat16):
    values = jax.random.normal(key, dims, jnp.float32) * deviation
    if len(split) > 0:
        values = level_of(key, dims, split, -0.22, 0.18) * values
    return jnp.clip(values, min=-limit, max=limit).astype(held_as)


def bell_draw_with(stream_key, dims, width, bound, cuts, heavy, kind=jnp.bfloat16):
    array = width * jax.random.normal(stream_key, dims, jnp.float32)
    if cuts:
        array = array * level_of(stream_key, dims, cuts, -0.22, 0.18)
    return jnp.clip(raised(array, jax.random.fold_in(stream_key, 3), *heavy), -bound, bound).astype(kind)


def setup_inputs(seed: int = 0) -> dict:
    key_list = jax.random.split(jax.random.key(seed), 9)
    return {
        "conv_input": bell_draw_with(key_list[0], (BATCH, POS, C), 1.0, 6.0, ((0, 4), (1, 32)), (1, 2, 32, 2.75)),
        "skip_grad": centred(key_list[1], (BATCH, POS, C), 0.5, 3.0, ((0, 4), (1, 32))),
        "conv_weight": centred(key_list[2], (TAPS, C, C), (TAPS * C) ** -0.5, 0.09375),
        "proj_weight": centred(key_list[3], (C, 3 * D), (C // 64) ** -0.5, 1.75),
        "saved_query": draw_saved_query(jax.random.fold_in(key_list[8], 71), 0),
        "saved_key": draw_saved_key(jax.random.fold_in(key_list[8], 71), 0),
        "saved_value": centred(key_list[6], (BATCH, L, D), 1.0, 6.0, ((0, 4), (1, 32))),
        "attn_grad": centred(key_list[7], (BATCH, L, D), 24.0, 144.0, ((0, 4), (1, 32))),
    }


SQRT_HALF = 0.7071067811865476
INV_ROOT_TWO_PI = 0.3989422804014327


def gelu_pair(preact):
    cumul = 0.5 * (1.0 + lax.erf(preact * SQRT_HALF))
    return preact * cumul, cumul + preact * INV_ROOT_TWO_PI * jnp.exp(-0.5 * preact * preact)


def head_gradients(query, keyset, valueset, grad_out, score_scale):
    scores = jnp.dot(query, keyset.T, preferred_element_type=jnp.float32) * score_scale
    top = jnp.max(scores, axis=1, keepdims=True)
    powers = jnp.exp(scores - top)
    probs = powers / jnp.sum(powers, axis=1, keepdims=True)
    probs_low = probs.astype(jnp.bfloat16)
    output = jnp.dot(probs_low, valueset, preferred_element_type=jnp.float32)
    row_delta = jnp.sum(grad_out.astype(jnp.float32) * output, axis=1, keepdims=True)
    prob_grad = jnp.dot(grad_out, valueset.T, preferred_element_type=jnp.float32)
    score_grad = (probs * (prob_grad - row_delta)).astype(jnp.bfloat16)
    query_grad = jnp.dot(score_grad, keyset, preferred_element_type=jnp.float32) * score_scale
    key_grad = jnp.dot(score_grad.T, query, preferred_element_type=jnp.float32) * score_scale
    value_grad = jnp.dot(probs_low.T, grad_out, preferred_element_type=jnp.float32)
    return query_grad, key_grad, value_grad


def reference(conv_input, skip_grad, conv_weight, proj_weight, saved_query, saved_key, saved_value, attn_grad):
    score_scale = HD ** -0.5
    rim_width = TAPS // 2
    conv_total = jnp.zeros((TAPS, C, C), jnp.float32)
    proj_total = jnp.zeros((C, 3 * D), jnp.float32)
    results = []
    for batch_index in range(BATCH):
        inputs = conv_input[batch_index]
        padded = jnp.pad(inputs, ((rim_width, rim_width), (0, 0)))
        preact = jnp.zeros((POS, C), jnp.float32)
        for offset in range(TAPS):
            preact = preact + jnp.dot(padded[offset:offset + POS], conv_weight[offset], preferred_element_type=jnp.float32)
        act, slope = gelu_pair(preact)
        block_out = (inputs.astype(jnp.float32) + act).astype(jnp.bfloat16)
        pooled = jnp.mean(block_out.astype(jnp.float32).reshape(L, UP, C), axis=1).astype(jnp.bfloat16)
        parts_q = []
        parts_k = []
        parts_v = []
        for head_index in range(HEADS):
            lower = head_index * HD
            upper = lower + HD
            grads = head_gradients(saved_query[batch_index][:, lower:upper], saved_key[batch_index][:, lower:upper],
                                   saved_value[batch_index][:, lower:upper], attn_grad[batch_index][:, lower:upper], score_scale)
            parts_q.append(grads[0])
            parts_k.append(grads[1])
            parts_v.append(grads[2])
        qkv_grad = jnp.concatenate(parts_q + parts_k + parts_v, axis=1).astype(jnp.bfloat16)
        pool_grad = jnp.dot(qkv_grad, proj_weight.T, preferred_element_type=jnp.float32)
        spread = jnp.broadcast_to((pool_grad / UP)[:, None, :], (L, UP, C)).reshape(POS, C)
        row_grad = skip_grad[batch_index].astype(jnp.float32) + spread
        pre_grad = (row_grad * slope).astype(jnp.bfloat16)
        grad_pad = jnp.pad(pre_grad, ((rim_width, rim_width), (0, 0)))
        total = row_grad
        for offset in range(TAPS):
            start = 2 * rim_width - offset
            total = total + jnp.dot(grad_pad[start:start + POS], conv_weight[offset].T, preferred_element_type=jnp.float32)
        results.append(total.astype(jnp.bfloat16))
        conv_total = conv_total + jnp.stack([jnp.dot(padded[offset:offset + POS].T, pre_grad, preferred_element_type=jnp.float32) for offset in range(TAPS)])
        proj_total = proj_total + jnp.dot(pooled.T, qkv_grad, preferred_element_type=jnp.float32)
    return (jnp.stack(results), conv_total / LOSS_SCALE, proj_total / LOSS_SCALE)
```

```python
import jax
import jax.numpy as jnp
from jax import lax
from jax.experimental import pallas as pl
from jax.experimental.pallas import tpu as pltpu
from jax.sharding import Mesh, PartitionSpec as P

HEADS = 8
TAPS = 5
LOSS_SCALE = 32
HD = 192
C = 768
ROWS = 768
ATT = 48
BLK = 384
FACTOR = 16
HALF = 384
QH = 288
SCALE = HD ** (-0.5)
SQRT_HALF = 0.7071067811865476
INV_ROOT_TWO_PI = 0.3989422804014327

BF = jnp.bfloat16
F32 = jnp.float32
DP = ("yh", "core")
SEQ = ("yl", "x", "z")
HAX = ("yl", "x")

NT = (((1,), (1,)), ((), ()))
TN = (((0,), (0,)), ((), ()))

A_PAIR = [(0, 1), (1, 0), (2, 3), (3, 2)]
B_PAIR = [(0, 3), (3, 0), (1, 2), (2, 1)]
SWAP = [(0, 1), (1, 0)]


def sds(shape, dtype):
    return jax.ShapeDtypeStruct(shape, dtype)


def params(mib):
    return pltpu.CompilerParams(vmem_limit_bytes=mib * 1024 * 1024)


def cost(flops, nbytes, trans=0):
    return pl.CostEstimate(flops=flops, bytes_accessed=nbytes, transcendentals=trans)


VM = pl.BlockSpec(memory_space=pltpu.VMEM)
SM = pl.BlockSpec(memory_space=pltpu.SMEM)


def nt(a, b):
    return lax.dot_general(a, b, NT, preferred_element_type=F32)


def tn(a, b):
    return lax.dot_general(a, b, TN, preferred_element_type=F32)


def mm(a, b):
    return jnp.dot(a, b, preferred_element_type=F32)


def pack_kernel(q, k, v, g, out):
    for h in range(HEADS):
        cols = slice(h * HD, (h + 1) * HD)
        for slot, ref in enumerate((q, g, k, v)):
            out[h, :, slot * HD : (slot + 1) * HD] = ref[:, cols]


def pack_heads(q, k, v, g):
    return pl.pallas_call(
        pack_kernel,
        out_shape=sds((HEADS, ATT, 4 * HD), BF),
        in_specs=[VM] * 4,
        out_specs=VM,
        name="pack_heads",
        cost_estimate=cost(0, 1200000),
    )(q, k, v, g)


def att_parts(own, qg, kv):
    query = jnp.concatenate([own[:, 0:HD], qg[:, 0:HD]], axis=0)
    grads = jnp.concatenate([own[:, HD : 2 * HD], qg[:, HD : 2 * HD]], axis=0)
    keys = jnp.concatenate([own[:, 2 * HD : 3 * HD], kv[:, 0:HD]], axis=0)
    values = jnp.concatenate([own[:, 3 * HD : 4 * HD], kv[:, HD : 2 * HD]], axis=0)
    return query, grads, keys, values


def stats_kernel(own, qg, kv, out):
    query, grads, keys, values = att_parts(own, qg, kv)
    out[...] = jnp.zeros_like(out)
    for i in range(2):
        rows = slice(i * BLK, (i + 1) * BLK)
        scores = nt(keys, query[rows]) * SCALE
        top = jnp.max(scores, axis=0, keepdims=True)
        powers = jnp.exp(scores - top)
        pgrad = nt(values, grads[rows])
        out[0:1, rows] = top
        out[1:2, rows] = jnp.sum(powers, axis=0, keepdims=True)
        out[2:3, rows] = jnp.sum(powers * pgrad, axis=0, keepdims=True)


def att_stats(own, qg, kv):
    return pl.pallas_call(
        stats_kernel,
        out_shape=sds((8, 2 * BLK), F32),
        in_specs=[VM] * 3,
        out_specs=VM,
        name="att_stats",
        compiler_params=params(32),
        cost_estimate=cost(2 * 768 * 768 * 192 * 2, 1200000, 768 * 768),
    )(own, qg, kv)


def grads_kernel(own, qg, kv, st, st2, dq_own, dq_send, dkv_own, dkv_send):
    query, grads, keys, values = att_parts(own, qg, kv)
    dk = jnp.zeros((2 * BLK, HD), F32)
    dv = jnp.zeros((2 * BLK, HD), F32)
    for i in range(2):
        rows = slice(i * BLK, (i + 1) * BLK)
        other = slice((1 - i) * BLK, (2 - i) * BLK)
        m0, m1 = st[0:1, rows], st2[0:1, other]
        top = jnp.maximum(m0, m1)
        e0, e1 = jnp.exp(m0 - top), jnp.exp(m1 - top)
        inv = 1.0 / (st[1:2, rows] * e0 + st2[1:2, other] * e1)
        delta = (st[2:3, rows] * e0 + st2[2:3, other] * e1) * inv
        scores = nt(keys, query[rows]) * SCALE
        probs = jnp.exp(scores - top) * inv
        pgrad = nt(values, grads[rows])
        sgrad = (probs * (pgrad - delta)).astype(BF)
        dq = tn(sgrad, keys) * SCALE
        dk = dk + mm(sgrad, query[rows])
        dv = dv + mm(probs.astype(BF), grads[rows])
        if i == 0:
            dq_own[...] = dq
        else:
            dq_send[:, 0:HD] = dq[0 : BLK // 2].astype(BF)
            dq_send[:, HD : 2 * HD] = dq[BLK // 2 : BLK].astype(BF)
    dk = dk * SCALE
    dkv_own[:, 0:HD] = dk[0:BLK]
    dkv_own[:, HD : 2 * HD] = dv[0:BLK]
    dkv_send[:, 0:HD] = dk[BLK:].astype(BF)
    dkv_send[:, HD : 2 * HD] = dv[BLK:].astype(BF)


def att_grads(own, qg, kv, st, st2):
    return pl.pallas_call(
        grads_kernel,
        out_shape=(
            sds((BLK, HD), F32),
            sds((BLK // 2, 2 * HD), BF),
            sds((BLK, 2 * HD), F32),
            sds((BLK, 2 * HD), BF),
        ),
        in_specs=[VM] * 5,
        out_specs=(VM,) * 4,
        name="att_grads",
        compiler_params=params(40),
        cost_estimate=cost(5 * 768 * 768 * 192 * 2, 3000000, 768 * 768),
    )(own, qg, kv, st, st2)


def join_kernel(core, dq_own, dkv_own, dq_in, dkv_in, wh, pool, keep, send):
    dq_got = jnp.concatenate([dq_in[:, 0:HD], dq_in[:, HD : 2 * HD]], axis=0).astype(F32)
    dq = (dq_own[...] + dq_got).astype(BF)
    dkv = (dkv_own[...] + dkv_in[...].astype(F32)).astype(BF)
    qkv = jnp.concatenate([dq, dkv], axis=1)
    pool[...] = nt(qkv, wh[...]).astype(BF)

    @pl.when(core[0] == 0)
    def _():
        keep[...] = qkv[:, 0:QH]
        send[...] = qkv[:, QH : 2 * QH]

    @pl.when(core[0] != 0)
    def _():
        keep[...] = qkv[:, QH : 2 * QH]
        send[...] = qkv[:, 0:QH]


def att_join(core, dq_own, dkv_own, dq_in, dkv_in, wh):
    return pl.pallas_call(
        join_kernel,
        out_shape=(sds((BLK, C), BF), sds((BLK, QH), BF), sds((BLK, QH), BF)),
        in_specs=[SM] + [VM] * 5,
        out_specs=(VM,) * 3,
        name="att_join",
        compiler_params=params(24),
        cost_estimate=cost(2 * 384 * 576 * 768, 3500000),
    )(core, dq_own, dkv_own, dq_in, dkv_in, wh)


def forward_kernel(xp, w, slope, pooled, xf, acc):
    tap = pl.program_id(0)

    @pl.when(tap == 0)
    def _():
        xf[...] = xp[...].astype(F32)

    for t in range(TAPS):

        @pl.when(tap == t)
        def _(t=t):
            for r in range(0, ROWS, 256):
                rows = xf[6 + t + r : 6 + t + r + 256, :].astype(BF)
                got = mm(rows, w[0])
                if t == 0:
                    acc[r : r + 256, :] = got
                else:
                    acc[r : r + 256, :] += got

    @pl.when(tap == TAPS - 1)
    def _():
        @pl.loop(0, ROWS // 64)
        def _(i):
            at = pl.multiple_of(i * 64, 64)
            pre = acc[pl.ds(at, 64), :]
            cumul = 0.5 * (1.0 + lax.erf(pre * SQRT_HALF))
            slope[pl.ds(at, 64), :] = (
                cumul + pre * INV_ROOT_TWO_PI * jnp.exp(-0.5 * pre * pre)
            ).astype(BF)
            rows = xf[pl.ds(pl.multiple_of(at + 8, 8), 64), :]
            block = (rows + pre * cumul).astype(BF).astype(F32)
            acc[pl.ds(pl.multiple_of(i * 8, 8), 8), :] = jnp.concatenate(
                [jnp.mean(block.reshape(4, FACTOR, C), axis=1), jnp.zeros((4, C), F32)], axis=0
            )

        for i in range(ROWS // 64):
            pooled[4 * i : 4 * i + 4, :] = acc[8 * i : 8 * i + 4, :]


def conv_forward(xp, w):
    return pl.pallas_call(
        forward_kernel,
        grid=(TAPS,),
        out_shape=(sds((ROWS, C), BF), sds((ATT, C), F32)),
        in_specs=[
            pl.BlockSpec((ROWS + 16, C), lambda t: (0, 0)),
            pl.BlockSpec((1, C, C), lambda t: (t, 0, 0)),
        ],
        out_specs=(
            pl.BlockSpec((ROWS, C), lambda t: (0, 0)),
            pl.BlockSpec((ATT, C), lambda t: (0, 0)),
        ),
        scratch_shapes=[pltpu.VMEM((ROWS + 16, C), F32), pltpu.VMEM((ROWS, C), F32)],
        name="conv_forward",
        compiler_params=params(32),
        cost_estimate=cost(2 * 5 * 768**3, 9500000, 2 * 768 * 768),
    )(xp, w)


def turn_kernel(xp, xt, alts, edge):
    for r in range(0, ROWS, 128):
        xt[:, r : r + 128] = xp[8 + r : 8 + r + 128, :].T
    last = xp[8 + ROWS - 128 : 8 + ROWS, :].astype(F32)
    first = xp[8 : 8 + 128, :].astype(F32)
    top = xp[0:16, :].astype(F32)[0:8]
    bottom = xp[ROWS : ROWS + 16, :].astype(F32)[8:16]
    edge[...] = last
    edge[126:128, :] = top[6:8]
    alts[:, 0:128] = edge[...].astype(BF).T
    edge[126:127, :] = last[126:127]
    alts[:, 128:256] = edge[...].astype(BF).T
    edge[...] = first
    edge[0:1, :] = bottom[0:1]
    alts[:, 256:384] = edge[...].astype(BF).T
    edge[1:2, :] = bottom[1:2]
    alts[:, 384:512] = edge[...].astype(BF).T


def turn_input(xp):
    return pl.pallas_call(
        turn_kernel,
        out_shape=(sds((C, ROWS), BF), sds((C, 512), BF)),
        in_specs=[VM],
        out_specs=(VM, VM),
        scratch_shapes=[pltpu.VMEM((128, C), F32)],
        name="turn_input",
        compiler_params=params(24),
        cost_estimate=cost(10 * 768 * 768, 3200000),
    )(xp)


def slope_kernel(core, parts, skip, slope, pre, send, keep, pool):
    total = jnp.sum(parts[...].astype(F32), axis=0) * (1.0 / FACTOR)
    pool[...] = total
    for r in range(0, ATT, 8):
        piece = jnp.broadcast_to(total[r : r + 8, None, :], (8, FACTOR, C)).reshape(128, C)
        rows = slice(r * FACTOR, r * FACTOR + 128)
        grad = (skip[rows, :].astype(F32) + piece) * slope[rows, :].astype(F32)
        pre[rows, :] = grad.astype(BF)

    @pl.when(core[0] == 0)
    def _():
        keep[...] = pre[:, 0:HALF]
        send[...] = pre[:, HALF:]

    @pl.when(core[0] != 0)
    def _():
        keep[...] = pre[:, HALF:]
        send[...] = pre[:, 0:HALF]


def pre_grads(core, parts, skip, slope):
    return pl.pallas_call(
        slope_kernel,
        out_shape=(
            sds((ROWS, C), BF),
            sds((ROWS, HALF), BF),
            sds((ROWS, HALF), BF),
            sds((ATT, C), F32),
        ),
        in_specs=[SM] + [VM] * 3,
        out_specs=(VM,) * 4,
        name="pre_grads",
        compiler_params=params(24),
        cost_estimate=cost(5 * 768 * 768, 6000000),
    )(core, parts, skip, slope)


def weights_kernel(xt0, al0, xt1, al1, y0, y1, p0, p1, s0, s1, out, yf, yt):
    step = pl.program_id(0)

    @pl.when(step == 0)
    def _():
        for i, ref in enumerate((y0, y1)):
            got = ref[...].astype(F32)
            yf[8 : 8 + ROWS, :] = got
            yf[0:8, :] = got[ROWS - 8 :]
            yf[8 + ROWS : 16 + ROWS, :] = got[0:8]
            for t in range(TAPS):
                yt[t, i * ROWS : (i + 1) * ROWS, :] = yf[10 - t : 10 - t + ROWS, :].astype(BF)

    def shifted(xt, al, t):
        if t < 2:
            return jnp.concatenate([xt[:, : ROWS - 128], al[:, t * 128 : t * 128 + 128]], axis=1)
        if t > 2:
            return jnp.concatenate([al[:, (t - 1) * 128 : t * 128], xt[:, 128:]], axis=1)
        return xt[...]

    for t in range(TAPS):
        left = jnp.concatenate([shifted(xt0, al0, t), shifted(xt1, al1, t)], axis=1)
        out[:, t * HALF : (t + 1) * HALF] = mm(left, yt[t]).astype(BF)
    out[:, TAPS * HALF : TAPS * HALF + QH] = (tn(p0[...], s0[...]) + tn(p1[...], s1[...])).astype(BF)
    out[:, TAPS * HALF + QH :] = jnp.zeros((256, 2304 - TAPS * HALF - QH), BF)


def weight_grads(xt0, al0, xt1, al1, y0, y1, p0, p1, s0, s1):
    rows = lambda n: pl.BlockSpec((256, n), lambda i: (i, 0))
    whole = lambda a, b: pl.BlockSpec((a, b), lambda i: (0, 0))
    cols = pl.BlockSpec((BLK, 256), lambda i: (0, i))
    return pl.pallas_call(
        weights_kernel,
        grid=(3,),
        out_shape=sds((C, 2304), BF),
        in_specs=[
            rows(ROWS),
            rows(512),
            rows(ROWS),
            rows(512),
            whole(ROWS, HALF),
            whole(ROWS, HALF),
            cols,
            cols,
            whole(BLK, QH),
            whole(BLK, QH),
        ],
        out_specs=rows(2304),
        scratch_shapes=[
            pltpu.VMEM((ROWS + 16, HALF), F32),
            pltpu.VMEM((TAPS, 2 * ROWS, HALF), BF),
        ],
        name="weight_grads",
        compiler_params=params(40),
        cost_estimate=cost(2 * 5 * 768 * 1536 * 384, 10000000),
    )(xt0, al0, xt1, al1, y0, y1, p0, p1, s0, s1)


def adjoint_kernel(pre, top, bottom, w, skip, pool, out, yf, acc):
    tap = pl.program_id(0)

    @pl.when(tap == 0)
    def _():
        yf[8 : 8 + ROWS, :] = pre[...].astype(F32)
        yf[6:8, :] = top[...].astype(F32)
        yf[8 + ROWS : 10 + ROWS, :] = bottom[...].astype(F32)
        for r in range(0, ATT, 8):
            piece = jnp.broadcast_to(pool[r : r + 8, :][:, None, :], (8, FACTOR, C)).reshape(128, C)
            rows = slice(r * FACTOR, r * FACTOR + 128)
            acc[rows, :] = skip[rows, :].astype(F32) + piece

    for t in range(TAPS):

        @pl.when(tap == t)
        def _(t=t):
            for r in range(0, ROWS, 256):
                rows = yf[10 - t + r : 10 - t + r + 256, :].astype(BF)
                got = acc[r : r + 256, :] + nt(rows, w[0])
                if t == TAPS - 1:
                    out[r : r + 256, :] = got.astype(BF)
                else:
                    acc[r : r + 256, :] = got


def conv_adjoint(pre, top, bottom, w, skip, pool):
    whole = lambda a, b: pl.BlockSpec((a, b), lambda t: (0, 0))
    return pl.pallas_call(
        adjoint_kernel,
        grid=(TAPS,),
        out_shape=sds((ROWS, C), BF),
        in_specs=[
            whole(ROWS, C),
            whole(2, C),
            whole(2, C),
            pl.BlockSpec((1, C, C), lambda t: (t, 0, 0)),
            whole(ROWS, C),
            whole(ATT, C),
        ],
        out_specs=whole(ROWS, C),
        scratch_shapes=[pltpu.VMEM((ROWS + 16, C), F32), pltpu.VMEM((ROWS, C), F32)],
        name="conv_adjoint",
        compiler_params=params(32),
        cost_estimate=cost(2 * 5 * 768**3, 9500000),
    )(pre, top, bottom, w, skip, pool)


def sum_conv_kernel(parts, out):
    total = parts[0].astype(F32)
    for s in range(1, 32):
        total = total + parts[s].astype(F32)
    out[0] = total.astype(BF)


def sum_proj_kernel(parts, out):
    for h in range(HEADS):
        total = parts[4 * h].astype(F32)
        for s in range(4 * h + 1, 4 * h + 4):
            total = total + parts[s].astype(F32)
        out[h] = total.astype(BF)


def sum_partials(parts):
    conv = pl.pallas_call(
        sum_conv_kernel,
        grid=(TAPS,),
        out_shape=sds((TAPS, 24, HALF), BF),
        in_specs=[pl.BlockSpec((32, 24, HALF), lambda t: (0, 0, t))],
        out_specs=pl.BlockSpec((1, 24, HALF), lambda t: (t, 0, 0)),
        name="sum_conv",
        cost_estimate=cost(32 * 24 * 1920, 3000000),
    )(parts)
    proj = pl.pallas_call(
        sum_proj_kernel,
        grid=(1,),
        out_shape=sds((HEADS, 24, HALF), BF),
        in_specs=[pl.BlockSpec((32, 24, HALF), lambda t: (0, 0, TAPS))],
        out_specs=pl.BlockSpec((HEADS, 24, HALF), lambda t: (0, 0, 0)),
        name="sum_proj",
        cost_estimate=cost(32 * 24 * 384, 700000),
    )(parts)
    return conv, proj


def add_kernel(a, b, c, d, out):
    out[0:TAPS] = (a[...].astype(F32) + b[...].astype(F32)) * (1.0 / LOSS_SCALE)
    out[TAPS:] = (c[...].astype(F32) + d[...].astype(F32)) * (1.0 / LOSS_SCALE)


def add_pair(a, b, c, d):
    return pl.pallas_call(
        add_kernel,
        out_shape=sds((TAPS + HEADS, 24, HALF), F32),
        in_specs=[VM] * 4,
        out_specs=VM,
        name="add_pair",
        cost_estimate=cost(300000, 1500000),
    )(a, b, c, d)


def place_kernel(core, mine, other, conv, proj):
    def put(low, high):
        conv[:, :, 0:HALF] = low[0:TAPS]
        conv[:, :, HALF:] = high[0:TAPS]
        for h in range(HEADS):
            at = h * HD
            proj[:, at : at + HD] = low[TAPS + h, :, 0:HD]
            proj[:, 1536 + at : 1536 + at + HD] = jnp.concatenate(
                [low[TAPS + h, :, HD:QH], high[TAPS + h, :, 0 : HD // 2]], axis=1
            )
            proj[:, 3072 + at : 3072 + at + HD] = high[TAPS + h, :, HD // 2 : QH]

    @pl.when(core[0] == 0)
    def _():
        put(mine, other)

    @pl.when(core[0] != 0)
    def _():
        put(other, mine)


def place(core, mine, other):
    return pl.pallas_call(
        place_kernel,
        out_shape=(sds((TAPS, 24, C), F32), sds((24, 4608), F32)),
        in_specs=[SM, VM, VM],
        out_specs=(VM, VM),
        name="place",
        cost_estimate=cost(0, 2500000),
    )(core, mine, other)


def halo(x):
    up = [(i, i + 1) for i in range(31)]
    down = [(i + 1, i) for i in range(31)]
    return lax.ppermute(x[ROWS - 2 :], SEQ, up), lax.ppermute(x[0:2], SEQ, down)


def local(conv_input, skip_grad, conv_weight, proj_weight, query, key, value, grad):
    core = lax.axis_index("core").astype(jnp.int32).reshape(1)
    head = lax.axis_index("yl") * 4 + lax.axis_index("x")
    x, skip = conv_input[0], skip_grad[0]

    packed = pack_heads(query[0], key[0], value[0], grad[0])
    own = lax.all_to_all(packed, HAX, 0, 0, tiled=True).reshape(BLK, 4 * HD)
    qg = lax.ppermute(own[:, : 2 * HD], "z", A_PAIR)
    kv = lax.ppermute(own[:, 2 * HD :], "z", B_PAIR)

    top, bottom = halo(x)
    edge = jnp.zeros((6, C), BF)
    xp = jnp.concatenate([edge, top, x, bottom, edge], axis=0)
    xp_sib = lax.ppermute(xp, "core", SWAP)
    slope, pooled = conv_forward(xp, conv_weight)
    pooled_blk = lax.all_gather(pooled.astype(BF), HAX, axis=0, tiled=True)
    pooled_sib = lax.ppermute(pooled_blk, "core", SWAP)
    xt0, al0 = turn_input(xp)
    xt1, al1 = turn_input(xp_sib)

    wh = jnp.concatenate(
        [lax.dynamic_slice_in_dim(proj_weight, p * 1536 + head * HD, HD, 1) for p in range(3)], axis=1
    )

    st = att_stats(own, qg, kv)
    st2 = lax.ppermute(st, "z", A_PAIR)
    dq_own, dq_send, dkv_own, dkv_send = att_grads(own, qg, kv, st, st2)
    dq_in = lax.ppermute(dq_send, "z", A_PAIR)
    dkv_in = lax.ppermute(dkv_send, "z", B_PAIR)
    pool_part, s0, s_send = att_join(core, dq_own, dkv_own, dq_in, dkv_in, wh)
    parts = lax.all_to_all(pool_part.reshape(HEADS, ATT, C), HAX, 0, 0, tiled=True)
    s1 = lax.ppermute(s_send, "core", SWAP)

    pre, y_send, y0, pool = pre_grads(core, parts, skip, slope)
    y1 = lax.ppermute(y_send, "core", SWAP)
    terms = weight_grads(xt0, al0, xt1, al1, y0, y1, pooled_blk, pooled_sib, s0, s1)
    got = lax.all_to_all(terms.reshape(32, 24, 2304), SEQ, 0, 0, tiled=True)

    ptop, pbottom = halo(pre)
    input_grad = conv_adjoint(pre, ptop, pbottom, conv_weight, skip, pool)

    conv, proj = sum_partials(got)
    far = [(0, 1), (1, 0)]
    mine = add_pair(conv, lax.ppermute(conv, "yh", far), proj, lax.ppermute(proj, "yh", far))
    other = lax.ppermute(mine, "core", SWAP)
    conv_grad, proj_grad = place(core, mine, other)
    return input_grad[None], conv_grad, proj_grad


def solution(mesh):
    fine = Mesh(mesh.devices.reshape(2, 2, 2, 4, 4), ("yh", "core", "yl", "x", "z"))
    rows = P(DP, SEQ, None)
    return jax.shard_map(
        local,
        mesh=fine,
        in_specs=(rows, rows, P(), P(), rows, rows, rows, rows),
        out_specs=(rows, P(None, SEQ, None), P(SEQ, None)),
        check_vma=False,
    )
```

```python
import jax
import jax.numpy as jnp
from jax import lax
from jax.experimental import pallas as pl
from jax.experimental.pallas import tpu as pltpu
from jax.sharding import Mesh, PartitionSpec as P

HEADS = 8
TAPS = 5
LOSS_SCALE = 32
HD = 192
C = 768
ROWS = 768
ATT = 48
BLK = 384
FACTOR = 16
HALF = 384
QH = 288
SCALE = HD ** (-0.5)
SQRT_HALF = 0.7071067811865476
INV_ROOT_TWO_PI = 0.3989422804014327

BF = jnp.bfloat16
F32 = jnp.float32
DP = ("yh", "core")
SEQ = ("yl", "x", "z")
HAX = ("yl", "x")

NT = (((1,), (1,)), ((), ()))
TN = (((0,), (0,)), ((), ()))

A_PAIR = [(0, 1), (1, 0), (2, 3), (3, 2)]
B_PAIR = [(0, 3), (3, 0), (1, 2), (2, 1)]
SWAP = [(0, 1), (1, 0)]


def sds(shape, dtype):
    return jax.ShapeDtypeStruct(shape, dtype)


def far(shape, dtype):
    return pltpu.HBM(shape, dtype)


def hbm(x):
    return pltpu.with_memory_space_constraint(x, pltpu.HBM)


def params(mib):
    return pltpu.CompilerParams(vmem_limit_bytes=mib * 1024 * 1024)


def cost(flops, nbytes, trans=0):
    return pl.CostEstimate(flops=flops, bytes_accessed=nbytes, transcendentals=trans)


VM = pl.BlockSpec(memory_space=pltpu.VMEM)
ANY = pl.BlockSpec(memory_space=pl.ANY)
SM = pl.BlockSpec(memory_space=pltpu.SMEM)


def nt(a, b):
    return lax.dot_general(a, b, NT, preferred_element_type=F32)


def tn(a, b):
    return lax.dot_general(a, b, TN, preferred_element_type=F32)


def mm(a, b):
    return jnp.dot(a, b, preferred_element_type=F32)


def pack_kernel(q, k, v, g, out):
    for h in range(HEADS):
        cols = slice(h * HD, (h + 1) * HD)
        for slot, ref in enumerate((q, g, k, v)):
            out[h, :, slot * HD : (slot + 1) * HD] = ref[:, cols]


def pack_heads(q, k, v, g):
    return pl.pallas_call(
        pack_kernel,
        out_shape=far((HEADS, ATT, 4 * HD), BF),
        in_specs=[VM] * 4,
        out_specs=VM,
        name="pack_heads",
        compiler_params=params(8),
        cost_estimate=cost(0, 1200000),
    )(hbm(q), hbm(k), hbm(v), hbm(g))


def att_parts(own, qg, kv):
    query = jnp.concatenate([own[:, 0:HD], qg[:, 0:HD]], axis=0)
    grads = jnp.concatenate([own[:, HD : 2 * HD], qg[:, HD : 2 * HD]], axis=0)
    keys = jnp.concatenate([own[:, 2 * HD : 3 * HD], kv[:, 0:HD]], axis=0)
    values = jnp.concatenate([own[:, 3 * HD : 4 * HD], kv[:, HD : 2 * HD]], axis=0)
    return query, grads, keys, values


def stats_kernel(own, qg, kv, after, out):
    query, grads, keys, values = att_parts(own, qg, kv)
    out[...] = jnp.zeros_like(out)
    for i in range(2):
        rows = slice(i * BLK, (i + 1) * BLK)
        scores = nt(keys, query[rows]) * SCALE
        top = jnp.max(scores, axis=0, keepdims=True)
        powers = jnp.exp(scores - top)
        pgrad = nt(values, grads[rows])
        out[0:1, rows] = top
        out[1:2, rows] = jnp.sum(powers, axis=0, keepdims=True)
        out[2:3, rows] = jnp.sum(powers * pgrad, axis=0, keepdims=True)


def att_stats(own, qg, kv, after):
    return pl.pallas_call(
        stats_kernel,
        out_shape=sds((8, 2 * BLK), F32),
        in_specs=[VM] * 3 + [ANY],
        out_specs=VM,
        name="att_stats",
        compiler_params=params(16),
        cost_estimate=cost(8000000000, 1200000, 768 * 768),
    )(own, qg, kv, after)


def grads_kernel(own, qg, kv, st, st2, dq_own, dq_send, dkv_own, dkv_send):
    query, grads, keys, values = att_parts(own, qg, kv)
    dk = jnp.zeros((2 * BLK, HD), F32)
    dv = jnp.zeros((2 * BLK, HD), F32)
    for i in range(2):
        rows = slice(i * BLK, (i + 1) * BLK)
        other = slice((1 - i) * BLK, (2 - i) * BLK)
        m0, m1 = st[0:1, rows], st2[0:1, other]
        top = jnp.maximum(m0, m1)
        e0, e1 = jnp.exp(m0 - top), jnp.exp(m1 - top)
        inv = 1.0 / (st[1:2, rows] * e0 + st2[1:2, other] * e1)
        delta = (st[2:3, rows] * e0 + st2[2:3, other] * e1) * inv
        scores = nt(keys, query[rows]) * SCALE
        probs = jnp.exp(scores - top) * inv
        pgrad = nt(values, grads[rows])
        sgrad = (probs * (pgrad - delta)).astype(BF)
        dq = tn(sgrad, keys) * SCALE
        dk = dk + mm(sgrad, query[rows])
        dv = dv + mm(probs.astype(BF), grads[rows])
        if i == 0:
            dq_own[...] = dq
        else:
            dq_send[:, 0:HD] = dq[0 : BLK // 2].astype(BF)
            dq_send[:, HD : 2 * HD] = dq[BLK // 2 : BLK].astype(BF)
    dk = dk * SCALE
    dkv_own[:, 0:HD] = dk[0:BLK]
    dkv_own[:, HD : 2 * HD] = dv[0:BLK]
    dkv_send[:, 0:HD] = dk[BLK:].astype(BF)
    dkv_send[:, HD : 2 * HD] = dv[BLK:].astype(BF)


def att_grads(own, qg, kv, st, st2):
    return pl.pallas_call(
        grads_kernel,
        out_shape=(
            sds((BLK, HD), F32),
            sds((BLK // 2, 2 * HD), BF),
            sds((BLK, 2 * HD), F32),
            sds((BLK, 2 * HD), BF),
        ),
        in_specs=[VM] * 5,
        out_specs=(VM,) * 4,
        name="att_grads",
        compiler_params=params(20),
        cost_estimate=cost(20000000000, 3000000, 768 * 768),
    )(own, qg, kv, st, st2)


def split_kernel(own, qg, kv):
    qg[...] = own[:, 0 : 2 * HD]
    kv[...] = own[:, 2 * HD : 4 * HD]


def split_own(own):
    return pl.pallas_call(
        split_kernel,
        out_shape=(sds((BLK, 2 * HD), BF), sds((BLK, 2 * HD), BF)),
        in_specs=[VM],
        out_specs=(VM, VM),
        name="split_own",
        compiler_params=params(8),
        cost_estimate=cost(0, 1200000),
    )(own)


def head_kernel(pair, odd, wq, wk, wv, out):
    for p, ref in enumerate((wq, wk, wv)):
        turned = ref[...].T

        @pl.when(odd[0] == 0)
        def _():
            out[p * HD : (p + 1) * HD, :] = turned[0:HD]

        @pl.when(odd[0] != 0)
        def _():
            out[p * HD : (p + 1) * HD, :] = turned[HD : 2 * HD]


def head_weights(pair, odd, weight):
    part = lambda p: pl.BlockSpec((C, 2 * HD), lambda i, pair, odd, p=p: (0, 4 * p + pair[0]))
    return pl.pallas_call(
        head_kernel,
        out_shape=sds((3 * HD, C), BF),
        grid_spec=pltpu.PrefetchScalarGridSpec(
            num_scalar_prefetch=2,
            grid=(1,),
            in_specs=[part(0), part(1), part(2)],
            out_specs=pl.BlockSpec((3 * HD, C), lambda i, pair, odd: (0, 0)),
        ),
        name="head_weights",
        compiler_params=params(12),
        cost_estimate=cost(0, 3000000),
    )(pair, odd, hbm(weight), hbm(weight), hbm(weight))


def join_kernel(core, dq_own, dkv_own, dq_in, dkv_in, wh, after, pool, keep, send):
    dq_got = jnp.concatenate([dq_in[:, 0:HD], dq_in[:, HD : 2 * HD]], axis=0).astype(F32)
    dq = (dq_own[...] + dq_got).astype(BF)
    dkv = (dkv_own[...] + dkv_in[...].astype(F32)).astype(BF)
    qkv = jnp.concatenate([dq, dkv], axis=1)
    pool[...] = mm(qkv, wh[...]).astype(BF)

    @pl.when(core[0] == 0)
    def _():
        keep[...] = qkv[:, 0:QH]
        send[...] = qkv[:, QH : 2 * QH]

    @pl.when(core[0] != 0)
    def _():
        keep[...] = qkv[:, QH : 2 * QH]
        send[...] = qkv[:, 0:QH]


def att_join(core, dq_own, dkv_own, dq_in, dkv_in, wh, after):
    return pl.pallas_call(
        join_kernel,
        out_shape=(far((BLK, C), BF), sds((BLK, QH), BF), sds((BLK, QH), BF)),
        in_specs=[SM] + [VM] * 5 + [ANY],
        out_specs=(VM,) * 3,
        name="att_join",
        compiler_params=params(12),
        cost_estimate=cost(10000000000, 3500000),
    )(core, dq_own, dkv_own, dq_in, dkv_in, wh, after)


def forward_kernel(xp, w, after, slope, pooled, xf, acc):
    tap = pl.program_id(0)

    @pl.when(tap == 0)
    def _():
        xf[...] = xp[...].astype(F32)

    for t in range(TAPS):

        @pl.when(tap == t)
        def _(t=t):
            for r in range(0, ROWS, 256):
                rows = xf[6 + t + r : 6 + t + r + 256, :].astype(BF)
                got = mm(rows, w[0])
                if t == 0:
                    acc[r : r + 256, :] = got
                else:
                    acc[r : r + 256, :] += got

    @pl.when(tap == TAPS - 1)
    def _():
        @pl.loop(0, ROWS // 64)
        def _(i):
            at = pl.multiple_of(i * 64, 64)
            pre = acc[pl.ds(at, 64), :]
            cumul = 0.5 * (1.0 + lax.erf(pre * SQRT_HALF))
            slope[pl.ds(at, 64), :] = (
                cumul + pre * INV_ROOT_TWO_PI * jnp.exp(-0.5 * pre * pre)
            ).astype(BF)
            rows = xf[pl.ds(pl.multiple_of(at + 8, 8), 64), :]
            block = (rows + pre * cumul).astype(BF).astype(F32)
            acc[pl.ds(pl.multiple_of(i * 8, 8), 8), :] = jnp.concatenate(
                [jnp.mean(block.reshape(4, FACTOR, C), axis=1), jnp.zeros((4, C), F32)], axis=0
            )

        for i in range(ROWS // 64):
            xf[4 * i : 4 * i + 4, :] = acc[8 * i : 8 * i + 4, :]
        rows = xf[0:ATT, :].astype(BF)
        for h in range(HEADS):
            pooled[h] = rows


def conv_forward(xp, w, after):
    return pl.pallas_call(
        forward_kernel,
        grid=(TAPS,),
        out_shape=(sds((ROWS, C), BF), far((HEADS, ATT, C), BF)),
        in_specs=[
            pl.BlockSpec((ROWS + 16, C), lambda t: (0, 0)),
            pl.BlockSpec((1, C, C), lambda t: (t, 0, 0)),
            ANY,
        ],
        out_specs=(
            pl.BlockSpec((ROWS, C), lambda t: (0, 0)),
            pl.BlockSpec((HEADS, ATT, C), lambda t: (0, 0, 0)),
        ),
        scratch_shapes=[pltpu.VMEM((ROWS + 16, C), F32), pltpu.VMEM((ROWS, C), F32)],
        name="conv_forward",
        compiler_params=params(20),
        cost_estimate=cost(2 * 5 * 768**3, 9500000, 2 * 768 * 768),
    )(xp, hbm(w), after)


def turn_kernel(xp, xt, alts, edge):
    for r in range(0, ROWS, 128):
        xt[:, r : r + 128] = xp[8 + r : 8 + r + 128, :].T
    last = xp[8 + ROWS - 128 : 8 + ROWS, :].astype(F32)
    first = xp[8 : 8 + 128, :].astype(F32)
    top = xp[0:16, :].astype(F32)[0:8]
    bottom = xp[ROWS : ROWS + 16, :].astype(F32)[8:16]
    edge[...] = last
    edge[126:128, :] = top[6:8]
    alts[:, 0:128] = edge[...].astype(BF).T
    edge[126:127, :] = last[126:127]
    alts[:, 128:256] = edge[...].astype(BF).T
    edge[...] = first
    edge[0:1, :] = bottom[0:1]
    alts[:, 256:384] = edge[...].astype(BF).T
    edge[1:2, :] = bottom[1:2]
    alts[:, 384:512] = edge[...].astype(BF).T


def turn_input(xp):
    return pl.pallas_call(
        turn_kernel,
        out_shape=(sds((C, ROWS), BF), sds((C, 512), BF)),
        in_specs=[VM],
        out_specs=(VM, VM),
        scratch_shapes=[pltpu.VMEM((128, C), F32)],
        name="turn_input",
        compiler_params=params(12),
        cost_estimate=cost(10 * 768 * 768, 3200000),
    )(xp)


def slope_kernel(core, parts, skip, slope, pre, send, keep, pool):
    total = jnp.sum(parts[...].astype(F32), axis=0) * (1.0 / FACTOR)
    pool[...] = total
    for r in range(0, ATT, 8):
        piece = jnp.broadcast_to(total[r : r + 8, None, :], (8, FACTOR, C)).reshape(128, C)
        rows = slice(r * FACTOR, r * FACTOR + 128)
        grad = (skip[rows, :].astype(F32) + piece) * slope[rows, :].astype(F32)
        pre[rows, :] = grad.astype(BF)

    @pl.when(core[0] == 0)
    def _():
        keep[...] = pre[:, 0:HALF]
        send[...] = pre[:, HALF:]

    @pl.when(core[0] != 0)
    def _():
        keep[...] = pre[:, HALF:]
        send[...] = pre[:, 0:HALF]


def pre_grads(core, parts, skip, slope):
    return pl.pallas_call(
        slope_kernel,
        out_shape=(
            sds((ROWS, C), BF),
            sds((ROWS, HALF), BF),
            sds((ROWS, HALF), BF),
            sds((ATT, C), F32),
        ),
        in_specs=[SM] + [VM] * 3,
        out_specs=(VM,) * 4,
        name="pre_grads",
        compiler_params=params(12),
        cost_estimate=cost(5 * 768 * 768, 6000000),
    )(core, parts, skip, slope)


def weights_kernel(xt0, al0, xt1, al1, y0, y1, p0, p1, s0, s1, out, yf, yt, made, sems):
    def copy(t):
        cols = pl.ds(t * HALF, HALF)
        return pltpu.make_async_copy(made.at[t], out.at[:, cols], sems.at[t])

    def shifted(xt, al, t, rows):
        if t < 2:
            return jnp.concatenate([xt[rows, : ROWS - 128], al[rows, t * 128 : t * 128 + 128]], axis=1)
        if t > 2:
            return jnp.concatenate([al[rows, (t - 1) * 128 : t * 128], xt[rows, 128:]], axis=1)
        return xt[rows, :]

    made[TAPS, :, 0:QH] = (tn(p0[...], s0[...]) + tn(p1[...], s1[...])).astype(BF)
    made[TAPS, :, QH:HALF] = jnp.zeros((C, HALF - QH), BF)
    copy(TAPS).start()
    for i, ref in enumerate((y0, y1)):
        got = ref[...].astype(F32)
        yf[i, 8 : 8 + ROWS, :] = got
        yf[i, 0:8, :] = got[ROWS - 8 :]
        yf[i, 8 + ROWS : 16 + ROWS, :] = got[0:8]
    for t in (2, 0, 1, 3, 4):
        if t == 2:
            right = [y0[...], y1[...]]
        else:
            for i in range(2):
                yt[t, i] = yf[i, 10 - t : 10 - t + ROWS, :].astype(BF)
            right = [yt[t, 0], yt[t, 1]]
        for r in range(0, C, 256):
            rows = slice(r, r + 256)
            made[t, rows, :] = (
                mm(shifted(xt0, al0, t, rows), right[0]) + mm(shifted(xt1, al1, t, rows), right[1])
            ).astype(BF)
        copy(t).start()
    for t in range(TAPS + 1):
        copy(t).wait()


def weight_grads(xt0, al0, xt1, al1, y0, y1, p0, p1, s0, s1):
    return pl.pallas_call(
        weights_kernel,
        out_shape=far((C, 2304), BF),
        in_specs=[VM] * 10,
        out_specs=pl.BlockSpec(memory_space=pltpu.HBM),
        scratch_shapes=[
            pltpu.VMEM((2, ROWS + 16, HALF), F32),
            pltpu.VMEM((TAPS, 2, ROWS, HALF), BF),
            pltpu.VMEM((TAPS + 1, C, HALF), BF),
            pltpu.SemaphoreType.DMA((TAPS + 1,)),
        ],
        name="weight_grads",
        compiler_params=params(32),
        cost_estimate=cost(2 * 5 * 768 * 1536 * 384, 10000000),
    )(xt0, al0, xt1, al1, y0, y1, p0, p1, s0, s1)


def adjoint_kernel(pre, w, skip, pool, out, before, after, first, last, yf, acc):
    tap = pl.program_id(0)

    @pl.when(tap == 0)
    def _():
        yf[0:16, :] = jnp.zeros((16, C), F32)
        yf[16 : 16 + ROWS, :] = pre[...].astype(F32)
        yf[16 + ROWS :, :] = jnp.zeros((16, C), F32)
        acc[0:8, :] = jnp.zeros((8, C), F32)
        acc[8 + ROWS :, :] = jnp.zeros((8, C), F32)
        for r in range(0, ATT, 8):
            piece = jnp.broadcast_to(pool[r : r + 8, :][:, None, :], (8, FACTOR, C)).reshape(128, C)
            rows = slice(r * FACTOR, r * FACTOR + 128)
            acc[8 + r * FACTOR : 136 + r * FACTOR, :] = skip[rows, :].astype(F32) + piece

    for t in range(TAPS):

        @pl.when(tap == t)
        def _(t=t):
            for r, n in ((0, 256), (256, 256), (512, 272)):
                rows = yf[10 - t + r : 10 - t + r + n, :].astype(BF)
                acc[r : r + n, :] += nt(rows, w[0])

    @pl.when(tap == TAPS - 1)
    def _():
        out[...] = acc[8 : 8 + ROWS, :].astype(BF)
        before[...] = acc[0:8, :]
        first[...] = acc[8:16, :]
        last[...] = acc[ROWS : ROWS + 8, :]
        after[...] = acc[ROWS + 8 :, :]


def conv_adjoint(pre, w, skip, pool):
    whole = lambda a, b: pl.BlockSpec((a, b), lambda t: (0, 0))
    return pl.pallas_call(
        adjoint_kernel,
        grid=(TAPS,),
        out_shape=(far((ROWS, C), BF),) + (sds((8, C), F32),) * 4,
        in_specs=[
            whole(ROWS, C),
            pl.BlockSpec((1, C, C), lambda t: (t, 0, 0)),
            whole(ROWS, C),
            whole(ATT, C),
        ],
        out_specs=(whole(ROWS, C),) + (whole(8, C),) * 4,
        scratch_shapes=[pltpu.VMEM((ROWS + 32, C), F32), pltpu.VMEM((ROWS + 16, C), F32)],
        name="conv_adjoint",
        compiler_params=params(24),
        cost_estimate=cost(2 * 5 * 768**3, 9500000),
    )(pre, hbm(w), skip, pool)


def edge_kernel(rows, first, last, top, bottom, out):
    step = pl.program_id(0)
    held = rows[...].astype(F32)

    @pl.when(step == 0)
    def _():
        out[...] = jnp.concatenate([first[...] + top[...], held[8:16]], axis=0).astype(BF)

    @pl.when(step != 0)
    def _():
        out[...] = jnp.concatenate([held[0:8], last[...] + bottom[...]], axis=0).astype(BF)


def add_edges(rows, first, last, top, bottom):
    block = pl.BlockSpec((16, C), lambda i: (i * (ROWS // 16 - 1), 0))
    whole = pl.BlockSpec((8, C), lambda i: (0, 0))
    return pl.pallas_call(
        edge_kernel,
        grid=(2,),
        out_shape=far((ROWS, C), BF),
        in_specs=[block, whole, whole, whole, whole],
        out_specs=block,
        input_output_aliases={0: 0},
        name="add_edges",
        compiler_params=params(8),
        cost_estimate=cost(30000, 150000),
    )(hbm(rows), first, last, top, bottom)


def sum_kernel(parts, after, after2, out):
    step = pl.program_id(0)

    @pl.when(step < TAPS)
    def _():
        total = parts[0].astype(F32)
        for s in range(1, 32):
            total = total + parts[s].astype(F32)
        out[step] = total.astype(BF)

    @pl.when(step == TAPS)
    def _():
        for h in range(HEADS):
            total = parts[4 * h].astype(F32)
            for s in range(4 * h + 1, 4 * h + 4):
                total = total + parts[s].astype(F32)
            out[TAPS + h] = total.astype(BF)


def sum_partials(parts, after, after2):
    return pl.pallas_call(
        sum_kernel,
        grid=(TAPS + 1,),
        out_shape=sds((TAPS + HEADS, 24, HALF), BF),
        in_specs=[pl.BlockSpec((32, 24, HALF), lambda t: (0, 0, t)), ANY, ANY],
        out_specs=pl.BlockSpec((TAPS + HEADS, 24, HALF), lambda t: (0, 0, 0)),
        name="sum_partials",
        compiler_params=params(8),
        cost_estimate=cost(32 * 24 * 2304, 3700000),
    )(parts, after, after2)


def add_kernel(a, b, after, out):
    out[...] = (a[...].astype(F32) + b[...].astype(F32)) * (1.0 / LOSS_SCALE)


def add_pair(a, b, after):
    return pl.pallas_call(
        add_kernel,
        out_shape=sds((TAPS + HEADS, 24, HALF), F32),
        in_specs=[VM] * 2 + [ANY],
        out_specs=VM,
        name="add_pair",
        compiler_params=params(8),
        cost_estimate=cost(300000, 1500000),
    )(a, b, after)


def place_kernel(core, mine, other, conv, proj):
    def put(low, high):
        conv[:, :, 0:HALF] = low[0:TAPS]
        conv[:, :, HALF:] = high[0:TAPS]
        for h in range(HEADS):
            at = h * HD
            proj[:, at : at + HD] = low[TAPS + h, :, 0:HD]
            proj[:, 1536 + at : 1536 + at + HD] = jnp.concatenate(
                [low[TAPS + h, :, HD:QH], high[TAPS + h, :, 0 : HD // 2]], axis=1
            )
            proj[:, 3072 + at : 3072 + at + HD] = high[TAPS + h, :, HD // 2 : QH]

    @pl.when(core[0] == 0)
    def _():
        put(mine, other)

    @pl.when(core[0] != 0)
    def _():
        put(other, mine)


def place(core, mine, other):
    return pl.pallas_call(
        place_kernel,
        out_shape=(far((TAPS, 24, C), F32), far((24, 4608), F32)),
        in_specs=[SM, VM, VM],
        out_specs=(VM, VM),
        name="place",
        compiler_params=params(8),
        cost_estimate=cost(0, 2500000),
    )(core, mine, other)


UP = [(i, i + 1) for i in range(31)]
DOWN = [(i + 1, i) for i in range(31)]


def local(conv_input, skip_grad, conv_weight, proj_weight, query, key, value, grad):
    core = lax.axis_index("core").astype(jnp.int32).reshape(1)
    head = lax.axis_index(HAX).astype(jnp.int32)
    pair, odd = (head // 2).reshape(1), (head % 2).reshape(1)
    x, skip = conv_input[0], skip_grad[0]

    packed = pack_heads(query[0], key[0], value[0], grad[0])
    own = lax.all_to_all(packed, HAX, 0, 0, tiled=True).reshape(BLK, 4 * HD)
    qg_own, kv_own = split_own(own)
    qg = lax.ppermute(qg_own, "z", A_PAIR)
    kv = lax.ppermute(kv_own, "z", B_PAIR)

    top = lax.ppermute(x[ROWS - 2 :], SEQ, UP)
    bottom = lax.ppermute(x[0:2], SEQ, DOWN)
    edge = jnp.zeros((6, C), BF)
    xp = jnp.concatenate([edge, top, x, bottom, edge], axis=0)
    xp_sib = lax.ppermute(xp, "core", SWAP)
    slope, pooled = conv_forward(xp, conv_weight, own)
    wh = head_weights(pair, odd, proj_weight)

    st = att_stats(own, qg, kv, slope)
    st2 = lax.ppermute(st, "z", A_PAIR)
    dq_own, dq_send, dkv_own, dkv_send = att_grads(own, qg, kv, st, st2)
    dq_in = lax.ppermute(dq_send, "z", A_PAIR)
    dkv_in = lax.ppermute(dkv_send, "z", B_PAIR)
    pooled_blk = lax.all_to_all(pooled, HAX, 0, 0, tiled=True).reshape(BLK, C)
    pool_part, s0, s_send = att_join(core, dq_own, dkv_own, dq_in, dkv_in, wh, pooled_blk)
    parts = lax.all_to_all(pool_part.reshape(HEADS, ATT, C), HAX, 0, 0, tiled=True)
    pooled_sib = lax.ppermute(pooled_blk, "core", SWAP)
    s1 = lax.ppermute(s_send, "core", SWAP)
    xt0, al0 = turn_input(xp)
    xt1, al1 = turn_input(xp_sib)

    pre, y_send, y0, pool = pre_grads(core, parts, skip, slope)
    y1 = lax.ppermute(y_send, "core", SWAP)
    terms = weight_grads(xt0, al0, xt1, al1, y0, y1, pooled_blk, pooled_sib, s0, s1)
    got = lax.all_to_all(terms.reshape(32, 24, 2304), SEQ, 0, 0, tiled=True)

    rows, before, after, first, last = conv_adjoint(pre, conv_weight, skip, pool)
    from_left = lax.ppermute(after, SEQ, UP)
    from_right = lax.ppermute(before, SEQ, DOWN)

    total = sum_partials(got, from_left, from_right)
    total_far = lax.ppermute(total, "yh", SWAP)
    input_grad = add_edges(rows, first, last, from_left, from_right)
    mine = add_pair(total, total_far, input_grad)
    other = lax.ppermute(mine, "core", SWAP)
    conv_grad, proj_grad = place(core, mine, other)
    return input_grad[None], conv_grad, proj_grad


def solution(mesh):
    fine = Mesh(mesh.devices.reshape(2, 2, 2, 4, 4), ("yh", "core", "yl", "x", "z"))
    rows = P(DP, SEQ, None)
    return jax.shard_map(
        local,
        mesh=fine,
        in_specs=(rows, rows, P(), P(), rows, rows, rows, rows),
        out_specs=(rows, P(None, SEQ, None), P(SEQ, None)),
        check_vma=False,
    )
```

```python
import jax
import jax.numpy as jnp
from jax import lax
from jax.experimental import pallas as pl
from jax.experimental.pallas import tpu as pltpu
from jax.sharding import Mesh, PartitionSpec as P

HEADS = 8
TAPS = 5
LOSS_SCALE = 32
HD = 192
C = 768
ROWS = 768
ATT = 48
BLK = 384
FACTOR = 16
HALF = 384
QH = 288
WIDE = 5 * HALF + 8 * QH
SCALE = HD ** (-0.5)
SQRT_HALF = 0.7071067811865476
INV_ROOT_TWO_PI = 0.3989422804014327

BF = jnp.bfloat16
F32 = jnp.float32
DP = ("yh", "core")
SEQ = ("yl", "x", "z")
HAX = ("yl", "x")

NT = (((1,), (1,)), ((), ()))
TN = (((0,), (0,)), ((), ()))

A_PAIR = [(0, 1), (1, 0), (2, 3), (3, 2)]
B_PAIR = [(0, 3), (3, 0), (1, 2), (2, 1)]
SWAP = [(0, 1), (1, 0)]


def sds(shape, dtype):
    return jax.ShapeDtypeStruct(shape, dtype)


def far(shape, dtype):
    return pltpu.HBM(shape, dtype)


def hbm(x):
    return pltpu.with_memory_space_constraint(x, pltpu.HBM)


def params(mib):
    return pltpu.CompilerParams(vmem_limit_bytes=mib * 1024 * 1024)


def cost(flops, nbytes, trans=0):
    return pl.CostEstimate(flops=flops, bytes_accessed=nbytes, transcendentals=trans)


VM = pl.BlockSpec()
ANY = pl.BlockSpec(memory_space=pl.ANY)
SM = pl.BlockSpec(memory_space=pltpu.SMEM)


def nt(a, b):
    return lax.dot_general(a, b, NT, preferred_element_type=F32)


def tn(a, b):
    return lax.dot_general(a, b, TN, preferred_element_type=F32)


def mm(a, b):
    return jnp.dot(a, b, preferred_element_type=F32)


def pack_kernel(q, k, v, g, out):
    for h in range(HEADS):
        cols = slice(h * HD, (h + 1) * HD)
        for slot, ref in enumerate((q, g, k, v)):
            out[h, :, slot * HD : (slot + 1) * HD] = ref[:, cols]


def pack_heads(q, k, v, g):
    return pl.pallas_call(
        pack_kernel,
        out_shape=far((HEADS, ATT, 4 * HD), BF),
        in_specs=[VM] * 4,
        out_specs=VM,
        name="pack_heads",
        compiler_params=params(8),
        cost_estimate=cost(0, 1200000),
    )(hbm(q), hbm(k), hbm(v), hbm(g))


def att_parts(own, qg, kv):
    query = jnp.concatenate([own[:, 0:HD], qg[:, 0:HD]], axis=0)
    grads = jnp.concatenate([own[:, HD : 2 * HD], qg[:, HD : 2 * HD]], axis=0)
    keys = jnp.concatenate([own[:, 2 * HD : 3 * HD], kv[:, 0:HD]], axis=0)
    values = jnp.concatenate([own[:, 3 * HD : 4 * HD], kv[:, HD : 2 * HD]], axis=0)
    return query, grads, keys, values


def stats_kernel(own, qg, kv, after, out):
    query, grads, keys, values = att_parts(own, qg, kv)
    out[...] = jnp.zeros_like(out)
    for i in range(2):
        rows = slice(i * BLK, (i + 1) * BLK)
        scores = nt(keys, query[rows]) * SCALE
        top = jnp.max(scores, axis=0, keepdims=True)
        powers = jnp.exp(scores - top)
        pgrad = nt(values, grads[rows])
        out[0:1, rows] = top
        out[1:2, rows] = jnp.sum(powers, axis=0, keepdims=True)
        out[2:3, rows] = jnp.sum(powers * pgrad, axis=0, keepdims=True)


def att_stats(own, qg, kv, after):
    return pl.pallas_call(
        stats_kernel,
        out_shape=sds((8, 2 * BLK), F32),
        in_specs=[VM] * 3 + [ANY],
        out_specs=VM,
        name="att_stats",
        compiler_params=params(16),
        cost_estimate=cost(8000000000, 1200000, 768 * 768),
    )(own, qg, kv, hbm(after))


def grads_kernel(own, qg, kv, st, st2, after, dq_own, dq_send, dkv_own, dkv_send):
    query, grads, keys, values = att_parts(own, qg, kv)
    dk = jnp.zeros((2 * BLK, HD), F32)
    dv = jnp.zeros((2 * BLK, HD), F32)
    for i in range(2):
        rows = slice(i * BLK, (i + 1) * BLK)
        other = slice((1 - i) * BLK, (2 - i) * BLK)
        m0, m1 = st[0:1, rows], st2[0:1, other]
        top = jnp.maximum(m0, m1)
        e0, e1 = jnp.exp(m0 - top), jnp.exp(m1 - top)
        inv = 1.0 / (st[1:2, rows] * e0 + st2[1:2, other] * e1)
        delta = (st[2:3, rows] * e0 + st2[2:3, other] * e1) * inv
        scores = nt(keys, query[rows]) * SCALE
        probs = jnp.exp(scores - top) * inv
        pgrad = nt(values, grads[rows])
        sgrad = (probs * (pgrad - delta)).astype(BF)
        dq = tn(sgrad, keys) * SCALE
        dk = dk + mm(sgrad, query[rows])
        dv = dv + mm(probs.astype(BF), grads[rows])
        if i == 0:
            dq_own[...] = dq
        else:
            dq_send[:, 0:HD] = dq[0 : BLK // 2].astype(BF)
            dq_send[:, HD : 2 * HD] = dq[BLK // 2 : BLK].astype(BF)
    dk = dk * SCALE
    dkv_own[:, 0:HD] = dk[0:BLK]
    dkv_own[:, HD : 2 * HD] = dv[0:BLK]
    dkv_send[:, 0:HD] = dk[BLK:].astype(BF)
    dkv_send[:, HD : 2 * HD] = dv[BLK:].astype(BF)


def att_grads(own, qg, kv, st, st2, after):
    return pl.pallas_call(
        grads_kernel,
        out_shape=(
            far((BLK, HD), F32),
            sds((BLK // 2, 2 * HD), BF),
            far((BLK, 2 * HD), F32),
            sds((BLK, 2 * HD), BF),
        ),
        in_specs=[VM] * 5 + [ANY],
        out_specs=(VM,) * 4,
        name="att_grads",
        compiler_params=params(20),
        cost_estimate=cost(20000000000, 3000000, 768 * 768),
    )(own, qg, kv, st, st2, hbm(after))


def split_kernel(own, after, qg, kv):
    qg[...] = own[:, 0 : 2 * HD]
    kv[...] = own[:, 2 * HD : 4 * HD]


def split_own(own, after):
    return pl.pallas_call(
        split_kernel,
        out_shape=(sds((BLK, 2 * HD), BF), sds((BLK, 2 * HD), BF)),
        in_specs=[VM, ANY],
        out_specs=(VM, VM),
        name="split_own",
        compiler_params=params(8),
        cost_estimate=cost(0, 1200000),
    )(own, hbm(after))


def head_kernel(pair, odd, wq, wk, wv, after, out):
    for p, ref in enumerate((wq, wk, wv)):
        turned = ref[...].T

        @pl.when(odd[0] == 0)
        def _():
            out[p * HD : (p + 1) * HD, :] = turned[0:HD]

        @pl.when(odd[0] != 0)
        def _():
            out[p * HD : (p + 1) * HD, :] = turned[HD : 2 * HD]


def head_weights(pair, odd, weight, after):
    part = lambda p: pl.BlockSpec((C, 2 * HD), lambda i, pair, odd, p=p: (0, 4 * p + pair[0]))
    return pl.pallas_call(
        head_kernel,
        out_shape=far((3 * HD, C), BF),
        grid_spec=pltpu.PrefetchScalarGridSpec(
            num_scalar_prefetch=2,
            grid=(1,),
            in_specs=[part(0), part(1), part(2), ANY],
            out_specs=pl.BlockSpec((3 * HD, C), lambda i, pair, odd: (0, 0)),
        ),
        name="head_weights",
        compiler_params=params(12),
        cost_estimate=cost(0, 3000000),
    )(pair, odd, hbm(weight), hbm(weight), hbm(weight), after)


def join_kernel(core, dq_own, dkv_own, dq_in, dkv_in, wh, pooled, pool, keep, send, made, sems, sem2):
    others = [
        pltpu.make_async_copy(pooled, pool.at[h, pl.ds(ATT, ATT)], sem2.at[h]) for h in range(HEADS)
    ]
    for other in others:
        other.start()
    dq_got = jnp.concatenate([dq_in[:, 0:HD], dq_in[:, HD : 2 * HD]], axis=0).astype(F32)
    dq = (dq_own[...] + dq_got).astype(BF)
    dkv = (dkv_own[...] + dkv_in[...].astype(F32)).astype(BF)
    qkv = jnp.concatenate([dq, dkv], axis=1)
    stores = []
    for r in range(0, BLK, 2 * ATT):
        made[r : r + 2 * ATT, :] = mm(qkv[r : r + 2 * ATT], wh[...]).astype(BF)
        for h in (r // ATT, r // ATT + 1):
            rows = pl.ds(h * ATT, ATT)
            stores.append(pltpu.make_async_copy(made.at[rows], pool.at[h, pl.ds(0, ATT)], sems.at[h]))
            stores[-1].start()

    @pl.when(core[0] == 0)
    def _():
        keep[...] = qkv[:, 0:QH]
        send[...] = qkv[:, QH : 2 * QH]

    @pl.when(core[0] != 0)
    def _():
        keep[...] = qkv[:, QH : 2 * QH]
        send[...] = qkv[:, 0:QH]

    for copy in others + stores:
        copy.wait()


def att_join(core, dq_own, dkv_own, dq_in, dkv_in, wh, pooled):
    return pl.pallas_call(
        join_kernel,
        out_shape=(far((HEADS, 2 * ATT, C), BF), sds((BLK, QH), BF), sds((BLK, QH), BF)),
        in_specs=[SM] + [VM] * 6,
        out_specs=(pl.BlockSpec(memory_space=pltpu.HBM), VM, VM),
        scratch_shapes=[
            pltpu.VMEM((BLK, C), BF),
            pltpu.SemaphoreType.DMA((HEADS,)),
            pltpu.SemaphoreType.DMA((HEADS,)),
        ],
        name="att_join",
        compiler_params=params(12),
        cost_estimate=cost(10000000000, 3500000),
    )(core, hbm(dq_own), hbm(dkv_own), dq_in, dkv_in, hbm(wh), hbm(pooled))


def conv_kernel(par, x, got1, got2, w, after, pre, xp, xb, xf, wv, pv, xsem, wsems, psems):
    chunks = range(0, ROWS, 256)
    load = pltpu.make_async_copy(x, xb, xsem)
    loads = [pltpu.make_async_copy(w.at[t], wv.at[t], wsems.at[t]) for t in range(TAPS)]
    stores = [
        pltpu.make_async_copy(pv.at[pl.ds(r, 256)], pre.at[pl.ds(r, 256)], psems.at[r // 256])
        for r in chunks
    ]
    load.start()
    loads[0].start()
    xf[0:8, :] = jnp.zeros((8, C), F32)
    xf[8 + ROWS :, :] = jnp.zeros((8, C), F32)
    even = par[0] == 0
    one, two = got1[...].astype(F32), got2[...].astype(F32)
    xf[6:8, :] = jnp.where(even, two, one)
    xf[8 + ROWS : 10 + ROWS, :] = jnp.where(even, one, two)
    load.wait()
    loads[1].start()
    xf[8 : 8 + ROWS, :] = xb[...].astype(F32)
    for t in range(TAPS):
        loads[t].wait()
        if t + 2 < TAPS:
            loads[t + 2].start()
        for r in chunks:
            got = mm(xf[6 + t + r : 6 + t + r + 256, :].astype(BF), wv[t])
            if t == 0:
                pv[r : r + 256, :] = got
            else:
                pv[r : r + 256, :] += got
            if t == TAPS - 1:
                stores[r // 256].start()
    xp[...] = xf[...].astype(BF)
    for store in stores:
        store.wait()


def conv_apply(par, x, got1, got2, w, after):
    near = pl.BlockSpec(memory_space=pltpu.HBM)
    return pl.pallas_call(
        conv_kernel,
        out_shape=(far((ROWS, C), F32), sds((ROWS + 16, C), BF)),
        in_specs=[SM, near, VM, VM, near, ANY],
        out_specs=(near, VM),
        scratch_shapes=[
            pltpu.VMEM((ROWS, C), BF),
            pltpu.VMEM((ROWS + 16, C), F32),
            pltpu.VMEM((TAPS, C, C), BF),
            pltpu.VMEM((ROWS, C), F32),
            pltpu.SemaphoreType.DMA,
            pltpu.SemaphoreType.DMA((TAPS,)),
            pltpu.SemaphoreType.DMA((3,)),
        ],
        name="conv_apply",
        compiler_params=params(24),
        cost_estimate=cost(2 * 5 * 768**3, 9500000),
    )(par, hbm(x), got1, got2, hbm(w), after)


def gelu_kernel(pre, x, after, slope, pooled, means):
    for p in range(0, ROWS, 64):
        value = pre[p : p + 64, :]
        cumul = 0.5 * (1.0 + lax.erf(value * SQRT_HALF))
        bell = value * INV_ROOT_TWO_PI * jnp.exp(-0.5 * value * value)
        slope[p : p + 64, :] = (cumul + bell).astype(BF)
        block = (x[p : p + 64, :].astype(F32) + value * cumul).astype(BF).astype(F32)
        means[p // FACTOR : p // FACTOR + 4, :] = jnp.mean(block.reshape(4, FACTOR, C), axis=1)
    pooled[...] = means[...].astype(BF)


def gelu_pool(pre, x, after):
    return pl.pallas_call(
        gelu_kernel,
        out_shape=(far((ROWS, C), BF), far((ATT, C), BF)),
        in_specs=[VM, VM, ANY],
        out_specs=(VM, VM),
        scratch_shapes=[pltpu.VMEM((ATT, C), F32)],
        name="gelu_pool",
        compiler_params=params(16),
        cost_estimate=cost(3000000000, 5000000, 2 * 768 * 768),
    )(hbm(pre), hbm(x), after)


def turn_kernel(xp, xt, alts, edge):
    for r in range(0, ROWS, 128):
        xt[:, r : r + 128] = xp[8 + r : 8 + r + 128, :].T
    last = xp[8 + ROWS - 128 : 8 + ROWS, :].astype(F32)
    first = xp[8 : 8 + 128, :].astype(F32)
    top = xp[0:16, :].astype(F32)[0:8]
    bottom = xp[ROWS : ROWS + 16, :].astype(F32)[8:16]
    edge[...] = last
    edge[126:128, :] = top[6:8]
    alts[:, 0:128] = edge[...].astype(BF).T
    edge[126:127, :] = last[126:127]
    alts[:, 128:256] = edge[...].astype(BF).T
    edge[...] = first
    edge[0:1, :] = bottom[0:1]
    alts[:, 256:384] = edge[...].astype(BF).T
    edge[1:2, :] = bottom[1:2]
    alts[:, 384:512] = edge[...].astype(BF).T


def turn_input(xp):
    return pl.pallas_call(
        turn_kernel,
        out_shape=(sds((C, ROWS), BF), sds((C, 512), BF)),
        in_specs=[VM],
        out_specs=(VM, VM),
        scratch_shapes=[pltpu.VMEM((128, C), F32)],
        name="turn_input",
        compiler_params=params(12),
        cost_estimate=cost(10 * 768 * 768, 3200000),
    )(xp)


def slope_kernel(
    core, parts, skip, slope, pre, send, keep, pool, skip_v, slope_v, pre_v, pool_v, in_sems, out_sems, pool_sem
):
    chunks = range(0, ROWS, 256)
    loads = []
    for r in chunks:
        rows = pl.ds(r, 256)
        loads.append(pltpu.make_async_copy(skip.at[rows], skip_v.at[rows], in_sems.at[0, r // 256]))
        loads.append(pltpu.make_async_copy(slope.at[rows], slope_v.at[rows], in_sems.at[1, r // 256]))
    for load in loads:
        load.start()
    total = jnp.sum(parts[:, 0:ATT, :].astype(F32), axis=0) * (1.0 / FACTOR)
    pool_v[...] = total
    stores = [pltpu.make_async_copy(pool_v, pool, pool_sem)]
    stores[0].start()
    for r in chunks:
        loads[r // 128].wait()
        loads[r // 128 + 1].wait()
        for p in range(r, r + 256, 128):
            j = p // FACTOR
            piece = jnp.broadcast_to(total[j : j + 8, None, :], (8, FACTOR, C)).reshape(128, C)
            rows = slice(p, p + 128)
            grad = (skip_v[rows, :].astype(F32) + piece) * slope_v[rows, :].astype(F32)
            pre_v[rows, :] = grad.astype(BF)
        rows = pl.ds(r, 256)
        stores.append(pltpu.make_async_copy(pre_v.at[rows], pre.at[rows], out_sems.at[r // 256]))
        stores[-1].start()

    @pl.when(core[0] == 0)
    def _():
        keep[...] = pre_v[:, 0:HALF]
        send[...] = pre_v[:, HALF:]

    @pl.when(core[0] != 0)
    def _():
        keep[...] = pre_v[:, HALF:]
        send[...] = pre_v[:, 0:HALF]

    for store in stores:
        store.wait()


def pre_grads(core, parts, skip, slope):
    near = pl.BlockSpec(memory_space=pltpu.HBM)
    return pl.pallas_call(
        slope_kernel,
        out_shape=(
            far((ROWS, C), BF),
            sds((ROWS, HALF), BF),
            sds((ROWS, HALF), BF),
            far((ATT, C), F32),
        ),
        in_specs=[SM, VM, near, near],
        out_specs=(near, VM, VM, near),
        scratch_shapes=[
            pltpu.VMEM((ROWS, C), BF),
            pltpu.VMEM((ROWS, C), BF),
            pltpu.VMEM((ROWS, C), BF),
            pltpu.VMEM((ATT, C), F32),
            pltpu.SemaphoreType.DMA((2, 3)),
            pltpu.SemaphoreType.DMA((3,)),
            pltpu.SemaphoreType.DMA,
        ],
        name="pre_grads",
        compiler_params=params(12),
        cost_estimate=cost(5 * 768 * 768, 6000000),
    )(core, parts, hbm(skip), hbm(slope))


def weights_kernel(xt0, al0, xt1, al1, y0, y1, p0, p1, s0, s1, out, yf, yt, made, sems):
    def copy(t):
        cols = pl.ds(t * HALF, HALF)
        return pltpu.make_async_copy(made.at[t], out.at[:, cols], sems.at[t])

    def shifted(xt, al, t, rows):
        if t < 2:
            return jnp.concatenate([xt[rows, : ROWS - 128], al[rows, t * 128 : t * 128 + 128]], axis=1)
        if t > 2:
            return jnp.concatenate([al[rows, (t - 1) * 128 : t * 128], xt[rows, 128:]], axis=1)
        return xt[rows, :]

    def pooled(ref):
        return jnp.concatenate([ref[h, ATT : 2 * ATT, :] for h in range(HEADS)], axis=0)

    made[TAPS, :, 0:QH] = (tn(pooled(p0), s0[...]) + tn(pooled(p1), s1[...])).astype(BF)
    made[TAPS, :, QH:HALF] = jnp.zeros((C, HALF - QH), BF)
    copy(TAPS).start()
    for i, ref in enumerate((y0, y1)):
        got = ref[...].astype(F32)
        yf[i, 8 : 8 + ROWS, :] = got
        yf[i, 0:8, :] = got[ROWS - 8 :]
        yf[i, 8 + ROWS : 16 + ROWS, :] = got[0:8]
    for t in (2, 0, 1, 3, 4):
        if t == 2:
            right = [y0[...], y1[...]]
        else:
            for i in range(2):
                yt[t, i] = yf[i, 10 - t : 10 - t + ROWS, :].astype(BF)
            right = [yt[t, 0], yt[t, 1]]
        for r in range(0, C, 256):
            rows = slice(r, r + 256)
            made[t, rows, :] = (
                mm(shifted(xt0, al0, t, rows), right[0]) + mm(shifted(xt1, al1, t, rows), right[1])
            ).astype(BF)
        copy(t).start()
    for t in range(TAPS + 1):
        copy(t).wait()


def weight_grads(xt0, al0, xt1, al1, y0, y1, p0, p1, s0, s1):
    return pl.pallas_call(
        weights_kernel,
        out_shape=far((C, 2304), BF),
        in_specs=[VM] * 10,
        out_specs=pl.BlockSpec(memory_space=pltpu.HBM),
        scratch_shapes=[
            pltpu.VMEM((2, ROWS + 16, HALF), F32),
            pltpu.VMEM((TAPS, 2, ROWS, HALF), BF),
            pltpu.VMEM((TAPS + 1, C, HALF), BF),
            pltpu.SemaphoreType.DMA((TAPS + 1,)),
        ],
        name="weight_grads",
        compiler_params=params(32),
        cost_estimate=cost(2 * 5 * 768 * 1536 * 384, 10000000),
    )(xt0, al0, xt1, al1, y0, y1, p0, p1, s0, s1)


def adjoint_kernel(par, pre, w, skip, pool, out, near, far_, first, last, yf, acc):
    tap = pl.program_id(0)

    @pl.when(tap == 0)
    def _():
        yf[0:16, :] = jnp.zeros((16, C), F32)
        yf[16 : 16 + ROWS, :] = pre[...].astype(F32)
        yf[16 + ROWS :, :] = jnp.zeros((16, C), F32)
        acc[0:8, :] = jnp.zeros((8, C), F32)
        acc[8 + ROWS :, :] = jnp.zeros((8, C), F32)
        for r in range(0, ATT, 8):
            piece = jnp.broadcast_to(pool[r : r + 8, :][:, None, :], (8, FACTOR, C)).reshape(128, C)
            rows = slice(r * FACTOR, r * FACTOR + 128)
            acc[8 + r * FACTOR : 136 + r * FACTOR, :] = skip[rows, :].astype(F32) + piece

    for t in range(TAPS):

        @pl.when(tap == t)
        def _(t=t):
            for r, n in ((0, 256), (256, 256), (512, 272)):
                rows = yf[10 - t + r : 10 - t + r + n, :].astype(BF)
                acc[r : r + n, :] += nt(rows, w[0])

    @pl.when(tap == TAPS - 1)
    def _():
        out[...] = acc[8 : 8 + ROWS, :].astype(BF)
        first[...] = acc[8:16, :]
        last[...] = acc[ROWS : ROWS + 8, :]
        even = par[0] == 0
        before, after = acc[0:8, :], acc[ROWS + 8 :, :]
        near[...] = jnp.where(even, after, before)
        far_[...] = jnp.where(even, before, after)


def conv_adjoint(par, pre, w, skip, pool):
    whole = lambda a, b: pl.BlockSpec((a, b), lambda t: (0, 0))
    return pl.pallas_call(
        adjoint_kernel,
        grid=(TAPS,),
        out_shape=(far((ROWS, C), BF),) + (sds((8, C), F32),) * 4,
        in_specs=[
            SM,
            whole(ROWS, C),
            pl.BlockSpec((1, C, C), lambda t: (t, 0, 0)),
            whole(ROWS, C),
            whole(ATT, C),
        ],
        out_specs=(whole(ROWS, C),) + (whole(8, C),) * 4,
        scratch_shapes=[pltpu.VMEM((ROWS + 32, C), F32), pltpu.VMEM((ROWS + 16, C), F32)],
        name="conv_adjoint",
        compiler_params=params(24),
        cost_estimate=cost(2 * 5 * 768**3, 9500000),
    )(par, hbm(pre), hbm(w), hbm(skip), hbm(pool))


def edge_kernel(par, rows, first, last, got1, got2, out):
    step = pl.program_id(0)
    held = rows[...].astype(F32)
    even = par[0] == 0

    @pl.when(step == 0)
    def _():
        top = jnp.where(even, got2[...], got1[...])
        out[...] = jnp.concatenate([first[...] + top, held[8:16]], axis=0).astype(BF)

    @pl.when(step != 0)
    def _():
        bottom = jnp.where(even, got1[...], got2[...])
        out[...] = jnp.concatenate([held[0:8], last[...] + bottom], axis=0).astype(BF)


def add_edges(par, rows, first, last, got1, got2):
    block = pl.BlockSpec((16, C), lambda i: (i * (ROWS // 16 - 1), 0))
    whole = pl.BlockSpec((8, C), lambda i: (0, 0))
    return pl.pallas_call(
        edge_kernel,
        grid=(2,),
        out_shape=far((ROWS, C), BF),
        in_specs=[SM, block, whole, whole, whole, whole],
        out_specs=block,
        input_output_aliases={1: 0},
        name="add_edges",
        compiler_params=params(8),
        cost_estimate=cost(30000, 150000),
    )(par, hbm(rows), first, last, got1, got2)


def sum_kernel(parts, after, after2, out):
    step = pl.program_id(0)

    @pl.when(step < TAPS)
    def _():
        total = parts[0].astype(F32)
        for s in range(1, 32):
            total = total + parts[s].astype(F32)
        out[:, pl.ds(pl.multiple_of(step * HALF, HALF), HALF)] = total.astype(BF)

    @pl.when(step == TAPS)
    def _():
        for h in range(HEADS):
            total = parts[4 * h].astype(F32)
            for s in range(4 * h + 1, 4 * h + 4):
                total = total + parts[s].astype(F32)
            at = TAPS * HALF + h * QH
            out[:, at : at + QH] = total[:, 0:QH].astype(BF)


def sum_partials(parts, after, after2):
    return pl.pallas_call(
        sum_kernel,
        grid=(TAPS + 1,),
        out_shape=sds((24, WIDE), BF),
        in_specs=[pl.BlockSpec((32, 24, HALF), lambda t: (0, 0, t)), ANY, ANY],
        out_specs=pl.BlockSpec((24, WIDE), lambda t: (0, 0)),
        name="sum_partials",
        compiler_params=params(8),
        cost_estimate=cost(32 * 24 * 2304, 3700000),
    )(parts, hbm(after), hbm(after2))


def add_kernel(a, b, after, out):
    out[...] = (a[...].astype(F32) + b[...].astype(F32)) * (1.0 / LOSS_SCALE)


def add_pair(a, b, after):
    return pl.pallas_call(
        add_kernel,
        out_shape=sds((24, WIDE), F32),
        in_specs=[VM] * 2 + [ANY],
        out_specs=VM,
        name="add_pair",
        compiler_params=params(8),
        cost_estimate=cost(300000, 1500000),
    )(a, b, hbm(after))


def place_kernel(core, mine, other, conv, proj):
    def put(low, high):
        for t in range(TAPS):
            conv[t, :, 0:HALF] = low[:, t * HALF : (t + 1) * HALF]
            conv[t, :, HALF:] = high[:, t * HALF : (t + 1) * HALF]
        for h in range(HEADS):
            at = h * HD
            got = TAPS * HALF + h * QH
            proj[:, at : at + HD] = low[:, got : got + HD]
            proj[:, 1536 + at : 1536 + at + HD] = jnp.concatenate(
                [low[:, got + HD : got + QH], high[:, got : got + HD // 2]], axis=1
            )
            proj[:, 3072 + at : 3072 + at + HD] = high[:, got + HD // 2 : got + QH]

    @pl.when(core[0] == 0)
    def _():
        put(mine, other)

    @pl.when(core[0] != 0)
    def _():
        put(other, mine)


def place(core, mine, other):
    return pl.pallas_call(
        place_kernel,
        out_shape=(far((TAPS, 24, C), F32), far((24, 4608), F32)),
        in_specs=[SM, VM, VM],
        out_specs=(VM, VM),
        name="place",
        compiler_params=params(8),
        cost_estimate=cost(0, 2500000),
    )(core, mine, other)


NEAR = [(i, i ^ 1) for i in range(32)]
NEXT = [pair for i in range(1, 31, 2) for pair in ((i, i + 1), (i + 1, i))]


def local(conv_input, skip_grad, conv_weight, proj_weight, query, key, value, grad):
    core = lax.axis_index("core").astype(jnp.int32).reshape(1)
    head = lax.axis_index(HAX).astype(jnp.int32)
    pair, odd = (head // 2).reshape(1), (head % 2).reshape(1)
    x, skip = conv_input[0], skip_grad[0]

    packed = pack_heads(query[0], key[0], value[0], grad[0])
    own = lax.all_to_all(packed, HAX, 0, 0, tiled=True).reshape(BLK, 4 * HD)
    wh = head_weights(pair, odd, proj_weight, packed)
    qg_own, kv_own = split_own(own, wh)
    qg = lax.ppermute(qg_own, "z", A_PAIR)
    kv = lax.ppermute(kv_own, "z", B_PAIR)

    par = (lax.axis_index("z") % 2).astype(jnp.int32).reshape(1)
    head_rows, tail_rows = x[0:2], x[ROWS - 2 :]
    got1 = lax.ppermute(jnp.where(par[0] == 0, tail_rows, head_rows), SEQ, NEAR)
    got2 = lax.ppermute(jnp.where(par[0] == 0, head_rows, tail_rows), SEQ, NEXT)
    early, xp = conv_apply(par, x, got1, got2, conv_weight, qg_own)
    xp_sib = lax.ppermute(xp, "core", SWAP)

    st = att_stats(own, qg, kv, early)
    st2 = lax.ppermute(st, "z", A_PAIR)
    dq_own, dq_send, dkv_own, dkv_send = att_grads(own, qg, kv, st, st2, wh)
    dq_in = lax.ppermute(dq_send, "z", A_PAIR)
    dkv_in = lax.ppermute(dkv_send, "z", B_PAIR)
    slope, pooled = gelu_pool(early, x, dq_send)
    pool_part, s0, s_send = att_join(core, dq_own, dkv_own, dq_in, dkv_in, wh, pooled)
    parts = lax.all_to_all(pool_part, HAX, 0, 0, tiled=True)
    parts_sib = lax.ppermute(parts, "core", SWAP)
    s1 = lax.ppermute(s_send, "core", SWAP)
    xt0, al0 = turn_input(xp)
    xt1, al1 = turn_input(xp_sib)

    pre, y_send, y0, pool = pre_grads(core, parts, skip, slope)
    y1 = lax.ppermute(y_send, "core", SWAP)
    terms = weight_grads(xt0, al0, xt1, al1, y0, y1, parts, parts_sib, s0, s1)
    got = lax.all_to_all(terms.reshape(32, 24, 2304), SEQ, 0, 0, tiled=True)

    rows, near, next_, first, last = conv_adjoint(par, pre, conv_weight, skip, pool)
    rim1 = lax.ppermute(near, SEQ, NEAR)
    rim2 = lax.ppermute(next_, SEQ, NEXT)

    total = sum_partials(got, rim1, rim2)
    total_far = lax.ppermute(total, "yh", SWAP)
    input_grad = add_edges(par, rows, first, last, rim1, rim2)
    mine = add_pair(total, total_far, input_grad)
    other = lax.ppermute(mine, "core", SWAP)
    conv_grad, proj_grad = place(core, mine, other)
    return input_grad[None], conv_grad, proj_grad


def solution(mesh):
    fine = Mesh(mesh.devices.reshape(2, 2, 2, 4, 4), ("yh", "core", "yl", "x", "z"))
    rows = P(DP, SEQ, None)
    return jax.shard_map(
        local,
        mesh=fine,
        in_specs=(rows, rows, P(), P(), rows, rows, rows, rows),
        out_specs=(rows, P(None, SEQ, None), P(SEQ, None)),
        check_vma=False,
    )
```

```python
import jax
import jax.numpy as jnp
from jax import lax
from jax.experimental import pallas as pl
from jax.experimental.pallas import tpu as pltpu
from jax.sharding import Mesh, PartitionSpec as P

HEADS = 8
TAPS = 5
LOSS_SCALE = 32
HD = 192
C = 768
ROWS = 768
ATT = 48
BLK = 384
FACTOR = 16
HALF = 384
QH = 288
WIDE = 5 * HALF + 8 * QH
SCALE = HD ** (-0.5)
SQRT_HALF = 0.7071067811865476
INV_ROOT_TWO_PI = 0.3989422804014327

BF = jnp.bfloat16
F32 = jnp.float32
DP = ("yh", "core")
SEQ = ("yl", "x", "z")
HAX = ("yl", "x")

NT = (((1,), (1,)), ((), ()))
TN = (((0,), (0,)), ((), ()))

A_PAIR = [(0, 1), (1, 0), (2, 3), (3, 2)]
B_PAIR = [(0, 3), (3, 0), (1, 2), (2, 1)]
SWAP = [(0, 1), (1, 0)]


def sds(shape, dtype):
    return jax.ShapeDtypeStruct(shape, dtype)


def far(shape, dtype):
    return pltpu.HBM(shape, dtype)


def hbm(x):
    return pltpu.with_memory_space_constraint(x, pltpu.HBM)


def params(mib):
    return pltpu.CompilerParams(vmem_limit_bytes=mib * 1024 * 1024)


def cost(flops, nbytes, trans=0):
    return pl.CostEstimate(flops=flops, bytes_accessed=nbytes, transcendentals=trans)


VM = pl.BlockSpec()
ANY = pl.BlockSpec(memory_space=pl.ANY)
SM = pl.BlockSpec(memory_space=pltpu.SMEM)


def nt(a, b):
    return lax.dot_general(a, b, NT, preferred_element_type=F32)


def tn(a, b):
    return lax.dot_general(a, b, TN, preferred_element_type=F32)


def mm(a, b):
    return jnp.dot(a, b, preferred_element_type=F32)


def pack_kernel(q, k, v, g, out, held, made, in_sems, out_sems):
    loads = [pltpu.make_async_copy(ref, held.at[i], in_sems.at[i]) for i, ref in enumerate((q, g, k, v))]
    for load in loads:
        load.start()
    stores = []
    for half in range(2):
        for i in (2 * half, 2 * half + 1):
            loads[i].wait()
            for h in range(HEADS):
                made[h, :, i * HD : (i + 1) * HD] = held[i, :, h * HD : (h + 1) * HD]
        cols = pl.ds(half * 2 * HD, 2 * HD)
        stores.append(pltpu.make_async_copy(made.at[:, :, cols], out.at[:, :, cols], out_sems.at[half]))
        stores[-1].start()
    for store in stores:
        store.wait()


def pack_heads(q, k, v, g):
    near = pl.BlockSpec(memory_space=pltpu.HBM)
    return pl.pallas_call(
        pack_kernel,
        out_shape=far((HEADS, ATT, 4 * HD), BF),
        in_specs=[near] * 4,
        out_specs=near,
        scratch_shapes=[
            pltpu.VMEM((4, ATT, HEADS * HD), BF),
            pltpu.VMEM((HEADS, ATT, 4 * HD), BF),
            pltpu.SemaphoreType.DMA((4,)),
            pltpu.SemaphoreType.DMA((2,)),
        ],
        name="pack_heads",
        compiler_params=params(8),
        cost_estimate=cost(0, 1200000),
    )(hbm(q), hbm(k), hbm(v), hbm(g))


def att_parts(own, qg, kv):
    query = jnp.concatenate([own[:, 0:HD], qg[:, 0:HD]], axis=0)
    grads = jnp.concatenate([own[:, HD : 2 * HD], qg[:, HD : 2 * HD]], axis=0)
    keys = jnp.concatenate([own[:, 2 * HD : 3 * HD], kv[:, 0:HD]], axis=0)
    values = jnp.concatenate([own[:, 3 * HD : 4 * HD], kv[:, HD : 2 * HD]], axis=0)
    return query, grads, keys, values


def stats_kernel(own, qg, kv, after, out):
    query, grads, keys, values = att_parts(own, qg, kv)
    out[...] = jnp.zeros_like(out)
    for i in range(2):
        rows = slice(i * BLK, (i + 1) * BLK)
        scores = nt(keys, query[rows]) * SCALE
        top = jnp.max(scores, axis=0, keepdims=True)
        powers = jnp.exp(scores - top)
        pgrad = nt(values, grads[rows])
        out[0:1, rows] = top
        out[1:2, rows] = jnp.sum(powers, axis=0, keepdims=True)
        out[2:3, rows] = jnp.sum(powers * pgrad, axis=0, keepdims=True)


def att_stats(own, qg, kv, after):
    return pl.pallas_call(
        stats_kernel,
        out_shape=sds((8, 2 * BLK), F32),
        in_specs=[VM] * 3 + [ANY],
        out_specs=VM,
        name="att_stats",
        compiler_params=params(16),
        cost_estimate=cost(8000000000, 1200000, 768 * 768),
    )(own, qg, kv, hbm(after))


def grads_kernel(own, qg, kv, st, st2, after, dq_own, dq_send, dkv_own, dkv_send):
    query, grads, keys, values = att_parts(own, qg, kv)
    dk = jnp.zeros((2 * BLK, HD), F32)
    dv = jnp.zeros((2 * BLK, HD), F32)
    for i in range(2):
        rows = slice(i * BLK, (i + 1) * BLK)
        other = slice((1 - i) * BLK, (2 - i) * BLK)
        m0, m1 = st[0:1, rows], st2[0:1, other]
        top = jnp.maximum(m0, m1)
        e0, e1 = jnp.exp(m0 - top), jnp.exp(m1 - top)
        inv = 1.0 / (st[1:2, rows] * e0 + st2[1:2, other] * e1)
        delta = (st[2:3, rows] * e0 + st2[2:3, other] * e1) * inv
        scores = nt(keys, query[rows]) * SCALE
        probs = jnp.exp(scores - top) * inv
        pgrad = nt(values, grads[rows])
        sgrad = (probs * (pgrad - delta)).astype(BF)
        dq = tn(sgrad, keys) * SCALE
        dk = dk + mm(sgrad, query[rows])
        dv = dv + mm(probs.astype(BF), grads[rows])
        if i == 0:
            dq_own[...] = dq
        else:
            dq_send[:, 0:HD] = dq[0 : BLK // 2].astype(BF)
            dq_send[:, HD : 2 * HD] = dq[BLK // 2 : BLK].astype(BF)
    dk = dk * SCALE
    dkv_own[:, 0:HD] = dk[0:BLK]
    dkv_own[:, HD : 2 * HD] = dv[0:BLK]
    dkv_send[:, 0:HD] = dk[BLK:].astype(BF)
    dkv_send[:, HD : 2 * HD] = dv[BLK:].astype(BF)


def att_grads(own, qg, kv, st, st2, after):
    return pl.pallas_call(
        grads_kernel,
        out_shape=(
            far((BLK, HD), F32),
            sds((BLK // 2, 2 * HD), BF),
            far((BLK, 2 * HD), F32),
            sds((BLK, 2 * HD), BF),
        ),
        in_specs=[VM] * 5 + [ANY],
        out_specs=(VM,) * 4,
        name="att_grads",
        compiler_params=params(20),
        cost_estimate=cost(20000000000, 3000000, 768 * 768),
    )(own, qg, kv, st, st2, hbm(after))


def split_kernel(own, after, qg, kv):
    qg[...] = own[:, 0 : 2 * HD]
    kv[...] = own[:, 2 * HD : 4 * HD]


def split_own(own, after):
    return pl.pallas_call(
        split_kernel,
        out_shape=(sds((BLK, 2 * HD), BF), sds((BLK, 2 * HD), BF)),
        in_specs=[VM, ANY],
        out_specs=(VM, VM),
        name="split_own",
        compiler_params=params(8),
        cost_estimate=cost(0, 1200000),
    )(own, hbm(after))


def head_kernel(pair, odd, wq, wk, wv, after, out):
    @pl.when(odd[0] == 0)
    def _():
        for p, ref in enumerate((wq, wk, wv)):
            out[p * HD : (p + 1) * HD, :] = ref[:, 0:HD].T

    @pl.when(odd[0] != 0)
    def _():
        for p, ref in enumerate((wq, wk, wv)):
            out[p * HD : (p + 1) * HD, :] = ref[:, HD : 2 * HD].T


def head_weights(pair, odd, weight, after):
    part = lambda p: pl.BlockSpec((C, 2 * HD), lambda i, pair, odd, p=p: (0, 4 * p + pair[0]))
    return pl.pallas_call(
        head_kernel,
        out_shape=far((3 * HD, C), BF),
        grid_spec=pltpu.PrefetchScalarGridSpec(
            num_scalar_prefetch=2,
            grid=(1,),
            in_specs=[part(0), part(1), part(2), ANY],
            out_specs=pl.BlockSpec((3 * HD, C), lambda i, pair, odd: (0, 0)),
        ),
        name="head_weights",
        compiler_params=params(12),
        cost_estimate=cost(0, 3000000),
    )(pair, odd, hbm(weight), hbm(weight), hbm(weight), after)


def join_kernel(core, dq_own, dkv_own, dq_in, dkv_in, wh, pooled, pool, keep, send, made, sems, sem2):
    others = [
        pltpu.make_async_copy(pooled, pool.at[h, pl.ds(ATT, ATT)], sem2.at[h]) for h in range(HEADS)
    ]
    for other in others:
        other.start()
    dq_got = jnp.concatenate([dq_in[:, 0:HD], dq_in[:, HD : 2 * HD]], axis=0).astype(F32)
    dq = (dq_own[...] + dq_got).astype(BF)
    dkv = (dkv_own[...] + dkv_in[...].astype(F32)).astype(BF)
    qkv = jnp.concatenate([dq, dkv], axis=1)
    stores = []
    for r in range(0, BLK, 2 * ATT):
        made[r : r + 2 * ATT, :] = mm(qkv[r : r + 2 * ATT], wh[...]).astype(BF)
        for h in (r // ATT, r // ATT + 1):
            rows = pl.ds(h * ATT, ATT)
            stores.append(pltpu.make_async_copy(made.at[rows], pool.at[h, pl.ds(0, ATT)], sems.at[h]))
            stores[-1].start()

    @pl.when(core[0] == 0)
    def _():
        keep[...] = qkv[:, 0:QH]
        send[...] = qkv[:, QH : 2 * QH]

    @pl.when(core[0] != 0)
    def _():
        keep[...] = qkv[:, QH : 2 * QH]
        send[...] = qkv[:, 0:QH]

    for copy in others + stores:
        copy.wait()


def att_join(core, dq_own, dkv_own, dq_in, dkv_in, wh, pooled):
    return pl.pallas_call(
        join_kernel,
        out_shape=(far((HEADS, 2 * ATT, C), BF), sds((BLK, QH), BF), sds((BLK, QH), BF)),
        in_specs=[SM] + [VM] * 6,
        out_specs=(pl.BlockSpec(memory_space=pltpu.HBM), VM, VM),
        scratch_shapes=[
            pltpu.VMEM((BLK, C), BF),
            pltpu.SemaphoreType.DMA((HEADS,)),
            pltpu.SemaphoreType.DMA((HEADS,)),
        ],
        name="att_join",
        compiler_params=params(12),
        cost_estimate=cost(10000000000, 3500000),
    )(core, hbm(dq_own), hbm(dkv_own), dq_in, dkv_in, hbm(wh), hbm(pooled))


def conv_kernel(par, x, got1, got2, w, after, pre, xp, xb, xf, wv, pv, xsem, wsems, psems):
    chunks = range(0, ROWS, 256)
    load = pltpu.make_async_copy(x, xb, xsem)
    loads = [pltpu.make_async_copy(w.at[t], wv.at[t], wsems.at[t]) for t in range(TAPS)]
    stores = [
        pltpu.make_async_copy(pv.at[pl.ds(r, 256)], pre.at[pl.ds(r, 256)], psems.at[r // 256])
        for r in chunks
    ]
    load.start()
    loads[0].start()
    xf[0:8, :] = jnp.zeros((8, C), F32)
    xf[8 + ROWS :, :] = jnp.zeros((8, C), F32)
    even = par[0] == 0
    one, two = got1[...].astype(F32), got2[...].astype(F32)
    xf[6:8, :] = jnp.where(even, two, one)
    xf[8 + ROWS : 10 + ROWS, :] = jnp.where(even, one, two)
    load.wait()
    loads[1].start()
    xf[8 : 8 + ROWS, :] = xb[...].astype(F32)
    for t in range(TAPS):
        loads[t].wait()
        if t + 2 < TAPS:
            loads[t + 2].start()
        for r in chunks:
            got = mm(xf[6 + t + r : 6 + t + r + 256, :].astype(BF), wv[t])
            if t == 0:
                pv[r : r + 256, :] = got
            else:
                pv[r : r + 256, :] += got
            if t == TAPS - 1:
                stores[r // 256].start()
    xp[...] = xf[...].astype(BF)
    for store in stores:
        store.wait()


def conv_apply(par, x, got1, got2, w, after):
    near = pl.BlockSpec(memory_space=pltpu.HBM)
    return pl.pallas_call(
        conv_kernel,
        out_shape=(far((ROWS, C), F32), sds((ROWS + 16, C), BF)),
        in_specs=[SM, near, VM, VM, near, ANY],
        out_specs=(near, VM),
        scratch_shapes=[
            pltpu.VMEM((ROWS, C), BF),
            pltpu.VMEM((ROWS + 16, C), F32),
            pltpu.VMEM((TAPS, C, C), BF),
            pltpu.VMEM((ROWS, C), F32),
            pltpu.SemaphoreType.DMA,
            pltpu.SemaphoreType.DMA((TAPS,)),
            pltpu.SemaphoreType.DMA((3,)),
        ],
        name="conv_apply",
        compiler_params=params(24),
        cost_estimate=cost(2 * 5 * 768**3, 9500000),
    )(par, hbm(x), got1, got2, hbm(w), after)


def gelu_kernel(pre, x, after, slope, pooled, means):
    for p in range(0, ROWS, 64):
        value = pre[p : p + 64, :]
        cumul = 0.5 * (1.0 + lax.erf(value * SQRT_HALF))
        bell = value * INV_ROOT_TWO_PI * jnp.exp(-0.5 * value * value)
        slope[p : p + 64, :] = (cumul + bell).astype(BF)
        block = (x[p : p + 64, :].astype(F32) + value * cumul).astype(BF).astype(F32)
        means[p // FACTOR : p // FACTOR + 4, :] = jnp.mean(block.reshape(4, FACTOR, C), axis=1)
    pooled[...] = means[...].astype(BF)


def gelu_pool(pre, x, after):
    return pl.pallas_call(
        gelu_kernel,
        out_shape=(far((ROWS, C), BF), far((ATT, C), BF)),
        in_specs=[VM, VM, ANY],
        out_specs=(VM, VM),
        scratch_shapes=[pltpu.VMEM((ATT, C), F32)],
        name="gelu_pool",
        compiler_params=params(16),
        cost_estimate=cost(3000000000, 5000000, 2 * 768 * 768),
    )(hbm(pre), hbm(x), after)


def turn_kernel(xp, xt, alts, edge):
    for r in range(0, ROWS, 128):
        xt[:, r : r + 128] = xp[8 + r : 8 + r + 128, :].T
    last = xp[8 + ROWS - 128 : 8 + ROWS, :].astype(F32)
    first = xp[8 : 8 + 128, :].astype(F32)
    top = xp[0:16, :].astype(F32)[0:8]
    bottom = xp[ROWS : ROWS + 16, :].astype(F32)[8:16]
    edge[...] = last
    edge[126:128, :] = top[6:8]
    alts[:, 0:128] = edge[...].astype(BF).T
    edge[126:127, :] = last[126:127]
    alts[:, 128:256] = edge[...].astype(BF).T
    edge[...] = first
    edge[0:1, :] = bottom[0:1]
    alts[:, 256:384] = edge[...].astype(BF).T
    edge[1:2, :] = bottom[1:2]
    alts[:, 384:512] = edge[...].astype(BF).T


def turn_input(xp):
    return pl.pallas_call(
        turn_kernel,
        out_shape=(sds((C, ROWS), BF), sds((C, 512), BF)),
        in_specs=[VM],
        out_specs=(VM, VM),
        scratch_shapes=[pltpu.VMEM((128, C), F32)],
        name="turn_input",
        compiler_params=params(12),
        cost_estimate=cost(10 * 768 * 768, 3200000),
    )(xp)


def slope_kernel(
    core, parts, skip, slope, pre, send, keep, pool, skip_v, slope_v, pre_v, pool_v, in_sems, out_sems, pool_sem
):
    chunks = range(0, ROWS, 256)
    loads = []
    for r in chunks:
        rows = pl.ds(r, 256)
        loads.append(pltpu.make_async_copy(skip.at[rows], skip_v.at[rows], in_sems.at[0, r // 256]))
        loads.append(pltpu.make_async_copy(slope.at[rows], slope_v.at[rows], in_sems.at[1, r // 256]))
    for load in loads:
        load.start()
    total = jnp.sum(parts[:, 0:ATT, :].astype(F32), axis=0) * (1.0 / FACTOR)
    pool_v[...] = total
    stores = [pltpu.make_async_copy(pool_v, pool, pool_sem)]
    stores[0].start()
    for r in chunks:
        loads[r // 128].wait()
        loads[r // 128 + 1].wait()
        for p in range(r, r + 256, 128):
            j = p // FACTOR
            piece = jnp.broadcast_to(total[j : j + 8, None, :], (8, FACTOR, C)).reshape(128, C)
            rows = slice(p, p + 128)
            grad = (skip_v[rows, :].astype(F32) + piece) * slope_v[rows, :].astype(F32)
            pre_v[rows, :] = grad.astype(BF)
        rows = pl.ds(r, 256)
        stores.append(pltpu.make_async_copy(pre_v.at[rows], pre.at[rows], out_sems.at[r // 256]))
        stores[-1].start()

    @pl.when(core[0] == 0)
    def _():
        keep[...] = pre_v[:, 0:HALF]
        send[...] = pre_v[:, HALF:]

    @pl.when(core[0] != 0)
    def _():
        keep[...] = pre_v[:, HALF:]
        send[...] = pre_v[:, 0:HALF]

    for store in stores:
        store.wait()


def pre_grads(core, parts, skip, slope):
    near = pl.BlockSpec(memory_space=pltpu.HBM)
    return pl.pallas_call(
        slope_kernel,
        out_shape=(
            far((ROWS, C), BF),
            sds((ROWS, HALF), BF),
            sds((ROWS, HALF), BF),
            far((ATT, C), F32),
        ),
        in_specs=[SM, VM, near, near],
        out_specs=(near, VM, VM, near),
        scratch_shapes=[
            pltpu.VMEM((ROWS, C), BF),
            pltpu.VMEM((ROWS, C), BF),
            pltpu.VMEM((ROWS, C), BF),
            pltpu.VMEM((ATT, C), F32),
            pltpu.SemaphoreType.DMA((2, 3)),
            pltpu.SemaphoreType.DMA((3,)),
            pltpu.SemaphoreType.DMA,
        ],
        name="pre_grads",
        compiler_params=params(12),
        cost_estimate=cost(5 * 768 * 768, 6000000),
    )(core, parts, hbm(skip), hbm(slope))


def weights_kernel(xt0, al0, xt1, al1, y0, y1, p0, p1, s0, s1, out, yf, yt, made, sems):
    def copy(t):
        cols = pl.ds(t * HALF, HALF)
        return pltpu.make_async_copy(made.at[t], out.at[:, cols], sems.at[t])

    def shifted(xt, al, t, rows):
        if t < 2:
            return jnp.concatenate([xt[rows, : ROWS - 128], al[rows, t * 128 : t * 128 + 128]], axis=1)
        if t > 2:
            return jnp.concatenate([al[rows, (t - 1) * 128 : t * 128], xt[rows, 128:]], axis=1)
        return xt[rows, :]

    def pooled(ref):
        return jnp.concatenate([ref[h, ATT : 2 * ATT, :] for h in range(HEADS)], axis=0)

    made[TAPS, :, 0:QH] = (tn(pooled(p0), s0[...]) + tn(pooled(p1), s1[...])).astype(BF)
    made[TAPS, :, QH:HALF] = jnp.zeros((C, HALF - QH), BF)
    copy(TAPS).start()
    for i, ref in enumerate((y0, y1)):
        got = ref[...].astype(F32)
        yf[i, 8 : 8 + ROWS, :] = got
        yf[i, 0:8, :] = got[ROWS - 8 :]
        yf[i, 8 + ROWS : 16 + ROWS, :] = got[0:8]
    for t in (2, 0, 1, 3, 4):
        if t == 2:
            right = [y0[...], y1[...]]
        else:
            for i in range(2):
                yt[t, i] = yf[i, 10 - t : 10 - t + ROWS, :].astype(BF)
            right = [yt[t, 0], yt[t, 1]]
        for r in range(0, C, 256):
            rows = slice(r, r + 256)
            made[t, rows, :] = (
                mm(shifted(xt0, al0, t, rows), right[0]) + mm(shifted(xt1, al1, t, rows), right[1])
            ).astype(BF)
        copy(t).start()
    for t in range(TAPS + 1):
        copy(t).wait()


def weight_grads(xt0, al0, xt1, al1, y0, y1, p0, p1, s0, s1):
    return pl.pallas_call(
        weights_kernel,
        out_shape=far((C, 2304), BF),
        in_specs=[VM] * 10,
        out_specs=pl.BlockSpec(memory_space=pltpu.HBM),
        scratch_shapes=[
            pltpu.VMEM((2, ROWS + 16, HALF), F32),
            pltpu.VMEM((TAPS, 2, ROWS, HALF), BF),
            pltpu.VMEM((TAPS + 1, C, HALF), BF),
            pltpu.SemaphoreType.DMA((TAPS + 1,)),
        ],
        name="weight_grads",
        compiler_params=params(32),
        cost_estimate=cost(2 * 5 * 768 * 1536 * 384, 10000000),
    )(xt0, al0, xt1, al1, y0, y1, p0, p1, s0, s1)


def adjoint_kernel(par, pre, w, skip, pool, out, near, far_, first, last, yf, acc):
    tap = pl.program_id(0)

    @pl.when(tap == 0)
    def _():
        yf[0:16, :] = jnp.zeros((16, C), F32)
        yf[16 : 16 + ROWS, :] = pre[...].astype(F32)
        yf[16 + ROWS :, :] = jnp.zeros((16, C), F32)
        acc[0:8, :] = jnp.zeros((8, C), F32)
        acc[8 + ROWS :, :] = jnp.zeros((8, C), F32)
        for r in range(0, ATT, 8):
            piece = jnp.broadcast_to(pool[r : r + 8, :][:, None, :], (8, FACTOR, C)).reshape(128, C)
            rows = slice(r * FACTOR, r * FACTOR + 128)
            acc[8 + r * FACTOR : 136 + r * FACTOR, :] = skip[rows, :].astype(F32) + piece

    for t in range(TAPS):

        @pl.when(tap == t)
        def _(t=t):
            for r, n in ((0, 256), (256, 256), (512, 272)):
                rows = yf[10 - t + r : 10 - t + r + n, :].astype(BF)
                acc[r : r + n, :] += nt(rows, w[0])

    @pl.when(tap == TAPS - 1)
    def _():
        out[...] = acc[8 : 8 + ROWS, :].astype(BF)
        first[...] = acc[8:16, :]
        last[...] = acc[ROWS : ROWS + 8, :]
        even = par[0] == 0
        before, after = acc[0:8, :], acc[ROWS + 8 :, :]
        near[...] = jnp.where(even, after, before)
        far_[...] = jnp.where(even, before, after)


def conv_adjoint(par, pre, w, skip, pool):
    whole = lambda a, b: pl.BlockSpec((a, b), lambda t: (0, 0))
    return pl.pallas_call(
        adjoint_kernel,
        grid=(TAPS,),
        out_shape=(far((ROWS, C), BF),) + (sds((8, C), F32),) * 4,
        in_specs=[
            SM,
            whole(ROWS, C),
            pl.BlockSpec((1, C, C), lambda t: (t, 0, 0)),
            whole(ROWS, C),
            whole(ATT, C),
        ],
        out_specs=(whole(ROWS, C),) + (whole(8, C),) * 4,
        scratch_shapes=[pltpu.VMEM((ROWS + 32, C), F32), pltpu.VMEM((ROWS + 16, C), F32)],
        name="conv_adjoint",
        compiler_params=params(24),
        cost_estimate=cost(2 * 5 * 768**3, 9500000),
    )(par, hbm(pre), hbm(w), hbm(skip), hbm(pool))


def edge_kernel(par, rows, first, last, got1, got2, out):
    step = pl.program_id(0)
    held = rows[...].astype(F32)
    even = par[0] == 0

    @pl.when(step == 0)
    def _():
        top = jnp.where(even, got2[...], got1[...])
        out[...] = jnp.concatenate([first[...] + top, held[8:16]], axis=0).astype(BF)

    @pl.when(step != 0)
    def _():
        bottom = jnp.where(even, got1[...], got2[...])
        out[...] = jnp.concatenate([held[0:8], last[...] + bottom], axis=0).astype(BF)


def add_edges(par, rows, first, last, got1, got2):
    block = pl.BlockSpec((16, C), lambda i: (i * (ROWS // 16 - 1), 0))
    whole = pl.BlockSpec((8, C), lambda i: (0, 0))
    return pl.pallas_call(
        edge_kernel,
        grid=(2,),
        out_shape=far((ROWS, C), BF),
        in_specs=[SM, block, whole, whole, whole, whole],
        out_specs=block,
        input_output_aliases={1: 0},
        name="add_edges",
        compiler_params=params(8),
        cost_estimate=cost(30000, 150000),
    )(par, hbm(rows), first, last, got1, got2)


def sum_kernel(parts, after, after2, out):
    step = pl.program_id(0)

    @pl.when(step < TAPS)
    def _():
        total = parts[0].astype(F32)
        for s in range(1, 32):
            total = total + parts[s].astype(F32)
        out[:, pl.ds(pl.multiple_of(step * HALF, HALF), HALF)] = total.astype(BF)

    @pl.when(step == TAPS)
    def _():
        for h in range(HEADS):
            total = parts[4 * h].astype(F32)
            for s in range(4 * h + 1, 4 * h + 4):
                total = total + parts[s].astype(F32)
            at = TAPS * HALF + h * QH
            out[:, at : at + QH] = total[:, 0:QH].astype(BF)


def sum_partials(parts, after, after2):
    return pl.pallas_call(
        sum_kernel,
        grid=(TAPS + 1,),
        out_shape=sds((24, WIDE), BF),
        in_specs=[pl.BlockSpec((32, 24, HALF), lambda t: (0, 0, t)), ANY, ANY],
        out_specs=pl.BlockSpec((24, WIDE), lambda t: (0, 0)),
        name="sum_partials",
        compiler_params=params(8),
        cost_estimate=cost(32 * 24 * 2304, 3700000),
    )(parts, hbm(after), hbm(after2))


def add_kernel(a, b, after, out):
    out[...] = (a[...].astype(F32) + b[...].astype(F32)) * (1.0 / LOSS_SCALE)


def add_pair(a, b, after):
    return pl.pallas_call(
        add_kernel,
        out_shape=sds((24, WIDE), F32),
        in_specs=[VM] * 2 + [ANY],
        out_specs=VM,
        name="add_pair",
        compiler_params=params(8),
        cost_estimate=cost(300000, 1500000),
    )(a, b, hbm(after))


def place_kernel(core, mine, other, conv, proj):
    def put(low, high):
        for t in range(TAPS):
            conv[t, :, 0:HALF] = low[:, t * HALF : (t + 1) * HALF]
            conv[t, :, HALF:] = high[:, t * HALF : (t + 1) * HALF]
        for h in range(HEADS):
            at = h * HD
            got = TAPS * HALF + h * QH
            proj[:, at : at + HD] = low[:, got : got + HD]
            proj[:, 1536 + at : 1536 + at + HD] = jnp.concatenate(
                [low[:, got + HD : got + QH], high[:, got : got + HD // 2]], axis=1
            )
            proj[:, 3072 + at : 3072 + at + HD] = high[:, got + HD // 2 : got + QH]

    @pl.when(core[0] == 0)
    def _():
        put(mine, other)

    @pl.when(core[0] != 0)
    def _():
        put(other, mine)


def place(core, mine, other):
    return pl.pallas_call(
        place_kernel,
        out_shape=(far((TAPS, 24, C), F32), far((24, 4608), F32)),
        in_specs=[SM, VM, VM],
        out_specs=(VM, VM),
        name="place",
        compiler_params=params(8),
        cost_estimate=cost(0, 2500000),
    )(core, mine, other)


NEAR = [(i, i ^ 1) for i in range(32)]
NEXT = [pair for i in range(1, 31, 2) for pair in ((i, i + 1), (i + 1, i))]


def local(conv_input, skip_grad, conv_weight, proj_weight, query, key, value, grad):
    core = lax.axis_index("core").astype(jnp.int32).reshape(1)
    head = lax.axis_index(HAX).astype(jnp.int32)
    pair, odd = (head // 2).reshape(1), (head % 2).reshape(1)
    x, skip = conv_input[0], skip_grad[0]

    packed = pack_heads(query[0], key[0], value[0], grad[0])
    own = lax.all_to_all(packed, HAX, 0, 0, tiled=True).reshape(BLK, 4 * HD)
    wh = head_weights(pair, odd, proj_weight, packed)
    qg_own, kv_own = split_own(own, wh)
    qg = lax.ppermute(qg_own, "z", A_PAIR)
    kv = lax.ppermute(kv_own, "z", B_PAIR)

    par = (lax.axis_index("z") % 2).astype(jnp.int32).reshape(1)
    head_rows, tail_rows = x[0:2], x[ROWS - 2 :]
    got1 = lax.ppermute(jnp.where(par[0] == 0, tail_rows, head_rows), SEQ, NEAR)
    got2 = lax.ppermute(jnp.where(par[0] == 0, head_rows, tail_rows), SEQ, NEXT)
    early, xp = conv_apply(par, x, got1, got2, conv_weight, qg_own)

    st = att_stats(own, qg, kv, early)
    st2 = lax.ppermute(st, "z", A_PAIR)
    dq_own, dq_send, dkv_own, dkv_send = att_grads(own, qg, kv, st, st2, wh)
    dq_in = lax.ppermute(dq_send, "z", A_PAIR)
    dkv_in = lax.ppermute(dkv_send, "z", B_PAIR)
    slope, pooled = gelu_pool(early, x, dq_send)
    pool_part, s0, s_send = att_join(core, dq_own, dkv_own, dq_in, dkv_in, wh, pooled)
    parts = lax.all_to_all(pool_part, HAX, 0, 0, tiled=True)
    parts, xp = lax.optimization_barrier((parts, xp))
    parts_sib = lax.ppermute(parts, "core", SWAP)
    xp_sib = lax.ppermute(xp, "core", SWAP)
    s1 = lax.ppermute(s_send, "core", SWAP)
    xt0, al0 = turn_input(xp)
    xt1, al1 = turn_input(xp_sib)

    pre, y_send, y0, pool = pre_grads(core, parts, skip, slope)
    y1 = lax.ppermute(y_send, "core", SWAP)
    terms = weight_grads(xt0, al0, xt1, al1, y0, y1, parts, parts_sib, s0, s1)
    got = lax.all_to_all(terms.reshape(32, 24, 2304), SEQ, 0, 0, tiled=True)

    rows, near, next_, first, last = conv_adjoint(par, pre, conv_weight, skip, pool)
    rim1 = lax.ppermute(near, SEQ, NEAR)
    rim2 = lax.ppermute(next_, SEQ, NEXT)

    total = sum_partials(got, rim1, rim2)
    total_far = lax.ppermute(total, "yh", SWAP)
    input_grad = add_edges(par, rows, first, last, rim1, rim2)
    mine = add_pair(total, total_far, input_grad)
    other = lax.ppermute(mine, "core", SWAP)
    conv_grad, proj_grad = place(core, mine, other)
    return input_grad[None], conv_grad, proj_grad


def solution(mesh):
    fine = Mesh(mesh.devices.reshape(2, 2, 2, 4, 4), ("yh", "core", "yl", "x", "z"))
    rows = P(DP, SEQ, None)
    return jax.shard_map(
        local,
        mesh=fine,
        in_specs=(rows, rows, P(), P(), rows, rows, rows, rows),
        out_specs=(rows, P(None, SEQ, None), P(SEQ, None)),
        check_vma=False,
    )
```

```python
import jax
import jax.numpy as jnp
from jax import lax
from jax.experimental import pallas as pl
from jax.experimental.pallas import tpu as pltpu
from jax.sharding import Mesh, PartitionSpec as P

HEADS = 8
TAPS = 5
LOSS_SCALE = 32
HD = 192
C = 768
ROWS = 768
ATT = 48
BLK = 384
FACTOR = 16
HALF = 384
QH = 288
WIDE = 5 * HALF + 8 * QH
SCALE = HD ** (-0.5)
SQRT_HALF = 0.7071067811865476
INV_ROOT_TWO_PI = 0.3989422804014327

BF = jnp.bfloat16
F32 = jnp.float32
DP = ("yh", "core")
SEQ = ("yl", "x", "z")
HAX = ("yl", "x")

NT = (((1,), (1,)), ((), ()))
TN = (((0,), (0,)), ((), ()))

A_PAIR = [(0, 1), (1, 0), (2, 3), (3, 2)]
B_PAIR = [(0, 3), (3, 0), (1, 2), (2, 1)]
SWAP = [(0, 1), (1, 0)]


def sds(shape, dtype):
    return jax.ShapeDtypeStruct(shape, dtype)


def far(shape, dtype):
    return pltpu.HBM(shape, dtype)


def hbm(x):
    return pltpu.with_memory_space_constraint(x, pltpu.HBM)


def params(mib):
    return pltpu.CompilerParams(vmem_limit_bytes=mib * 1024 * 1024)


def cost(flops, nbytes, trans=0):
    return pl.CostEstimate(flops=flops, bytes_accessed=nbytes, transcendentals=trans)


VM = pl.BlockSpec()
ANY = pl.BlockSpec(memory_space=pl.ANY)
SM = pl.BlockSpec(memory_space=pltpu.SMEM)


def nt(a, b):
    return lax.dot_general(a, b, NT, preferred_element_type=F32)


def tn(a, b):
    return lax.dot_general(a, b, TN, preferred_element_type=F32)


def mm(a, b):
    return jnp.dot(a, b, preferred_element_type=F32)


def pack_kernel(q, k, v, g, out, held, made, in_sems, out_sems):
    loads = [pltpu.make_async_copy(ref, held.at[i], in_sems.at[i]) for i, ref in enumerate((q, g, k, v))]
    for load in loads:
        load.start()
    stores = []
    for half in range(2):
        for i in (2 * half, 2 * half + 1):
            loads[i].wait()
            for h in range(HEADS):
                made[h, :, i * HD : (i + 1) * HD] = held[i, :, h * HD : (h + 1) * HD]
        cols = pl.ds(half * 2 * HD, 2 * HD)
        stores.append(pltpu.make_async_copy(made.at[:, :, cols], out.at[:, :, cols], out_sems.at[half]))
        stores[-1].start()
    for store in stores:
        store.wait()


def pack_heads(q, k, v, g):
    near = pl.BlockSpec(memory_space=pltpu.HBM)
    return pl.pallas_call(
        pack_kernel,
        out_shape=far((HEADS, ATT, 4 * HD), BF),
        in_specs=[near] * 4,
        out_specs=near,
        scratch_shapes=[
            pltpu.VMEM((4, ATT, HEADS * HD), BF),
            pltpu.VMEM((HEADS, ATT, 4 * HD), BF),
            pltpu.SemaphoreType.DMA((4,)),
            pltpu.SemaphoreType.DMA((2,)),
        ],
        name="pack_heads",
        compiler_params=params(8),
        cost_estimate=cost(0, 1200000),
    )(hbm(q), hbm(k), hbm(v), hbm(g))


def att_parts(own, qg, kv):
    query = jnp.concatenate([own[:, 0:HD], qg[:, 0:HD]], axis=0)
    grads = jnp.concatenate([own[:, HD : 2 * HD], qg[:, HD : 2 * HD]], axis=0)
    keys = jnp.concatenate([own[:, 2 * HD : 3 * HD], kv[:, 0:HD]], axis=0)
    values = jnp.concatenate([own[:, 3 * HD : 4 * HD], kv[:, HD : 2 * HD]], axis=0)
    return query, grads, keys, values


def stats_kernel(own, qg, kv, after, out):
    query, grads, keys, values = att_parts(own, qg, kv)
    out[...] = jnp.zeros_like(out)
    for i in range(2):
        rows = slice(i * BLK, (i + 1) * BLK)
        scores = nt(keys, query[rows]) * SCALE
        top = jnp.max(scores, axis=0, keepdims=True)
        powers = jnp.exp(scores - top)
        pgrad = nt(values, grads[rows])
        out[0:1, rows] = top
        out[1:2, rows] = jnp.sum(powers, axis=0, keepdims=True)
        out[2:3, rows] = jnp.sum(powers * pgrad, axis=0, keepdims=True)


def att_stats(own, qg, kv, after):
    return pl.pallas_call(
        stats_kernel,
        out_shape=sds((8, 2 * BLK), F32),
        in_specs=[VM] * 3 + [ANY],
        out_specs=VM,
        name="att_stats",
        compiler_params=params(16),
        cost_estimate=cost(8000000000, 1200000, 768 * 768),
    )(own, qg, kv, hbm(after))


def grads_kernel(own, qg, kv, st, st2, after, dq_own, dq_send, dkv_own, dkv_send):
    query, grads, keys, values = att_parts(own, qg, kv)
    dk = jnp.zeros((2 * BLK, HD), F32)
    dv = jnp.zeros((2 * BLK, HD), F32)
    for i in range(2):
        rows = slice(i * BLK, (i + 1) * BLK)
        other = slice((1 - i) * BLK, (2 - i) * BLK)
        m0, m1 = st[0:1, rows], st2[0:1, other]
        top = jnp.maximum(m0, m1)
        e0, e1 = jnp.exp(m0 - top), jnp.exp(m1 - top)
        inv = 1.0 / (st[1:2, rows] * e0 + st2[1:2, other] * e1)
        delta = (st[2:3, rows] * e0 + st2[2:3, other] * e1) * inv
        scores = nt(keys, query[rows]) * SCALE
        probs = jnp.exp(scores - top) * inv
        pgrad = nt(values, grads[rows])
        sgrad = (probs * (pgrad - delta)).astype(BF)
        dq = tn(sgrad, keys) * SCALE
        dk = dk + mm(sgrad, query[rows])
        dv = dv + mm(probs.astype(BF), grads[rows])
        if i == 0:
            dq_own[...] = dq
        else:
            dq_send[:, 0:HD] = dq[0 : BLK // 2].astype(BF)
            dq_send[:, HD : 2 * HD] = dq[BLK // 2 : BLK].astype(BF)
    dk = dk * SCALE
    dkv_own[:, 0:HD] = dk[0:BLK]
    dkv_own[:, HD : 2 * HD] = dv[0:BLK]
    dkv_send[:, 0:HD] = dk[BLK:].astype(BF)
    dkv_send[:, HD : 2 * HD] = dv[BLK:].astype(BF)


def att_grads(own, qg, kv, st, st2, after):
    return pl.pallas_call(
        grads_kernel,
        out_shape=(
            far((BLK, HD), F32),
            sds((BLK // 2, 2 * HD), BF),
            far((BLK, 2 * HD), F32),
            sds((BLK, 2 * HD), BF),
        ),
        in_specs=[VM] * 5 + [ANY],
        out_specs=(VM,) * 4,
        name="att_grads",
        compiler_params=params(20),
        cost_estimate=cost(20000000000, 3000000, 768 * 768),
    )(own, qg, kv, st, st2, hbm(after))


def split_kernel(own, after, qg, kv):
    qg[...] = own[:, 0 : 2 * HD]
    kv[...] = own[:, 2 * HD : 4 * HD]


def split_own(own, after):
    return pl.pallas_call(
        split_kernel,
        out_shape=(sds((BLK, 2 * HD), BF), sds((BLK, 2 * HD), BF)),
        in_specs=[VM, ANY],
        out_specs=(VM, VM),
        name="split_own",
        compiler_params=params(8),
        cost_estimate=cost(0, 1200000),
    )(own, hbm(after))


def head_kernel(pair, odd, wq, wk, wv, after, out):
    @pl.when(odd[0] == 0)
    def _():
        for p, ref in enumerate((wq, wk, wv)):
            out[p * HD : (p + 1) * HD, :] = ref[:, 0:HD].T

    @pl.when(odd[0] != 0)
    def _():
        for p, ref in enumerate((wq, wk, wv)):
            out[p * HD : (p + 1) * HD, :] = ref[:, HD : 2 * HD].T


def head_weights(pair, odd, weight, after):
    part = lambda p: pl.BlockSpec((C, 2 * HD), lambda i, pair, odd, p=p: (0, 4 * p + pair[0]))
    return pl.pallas_call(
        head_kernel,
        out_shape=far((3 * HD, C), BF),
        grid_spec=pltpu.PrefetchScalarGridSpec(
            num_scalar_prefetch=2,
            grid=(1,),
            in_specs=[part(0), part(1), part(2), ANY],
            out_specs=pl.BlockSpec((3 * HD, C), lambda i, pair, odd: (0, 0)),
        ),
        name="head_weights",
        compiler_params=params(12),
        cost_estimate=cost(0, 3000000),
    )(pair, odd, hbm(weight), hbm(weight), hbm(weight), after)


def join_kernel(core, dq_own, dkv_own, dq_in, dkv_in, wh, pooled, pool, keep, send, made, sems, sem2):
    others = [
        pltpu.make_async_copy(pooled, pool.at[h, pl.ds(ATT, ATT)], sem2.at[h]) for h in range(HEADS)
    ]
    for other in others:
        other.start()
    dq_got = jnp.concatenate([dq_in[:, 0:HD], dq_in[:, HD : 2 * HD]], axis=0).astype(F32)
    dq = (dq_own[...] + dq_got).astype(BF)
    dkv = (dkv_own[...] + dkv_in[...].astype(F32)).astype(BF)
    qkv = jnp.concatenate([dq, dkv], axis=1)
    stores = []
    for r in range(0, BLK, 2 * ATT):
        made[r : r + 2 * ATT, :] = mm(qkv[r : r + 2 * ATT], wh[...]).astype(BF)
        for h in (r // ATT, r // ATT + 1):
            rows = pl.ds(h * ATT, ATT)
            stores.append(pltpu.make_async_copy(made.at[rows], pool.at[h, pl.ds(0, ATT)], sems.at[h]))
            stores[-1].start()

    @pl.when(core[0] == 0)
    def _():
        keep[...] = qkv[:, 0:QH]
        send[...] = qkv[:, QH : 2 * QH]

    @pl.when(core[0] != 0)
    def _():
        keep[...] = qkv[:, QH : 2 * QH]
        send[...] = qkv[:, 0:QH]

    for copy in others + stores:
        copy.wait()


def att_join(core, dq_own, dkv_own, dq_in, dkv_in, wh, pooled):
    return pl.pallas_call(
        join_kernel,
        out_shape=(far((HEADS, 2 * ATT, C), BF), sds((BLK, QH), BF), sds((BLK, QH), BF)),
        in_specs=[SM] + [VM] * 6,
        out_specs=(pl.BlockSpec(memory_space=pltpu.HBM), VM, VM),
        scratch_shapes=[
            pltpu.VMEM((BLK, C), BF),
            pltpu.SemaphoreType.DMA((HEADS,)),
            pltpu.SemaphoreType.DMA((HEADS,)),
        ],
        name="att_join",
        compiler_params=params(12),
        cost_estimate=cost(10000000000, 3500000),
    )(core, hbm(dq_own), hbm(dkv_own), dq_in, dkv_in, hbm(wh), hbm(pooled))


def conv_kernel(par, x, got1, got2, w, after, pre, xp, xb, xf, wv, pv, xsem, wsems, psems):
    chunks = range(0, ROWS, 256)
    load = pltpu.make_async_copy(x, xb, xsem)
    loads = [pltpu.make_async_copy(w.at[t], wv.at[t], wsems.at[t]) for t in range(TAPS)]
    stores = [
        pltpu.make_async_copy(pv.at[pl.ds(r, 256)], pre.at[pl.ds(r, 256)], psems.at[r // 256])
        for r in chunks
    ]
    load.start()
    loads[0].start()
    xf[0:8, :] = jnp.zeros((8, C), F32)
    xf[8 + ROWS :, :] = jnp.zeros((8, C), F32)
    even = par[0] == 0
    one, two = got1[...].astype(F32), got2[...].astype(F32)
    xf[6:8, :] = jnp.where(even, two, one)
    xf[8 + ROWS : 10 + ROWS, :] = jnp.where(even, one, two)
    load.wait()
    loads[1].start()
    xf[8 : 8 + ROWS, :] = xb[...].astype(F32)
    for t in range(TAPS):
        loads[t].wait()
        if t + 2 < TAPS:
            loads[t + 2].start()
        for r in chunks:
            got = mm(xf[6 + t + r : 6 + t + r + 256, :].astype(BF), wv[t])
            if t == 0:
                pv[r : r + 256, :] = got
            else:
                pv[r : r + 256, :] += got
            if t == TAPS - 1:
                stores[r // 256].start()
    xp[...] = xf[...].astype(BF)
    for store in stores:
        store.wait()


def conv_apply(par, x, got1, got2, w, after):
    near = pl.BlockSpec(memory_space=pltpu.HBM)
    return pl.pallas_call(
        conv_kernel,
        out_shape=(far((ROWS, C), F32), sds((ROWS + 16, C), BF)),
        in_specs=[SM, near, VM, VM, near, ANY],
        out_specs=(near, VM),
        scratch_shapes=[
            pltpu.VMEM((ROWS, C), BF),
            pltpu.VMEM((ROWS + 16, C), F32),
            pltpu.VMEM((TAPS, C, C), BF),
            pltpu.VMEM((ROWS, C), F32),
            pltpu.SemaphoreType.DMA,
            pltpu.SemaphoreType.DMA((TAPS,)),
            pltpu.SemaphoreType.DMA((3,)),
        ],
        name="conv_apply",
        compiler_params=params(24),
        cost_estimate=cost(2 * 5 * 768**3, 9500000),
    )(par, hbm(x), got1, got2, hbm(w), after)


def gelu_kernel(pre, x, after, slope, pooled, means):
    for p in range(0, ROWS, 64):
        value = pre[p : p + 64, :]
        cumul = 0.5 * (1.0 + lax.erf(value * SQRT_HALF))
        bell = value * INV_ROOT_TWO_PI * jnp.exp(-0.5 * value * value)
        slope[p : p + 64, :] = (cumul + bell).astype(BF)
        block = (x[p : p + 64, :].astype(F32) + value * cumul).astype(BF).astype(F32)
        means[p // FACTOR : p // FACTOR + 4, :] = jnp.mean(block.reshape(4, FACTOR, C), axis=1)
    pooled[...] = means[...].astype(BF)


def gelu_pool(pre, x, after):
    return pl.pallas_call(
        gelu_kernel,
        out_shape=(far((ROWS, C), BF), far((ATT, C), BF)),
        in_specs=[VM, VM, ANY],
        out_specs=(VM, VM),
        scratch_shapes=[pltpu.VMEM((ATT, C), F32)],
        name="gelu_pool",
        compiler_params=params(16),
        cost_estimate=cost(3000000000, 5000000, 2 * 768 * 768),
    )(hbm(pre), hbm(x), after)


def turn_kernel(xp, xt, alts, edge):
    for r in range(0, ROWS, 128):
        xt[:, r : r + 128] = xp[8 + r : 8 + r + 128, :].T
    last = xp[8 + ROWS - 128 : 8 + ROWS, :].astype(F32)
    first = xp[8 : 8 + 128, :].astype(F32)
    top = xp[0:16, :].astype(F32)[0:8]
    bottom = xp[ROWS : ROWS + 16, :].astype(F32)[8:16]
    edge[...] = last
    edge[126:128, :] = top[6:8]
    alts[:, 0:128] = edge[...].astype(BF).T
    edge[126:127, :] = last[126:127]
    alts[:, 128:256] = edge[...].astype(BF).T
    edge[...] = first
    edge[0:1, :] = bottom[0:1]
    alts[:, 256:384] = edge[...].astype(BF).T
    edge[1:2, :] = bottom[1:2]
    alts[:, 384:512] = edge[...].astype(BF).T


def turn_input(xp):
    return pl.pallas_call(
        turn_kernel,
        out_shape=(sds((C, ROWS), BF), sds((C, 512), BF)),
        in_specs=[VM],
        out_specs=(VM, VM),
        scratch_shapes=[pltpu.VMEM((128, C), F32)],
        name="turn_input",
        compiler_params=params(12),
        cost_estimate=cost(10 * 768 * 768, 3200000),
    )(xp)


def slope_kernel(
    core, parts, skip, slope, pre, send, keep, pool, skip_v, slope_v, pre_v, pool_v, in_sems, out_sems, pool_sem
):
    chunks = range(0, ROWS, 256)
    loads = []
    for r in chunks:
        rows = pl.ds(r, 256)
        loads.append(pltpu.make_async_copy(skip.at[rows], skip_v.at[rows], in_sems.at[0, r // 256]))
        loads.append(pltpu.make_async_copy(slope.at[rows], slope_v.at[rows], in_sems.at[1, r // 256]))
    for load in loads:
        load.start()
    total = jnp.sum(parts[:, 0:ATT, :].astype(F32), axis=0) * (1.0 / FACTOR)
    pool_v[...] = total
    stores = [pltpu.make_async_copy(pool_v, pool, pool_sem)]
    stores[0].start()
    for r in chunks:
        loads[r // 128].wait()
        loads[r // 128 + 1].wait()
        for p in range(r, r + 256, 128):
            j = p // FACTOR
            piece = jnp.broadcast_to(total[j : j + 8, None, :], (8, FACTOR, C)).reshape(128, C)
            rows = slice(p, p + 128)
            grad = (skip_v[rows, :].astype(F32) + piece) * slope_v[rows, :].astype(F32)
            pre_v[rows, :] = grad.astype(BF)
        rows = pl.ds(r, 256)
        stores.append(pltpu.make_async_copy(pre_v.at[rows], pre.at[rows], out_sems.at[r // 256]))
        stores[-1].start()

    @pl.when(core[0] == 0)
    def _():
        keep[...] = pre_v[:, 0:HALF]
        send[...] = pre_v[:, HALF:]

    @pl.when(core[0] != 0)
    def _():
        keep[...] = pre_v[:, HALF:]
        send[...] = pre_v[:, 0:HALF]

    for store in stores:
        store.wait()


def pre_grads(core, parts, skip, slope):
    near = pl.BlockSpec(memory_space=pltpu.HBM)
    return pl.pallas_call(
        slope_kernel,
        out_shape=(
            far((ROWS, C), BF),
            sds((ROWS, HALF), BF),
            sds((ROWS, HALF), BF),
            far((ATT, C), F32),
        ),
        in_specs=[SM, VM, near, near],
        out_specs=(near, VM, VM, near),
        scratch_shapes=[
            pltpu.VMEM((ROWS, C), BF),
            pltpu.VMEM((ROWS, C), BF),
            pltpu.VMEM((ROWS, C), BF),
            pltpu.VMEM((ATT, C), F32),
            pltpu.SemaphoreType.DMA((2, 3)),
            pltpu.SemaphoreType.DMA((3,)),
            pltpu.SemaphoreType.DMA,
        ],
        name="pre_grads",
        compiler_params=params(12),
        cost_estimate=cost(5 * 768 * 768, 6000000),
    )(core, parts, hbm(skip), hbm(slope))


def weights_kernel(xt0, al0, xt1, al1, y0, y1, p0, p1, s0, s1, out, yf, wide, rest, made, sems):
    def copy(t):
        cols = pl.ds(t * HALF, HALF)
        return pltpu.make_async_copy(made.at[t], out.at[:, cols], sems.at[t])

    def pooled(ref):
        return jnp.concatenate([ref[h, ATT : 2 * ATT, :] for h in range(HEADS)], axis=0)

    part = jnp.concatenate([pooled(p0), pooled(p1)], axis=0)
    made[TAPS, :, 0:QH] = tn(part, jnp.concatenate([s0[...], s1[...]], axis=0)).astype(BF)
    made[TAPS, :, QH:HALF] = jnp.zeros((C, HALF - QH), BF)
    copy(TAPS).start()
    for i, ref in enumerate((y0, y1)):
        got = ref[...].astype(F32)
        yf[i, 8 : 8 + ROWS, :] = got
        yf[i, 0:8, :] = got[ROWS - 8 :]
        yf[i, 8 + ROWS : 16 + ROWS, :] = got[0:8]
    chunks = range(0, C, 256)
    for r in chunks:
        rows = slice(r, r + 256)
        left = jnp.concatenate([xt0[rows, :], xt1[rows, :]], axis=1)
        made[2, rows, :] = mm(left, jnp.concatenate([y0[...], y1[...]], axis=0)).astype(BF)
    copy(2).start()
    for g, taps in enumerate(((0, 1), (3, 4))):
        base, spot = (0, 2 * 256) if g == 0 else (256, 0)
        for k, t in enumerate(taps):
            cols = slice(k * HALF, (k + 1) * HALF)
            for i in range(2):
                at = 10 - t + base
                wide[g, i * 512 : (i + 1) * 512, cols] = yf[i, at : at + 512, :].astype(BF)
                at = 10 - t + spot
                rest[2 * g + k, i * 256 : (i + 1) * 256, :] = yf[i, at : at + 256, :].astype(BF)
        for r in chunks:
            rows = slice(r, r + 256)
            left = jnp.concatenate([xt0[rows, base : base + 512], xt1[rows, base : base + 512]], axis=1)
            both = mm(left, wide[g])
            for k, t in enumerate(taps):
                tiles = []
                for xt, al in ((xt0, al0), (xt1, al1)):
                    if g == 0:
                        tiles += [xt[rows, 512:640], al[rows, t * 128 : t * 128 + 128]]
                    else:
                        tiles += [al[rows, (t - 1) * 128 : t * 128], xt[rows, 128:256]]
                edge = mm(jnp.concatenate(tiles, axis=1), rest[2 * g + k])
                made[t, rows, :] = (both[:, k * HALF : (k + 1) * HALF] + edge).astype(BF)
        for t in taps:
            copy(t).start()
    for t in range(TAPS + 1):
        copy(t).wait()


def weight_grads(xt0, al0, xt1, al1, y0, y1, p0, p1, s0, s1):
    return pl.pallas_call(
        weights_kernel,
        out_shape=far((C, 2304), BF),
        in_specs=[VM] * 10,
        out_specs=pl.BlockSpec(memory_space=pltpu.HBM),
        scratch_shapes=[
            pltpu.VMEM((2, ROWS + 16, HALF), F32),
            pltpu.VMEM((2, 1024, 2 * HALF), BF),
            pltpu.VMEM((4, 512, HALF), BF),
            pltpu.VMEM((TAPS + 1, C, HALF), BF),
            pltpu.SemaphoreType.DMA((TAPS + 1,)),
        ],
        name="weight_grads",
        compiler_params=params(32),
        cost_estimate=cost(2 * 5 * 768 * 1536 * 384, 10000000),
    )(xt0, al0, xt1, al1, y0, y1, p0, p1, s0, s1)


def adjoint_kernel(par, pre, w, skip, pool, out, near, far_, first, last, yf, acc):
    tap = pl.program_id(0)

    @pl.when(tap == 0)
    def _():
        yf[0:16, :] = jnp.zeros((16, C), F32)
        yf[16 : 16 + ROWS, :] = pre[...].astype(F32)
        yf[16 + ROWS :, :] = jnp.zeros((16, C), F32)
        acc[0:8, :] = jnp.zeros((8, C), F32)
        acc[8 + ROWS :, :] = jnp.zeros((8, C), F32)
        for r in range(0, ATT, 8):
            piece = jnp.broadcast_to(pool[r : r + 8, :][:, None, :], (8, FACTOR, C)).reshape(128, C)
            rows = slice(r * FACTOR, r * FACTOR + 128)
            acc[8 + r * FACTOR : 136 + r * FACTOR, :] = skip[rows, :].astype(F32) + piece

    for t in range(TAPS):

        @pl.when(tap == t)
        def _(t=t):
            for r, n in ((0, 256), (256, 256), (512, 272)):
                rows = yf[10 - t + r : 10 - t + r + n, :].astype(BF)
                acc[r : r + n, :] += nt(rows, w[0])

    @pl.when(tap == TAPS - 1)
    def _():
        out[...] = acc[8 : 8 + ROWS, :].astype(BF)
        first[...] = acc[8:16, :]
        last[...] = acc[ROWS : ROWS + 8, :]
        even = par[0] == 0
        before, after = acc[0:8, :], acc[ROWS + 8 :, :]
        near[...] = jnp.where(even, after, before)
        far_[...] = jnp.where(even, before, after)


def conv_adjoint(par, pre, w, skip, pool):
    whole = lambda a, b: pl.BlockSpec((a, b), lambda t: (0, 0))
    return pl.pallas_call(
        adjoint_kernel,
        grid=(TAPS,),
        out_shape=(far((ROWS, C), BF),) + (sds((8, C), F32),) * 4,
        in_specs=[
            SM,
            whole(ROWS, C),
            pl.BlockSpec((1, C, C), lambda t: (t, 0, 0)),
            whole(ROWS, C),
            whole(ATT, C),
        ],
        out_specs=(whole(ROWS, C),) + (whole(8, C),) * 4,
        scratch_shapes=[pltpu.VMEM((ROWS + 32, C), F32), pltpu.VMEM((ROWS + 16, C), F32)],
        name="conv_adjoint",
        compiler_params=params(24),
        cost_estimate=cost(2 * 5 * 768**3, 9500000),
    )(par, hbm(pre), hbm(w), hbm(skip), hbm(pool))


def edge_kernel(par, rows, first, last, got1, got2, out):
    step = pl.program_id(0)
    held = rows[...].astype(F32)
    even = par[0] == 0

    @pl.when(step == 0)
    def _():
        top = jnp.where(even, got2[...], got1[...])
        out[...] = jnp.concatenate([first[...] + top, held[8:16]], axis=0).astype(BF)

    @pl.when(step != 0)
    def _():
        bottom = jnp.where(even, got1[...], got2[...])
        out[...] = jnp.concatenate([held[0:8], last[...] + bottom], axis=0).astype(BF)


def add_edges(par, rows, first, last, got1, got2):
    block = pl.BlockSpec((16, C), lambda i: (i * (ROWS // 16 - 1), 0))
    whole = pl.BlockSpec((8, C), lambda i: (0, 0))
    return pl.pallas_call(
        edge_kernel,
        grid=(2,),
        out_shape=far((ROWS, C), BF),
        in_specs=[SM, block, whole, whole, whole, whole],
        out_specs=block,
        input_output_aliases={1: 0},
        name="add_edges",
        compiler_params=params(8),
        cost_estimate=cost(30000, 150000),
    )(par, hbm(rows), first, last, got1, got2)


def sum_kernel(parts, after, after2, out):
    step = pl.program_id(0)

    @pl.when(step < TAPS)
    def _():
        total = parts[0].astype(F32)
        for s in range(1, 32):
            total = total + parts[s].astype(F32)
        out[:, pl.ds(pl.multiple_of(step * HALF, HALF), HALF)] = total.astype(BF)

    @pl.when(step == TAPS)
    def _():
        for h in range(HEADS):
            total = parts[4 * h].astype(F32)
            for s in range(4 * h + 1, 4 * h + 4):
                total = total + parts[s].astype(F32)
            at = TAPS * HALF + h * QH
            out[:, at : at + QH] = total[:, 0:QH].astype(BF)


def sum_partials(parts, after, after2):
    return pl.pallas_call(
        sum_kernel,
        grid=(TAPS + 1,),
        out_shape=sds((24, WIDE), BF),
        in_specs=[pl.BlockSpec((32, 24, HALF), lambda t: (0, 0, t)), ANY, ANY],
        out_specs=pl.BlockSpec((24, WIDE), lambda t: (0, 0)),
        name="sum_partials",
        compiler_params=params(8),
        cost_estimate=cost(32 * 24 * 2304, 3700000),
    )(parts, hbm(after), hbm(after2))


def add_kernel(a, b, after, out):
    out[...] = (a[...].astype(F32) + b[...].astype(F32)) * (1.0 / LOSS_SCALE)


def add_pair(a, b, after):
    return pl.pallas_call(
        add_kernel,
        out_shape=sds((24, WIDE), F32),
        in_specs=[VM] * 2 + [ANY],
        out_specs=VM,
        name="add_pair",
        compiler_params=params(8),
        cost_estimate=cost(300000, 1500000),
    )(a, b, hbm(after))


def place_kernel(core, mine, other, conv, proj):
    def put(low, high):
        for t in range(TAPS):
            conv[t, :, 0:HALF] = low[:, t * HALF : (t + 1) * HALF]
            conv[t, :, HALF:] = high[:, t * HALF : (t + 1) * HALF]
        for h in range(HEADS):
            at = h * HD
            got = TAPS * HALF + h * QH
            proj[:, at : at + HD] = low[:, got : got + HD]
            proj[:, 1536 + at : 1536 + at + HD] = jnp.concatenate(
                [low[:, got + HD : got + QH], high[:, got : got + HD // 2]], axis=1
            )
            proj[:, 3072 + at : 3072 + at + HD] = high[:, got + HD // 2 : got + QH]

    @pl.when(core[0] == 0)
    def _():
        put(mine, other)

    @pl.when(core[0] != 0)
    def _():
        put(other, mine)


def place(core, mine, other):
    return pl.pallas_call(
        place_kernel,
        out_shape=(far((TAPS, 24, C), F32), far((24, 4608), F32)),
        in_specs=[SM, VM, VM],
        out_specs=(VM, VM),
        name="place",
        compiler_params=params(8),
        cost_estimate=cost(0, 2500000),
    )(core, mine, other)


NEAR = [(i, i ^ 1) for i in range(32)]
NEXT = [pair for i in range(1, 31, 2) for pair in ((i, i + 1), (i + 1, i))]


def local(conv_input, skip_grad, conv_weight, proj_weight, query, key, value, grad):
    core = lax.axis_index("core").astype(jnp.int32).reshape(1)
    head = lax.axis_index(HAX).astype(jnp.int32)
    pair, odd = (head // 2).reshape(1), (head % 2).reshape(1)
    x, skip = conv_input[0], skip_grad[0]

    packed = pack_heads(query[0], key[0], value[0], grad[0])
    own = lax.all_to_all(packed, HAX, 0, 0, tiled=True).reshape(BLK, 4 * HD)
    wh = head_weights(pair, odd, proj_weight, packed)
    qg_own, kv_own = split_own(own, wh)
    qg = lax.ppermute(qg_own, "z", A_PAIR)
    kv = lax.ppermute(kv_own, "z", B_PAIR)

    par = (lax.axis_index("z") % 2).astype(jnp.int32).reshape(1)
    head_rows, tail_rows = x[0:2], x[ROWS - 2 :]
    got1 = lax.ppermute(jnp.where(par[0] == 0, tail_rows, head_rows), SEQ, NEAR)
    got2 = lax.ppermute(jnp.where(par[0] == 0, head_rows, tail_rows), SEQ, NEXT)
    early, xp = conv_apply(par, x, got1, got2, conv_weight, qg_own)

    st = att_stats(own, qg, kv, early)
    st2 = lax.ppermute(st, "z", A_PAIR)
    dq_own, dq_send, dkv_own, dkv_send = att_grads(own, qg, kv, st, st2, wh)
    dq_in = lax.ppermute(dq_send, "z", A_PAIR)
    dkv_in = lax.ppermute(dkv_send, "z", B_PAIR)
    slope, pooled = gelu_pool(early, x, dq_send)
    pool_part, s0, s_send = att_join(core, dq_own, dkv_own, dq_in, dkv_in, wh, pooled)
    parts = lax.all_to_all(pool_part, HAX, 0, 0, tiled=True)
    parts, xp = lax.optimization_barrier((parts, xp))
    parts_sib = lax.ppermute(parts, "core", SWAP)
    xp_sib = lax.ppermute(xp, "core", SWAP)
    s1 = lax.ppermute(s_send, "core", SWAP)
    xt0, al0 = turn_input(xp)
    xt1, al1 = turn_input(xp_sib)

    pre, y_send, y0, pool = pre_grads(core, parts, skip, slope)
    y1 = lax.ppermute(y_send, "core", SWAP)
    terms = weight_grads(xt0, al0, xt1, al1, y0, y1, parts, parts_sib, s0, s1)
    got = lax.all_to_all(terms.reshape(32, 24, 2304), SEQ, 0, 0, tiled=True)

    rows, near, next_, first, last = conv_adjoint(par, pre, conv_weight, skip, pool)
    rim1 = lax.ppermute(near, SEQ, NEAR)
    rim2 = lax.ppermute(next_, SEQ, NEXT)

    total = sum_partials(got, rim1, rim2)
    total_far = lax.ppermute(total, "yh", SWAP)
    input_grad = add_edges(par, rows, first, last, rim1, rim2)
    mine = add_pair(total, total_far, input_grad)
    other = lax.ppermute(mine, "core", SWAP)
    conv_grad, proj_grad = place(core, mine, other)
    return input_grad[None], conv_grad, proj_grad


def solution(mesh):
    fine = Mesh(mesh.devices.reshape(2, 2, 2, 4, 4), ("yh", "core", "yl", "x", "z"))
    rows = P(DP, SEQ, None)
    return jax.shard_map(
        local,
        mesh=fine,
        in_specs=(rows, rows, P(), P(), rows, rows, rows, rows),
        out_specs=(rows, P(None, SEQ, None), P(SEQ, None)),
        check_vma=False,
    )
```

```python
import jax
import jax.numpy as jnp
from jax import lax
from jax.experimental import pallas as pl
from jax.experimental.pallas import tpu as pltpu
from jax.sharding import Mesh, PartitionSpec as P

HEADS = 8
TAPS = 5
LOSS_SCALE = 32
HD = 192
C = 768
ROWS = 768
ATT = 48
BLK = 384
FACTOR = 16
HALF = 384
QH = 288
WIDE = 5 * HALF + 8 * QH
SCALE = HD ** (-0.5)
SQRT_HALF = 0.7071067811865476
INV_ROOT_TWO_PI = 0.3989422804014327

BF = jnp.bfloat16
F32 = jnp.float32
DP = ("yh", "core")
SEQ = ("yl", "x", "z")
HAX = ("yl", "x")

NT = (((1,), (1,)), ((), ()))
TN = (((0,), (0,)), ((), ()))

A_PAIR = [(0, 1), (1, 0), (2, 3), (3, 2)]
B_PAIR = [(0, 3), (3, 0), (1, 2), (2, 1)]
SWAP = [(0, 1), (1, 0)]


def sds(shape, dtype):
    return jax.ShapeDtypeStruct(shape, dtype)


def far(shape, dtype):
    return pltpu.HBM(shape, dtype)


def hbm(x):
    return pltpu.with_memory_space_constraint(x, pltpu.HBM)


def params(mib):
    return pltpu.CompilerParams(vmem_limit_bytes=mib * 1024 * 1024)


def cost(flops, nbytes, trans=0):
    return pl.CostEstimate(flops=flops, bytes_accessed=nbytes, transcendentals=trans)


VM = pl.BlockSpec()
ANY = pl.BlockSpec(memory_space=pl.ANY)
SM = pl.BlockSpec(memory_space=pltpu.SMEM)


def nt(a, b):
    return lax.dot_general(a, b, NT, preferred_element_type=F32)


def tn(a, b):
    return lax.dot_general(a, b, TN, preferred_element_type=F32)


def mm(a, b):
    return jnp.dot(a, b, preferred_element_type=F32)


def pack_kernel(q, k, v, g, out, held, made, in_sems, out_sems):
    loads = [pltpu.make_async_copy(ref, held.at[i], in_sems.at[i]) for i, ref in enumerate((q, g, k, v))]
    for load in loads:
        load.start()
    stores = []
    for half in range(2):
        for i in (2 * half, 2 * half + 1):
            loads[i].wait()
            for h in range(HEADS):
                made[h, :, i * HD : (i + 1) * HD] = held[i, :, h * HD : (h + 1) * HD]
        cols = pl.ds(half * 2 * HD, 2 * HD)
        stores.append(pltpu.make_async_copy(made.at[:, :, cols], out.at[:, :, cols], out_sems.at[half]))
        stores[-1].start()
    for store in stores:
        store.wait()


def pack_heads(q, k, v, g):
    near = pl.BlockSpec(memory_space=pltpu.HBM)
    return pl.pallas_call(
        pack_kernel,
        out_shape=far((HEADS, ATT, 4 * HD), BF),
        in_specs=[near] * 4,
        out_specs=near,
        scratch_shapes=[
            pltpu.VMEM((4, ATT, HEADS * HD), BF),
            pltpu.VMEM((HEADS, ATT, 4 * HD), BF),
            pltpu.SemaphoreType.DMA((4,)),
            pltpu.SemaphoreType.DMA((2,)),
        ],
        name="pack_heads",
        compiler_params=params(8),
        cost_estimate=cost(0, 1200000),
    )(hbm(q), hbm(k), hbm(v), hbm(g))


def att_parts(own, qg, kv):
    query = jnp.concatenate([own[:, 0:HD], qg[:, 0:HD]], axis=0)
    grads = jnp.concatenate([own[:, HD : 2 * HD], qg[:, HD : 2 * HD]], axis=0)
    keys = jnp.concatenate([own[:, 2 * HD : 3 * HD], kv[:, 0:HD]], axis=0)
    values = jnp.concatenate([own[:, 3 * HD : 4 * HD], kv[:, HD : 2 * HD]], axis=0)
    return query, grads, keys, values


def stats_kernel(own, qg, kv, after, out):
    query, grads, keys, values = att_parts(own, qg, kv)
    out[...] = jnp.zeros_like(out)
    for i in range(2):
        rows = slice(i * BLK, (i + 1) * BLK)
        scores = nt(keys, query[rows]) * SCALE
        top = jnp.max(scores, axis=0, keepdims=True)
        powers = jnp.exp(scores - top)
        pgrad = nt(values, grads[rows])
        out[0:1, rows] = top
        out[1:2, rows] = jnp.sum(powers, axis=0, keepdims=True)
        out[2:3, rows] = jnp.sum(powers * pgrad, axis=0, keepdims=True)


def att_stats(own, qg, kv, after):
    return pl.pallas_call(
        stats_kernel,
        out_shape=sds((8, 2 * BLK), F32),
        in_specs=[VM] * 3 + [ANY],
        out_specs=VM,
        name="att_stats",
        compiler_params=params(16),
        cost_estimate=cost(8000000000, 1200000, 768 * 768),
    )(own, qg, kv, hbm(after))


def grads_kernel(own, qg, kv, st, st2, after, dq_own, dq_send, dkv_own, dkv_send):
    query, grads, keys, values = att_parts(own, qg, kv)
    dk = jnp.zeros((2 * BLK, HD), F32)
    dv = jnp.zeros((2 * BLK, HD), F32)
    for i in range(2):
        rows = slice(i * BLK, (i + 1) * BLK)
        other = slice((1 - i) * BLK, (2 - i) * BLK)
        m0, m1 = st[0:1, rows], st2[0:1, other]
        top = jnp.maximum(m0, m1)
        e0, e1 = jnp.exp(m0 - top), jnp.exp(m1 - top)
        inv = 1.0 / (st[1:2, rows] * e0 + st2[1:2, other] * e1)
        delta = (st[2:3, rows] * e0 + st2[2:3, other] * e1) * inv
        scores = nt(keys, query[rows]) * SCALE
        probs = jnp.exp(scores - top) * inv
        pgrad = nt(values, grads[rows])
        sgrad = (probs * (pgrad - delta)).astype(BF)
        dq = tn(sgrad, keys) * SCALE
        dk = dk + mm(sgrad, query[rows])
        dv = dv + mm(probs.astype(BF), grads[rows])
        if i == 0:
            dq_own[...] = dq
        else:
            dq_send[:, 0:HD] = dq[0 : BLK // 2].astype(BF)
            dq_send[:, HD : 2 * HD] = dq[BLK // 2 : BLK].astype(BF)
    dk = dk * SCALE
    dkv_own[:, 0:HD] = dk[0:BLK]
    dkv_own[:, HD : 2 * HD] = dv[0:BLK]
    dkv_send[:, 0:HD] = dk[BLK:].astype(BF)
    dkv_send[:, HD : 2 * HD] = dv[BLK:].astype(BF)


def att_grads(own, qg, kv, st, st2, after):
    return pl.pallas_call(
        grads_kernel,
        out_shape=(
            far((BLK, HD), F32),
            sds((BLK // 2, 2 * HD), BF),
            far((BLK, 2 * HD), F32),
            sds((BLK, 2 * HD), BF),
        ),
        in_specs=[VM] * 5 + [ANY],
        out_specs=(VM,) * 4,
        name="att_grads",
        compiler_params=params(20),
        cost_estimate=cost(20000000000, 3000000, 768 * 768),
    )(own, qg, kv, st, st2, hbm(after))


def split_kernel(own, after, qg, kv):
    qg[...] = own[:, 0 : 2 * HD]
    kv[...] = own[:, 2 * HD : 4 * HD]


def split_own(own, after):
    return pl.pallas_call(
        split_kernel,
        out_shape=(sds((BLK, 2 * HD), BF), sds((BLK, 2 * HD), BF)),
        in_specs=[VM, ANY],
        out_specs=(VM, VM),
        name="split_own",
        compiler_params=params(8),
        cost_estimate=cost(0, 1200000),
    )(own, hbm(after))


def head_kernel(pair, odd, wq, wk, wv, after, out):
    @pl.when(odd[0] == 0)
    def _():
        for p, ref in enumerate((wq, wk, wv)):
            out[p * HD : (p + 1) * HD, :] = ref[:, 0:HD].T

    @pl.when(odd[0] != 0)
    def _():
        for p, ref in enumerate((wq, wk, wv)):
            out[p * HD : (p + 1) * HD, :] = ref[:, HD : 2 * HD].T


def head_weights(pair, odd, weight, after):
    part = lambda p: pl.BlockSpec((C, 2 * HD), lambda i, pair, odd, p=p: (0, 4 * p + pair[0]))
    return pl.pallas_call(
        head_kernel,
        out_shape=far((3 * HD, C), BF),
        grid_spec=pltpu.PrefetchScalarGridSpec(
            num_scalar_prefetch=2,
            grid=(1,),
            in_specs=[part(0), part(1), part(2), ANY],
            out_specs=pl.BlockSpec((3 * HD, C), lambda i, pair, odd: (0, 0)),
        ),
        name="head_weights",
        compiler_params=params(12),
        cost_estimate=cost(0, 3000000),
    )(pair, odd, hbm(weight), hbm(weight), hbm(weight), after)


def join_kernel(core, dq_own, dkv_own, dq_in, dkv_in, wh, pooled, pool, keep, send, made, sems, sem2):
    others = [
        pltpu.make_async_copy(pooled, pool.at[h, pl.ds(ATT, ATT)], sem2.at[h]) for h in range(HEADS)
    ]
    for other in others:
        other.start()
    dq_got = jnp.concatenate([dq_in[:, 0:HD], dq_in[:, HD : 2 * HD]], axis=0).astype(F32)
    dq = (dq_own[...] + dq_got).astype(BF)
    dkv = (dkv_own[...] + dkv_in[...].astype(F32)).astype(BF)
    qkv = jnp.concatenate([dq, dkv], axis=1)
    stores = []
    for r in range(0, BLK, 2 * ATT):
        made[r : r + 2 * ATT, :] = mm(qkv[r : r + 2 * ATT], wh[...]).astype(BF)
        for h in (r // ATT, r // ATT + 1):
            rows = pl.ds(h * ATT, ATT)
            stores.append(pltpu.make_async_copy(made.at[rows], pool.at[h, pl.ds(0, ATT)], sems.at[h]))
            stores[-1].start()

    send[:, QH:] = jnp.zeros((BLK, HALF - QH), BF)

    @pl.when(core[0] == 0)
    def _():
        keep[...] = qkv[:, 0:QH]
        send[:, 0:QH] = qkv[:, QH : 2 * QH]

    @pl.when(core[0] != 0)
    def _():
        keep[...] = qkv[:, QH : 2 * QH]
        send[:, 0:QH] = qkv[:, 0:QH]

    for copy in others + stores:
        copy.wait()


def att_join(core, dq_own, dkv_own, dq_in, dkv_in, wh, pooled):
    return pl.pallas_call(
        join_kernel,
        out_shape=(far((HEADS, 2 * ATT, C), BF), sds((BLK, QH), BF), far((BLK, HALF), BF)),
        in_specs=[SM] + [VM] * 6,
        out_specs=(pl.BlockSpec(memory_space=pltpu.HBM), VM, VM),
        scratch_shapes=[
            pltpu.VMEM((BLK, C), BF),
            pltpu.SemaphoreType.DMA((HEADS,)),
            pltpu.SemaphoreType.DMA((HEADS,)),
        ],
        name="att_join",
        compiler_params=params(12),
        cost_estimate=cost(10000000000, 3500000),
    )(core, hbm(dq_own), hbm(dkv_own), dq_in, dkv_in, hbm(wh), hbm(pooled))


def conv_kernel(par, x, got1, got2, w, after, pre, xp, xb, xf, wv, pv, xsem, wsems, psems):
    chunks = range(0, ROWS, 256)
    load = pltpu.make_async_copy(x, xb, xsem)
    loads = [pltpu.make_async_copy(w.at[t], wv.at[t], wsems.at[t]) for t in range(TAPS)]
    stores = [
        pltpu.make_async_copy(pv.at[pl.ds(r, 256)], pre.at[pl.ds(r, 256)], psems.at[r // 256])
        for r in chunks
    ]
    load.start()
    loads[0].start()
    xf[0:8, :] = jnp.zeros((8, C), F32)
    xf[8 + ROWS :, :] = jnp.zeros((8, C), F32)
    even = par[0] == 0
    one, two = got1[...].astype(F32), got2[...].astype(F32)
    xf[6:8, :] = jnp.where(even, two, one)
    xf[8 + ROWS : 10 + ROWS, :] = jnp.where(even, one, two)
    load.wait()
    loads[1].start()
    xf[8 : 8 + ROWS, :] = xb[...].astype(F32)
    for t in range(TAPS):
        loads[t].wait()
        if t + 2 < TAPS:
            loads[t + 2].start()
        for r in chunks:
            got = mm(xf[6 + t + r : 6 + t + r + 256, :].astype(BF), wv[t])
            if t == 0:
                pv[r : r + 256, :] = got
            else:
                pv[r : r + 256, :] += got
            if t == TAPS - 1:
                stores[r // 256].start()
    xp[...] = xf[...].astype(BF)
    for store in stores:
        store.wait()


def conv_apply(par, x, got1, got2, w, after):
    near = pl.BlockSpec(memory_space=pltpu.HBM)
    return pl.pallas_call(
        conv_kernel,
        out_shape=(far((ROWS, C), F32), sds((ROWS + 16, C), BF)),
        in_specs=[SM, near, VM, VM, near, ANY],
        out_specs=(near, VM),
        scratch_shapes=[
            pltpu.VMEM((ROWS, C), BF),
            pltpu.VMEM((ROWS + 16, C), F32),
            pltpu.VMEM((TAPS, C, C), BF),
            pltpu.VMEM((ROWS, C), F32),
            pltpu.SemaphoreType.DMA,
            pltpu.SemaphoreType.DMA((TAPS,)),
            pltpu.SemaphoreType.DMA((3,)),
        ],
        name="conv_apply",
        compiler_params=params(24),
        cost_estimate=cost(2 * 5 * 768**3, 9500000),
    )(par, hbm(x), got1, got2, hbm(w), after)


def gelu_kernel(pre, x, after, slope, pooled, means):
    for p in range(0, ROWS, 64):
        value = pre[p : p + 64, :]
        cumul = 0.5 * (1.0 + lax.erf(value * SQRT_HALF))
        bell = value * INV_ROOT_TWO_PI * jnp.exp(-0.5 * value * value)
        slope[p : p + 64, :] = (cumul + bell).astype(BF)
        block = (x[p : p + 64, :].astype(F32) + value * cumul).astype(BF).astype(F32)
        means[p // FACTOR : p // FACTOR + 4, :] = jnp.mean(block.reshape(4, FACTOR, C), axis=1)
    pooled[...] = means[...].astype(BF)


def gelu_pool(pre, x, after):
    return pl.pallas_call(
        gelu_kernel,
        out_shape=(far((ROWS, C), BF), far((ATT, C), BF)),
        in_specs=[VM, VM, ANY],
        out_specs=(VM, VM),
        scratch_shapes=[pltpu.VMEM((ATT, C), F32)],
        name="gelu_pool",
        compiler_params=params(16),
        cost_estimate=cost(3000000000, 5000000, 2 * 768 * 768),
    )(hbm(pre), hbm(x), after)


def turn_kernel(xp, xt, alts, edge):
    for r in range(0, ROWS, 128):
        xt[:, r : r + 128] = xp[8 + r : 8 + r + 128, :].T
    last = xp[8 + ROWS - 128 : 8 + ROWS, :].astype(F32)
    first = xp[8 : 8 + 128, :].astype(F32)
    top = xp[0:16, :].astype(F32)[0:8]
    bottom = xp[ROWS : ROWS + 16, :].astype(F32)[8:16]
    edge[...] = last
    edge[126:128, :] = top[6:8]
    alts[:, 0:128] = edge[...].astype(BF).T
    edge[126:127, :] = last[126:127]
    alts[:, 128:256] = edge[...].astype(BF).T
    edge[...] = first
    edge[0:1, :] = bottom[0:1]
    alts[:, 256:384] = edge[...].astype(BF).T
    edge[1:2, :] = bottom[1:2]
    alts[:, 384:512] = edge[...].astype(BF).T


def turn_input(xp):
    return pl.pallas_call(
        turn_kernel,
        out_shape=(sds((C, ROWS), BF), sds((C, 512), BF)),
        in_specs=[VM],
        out_specs=(VM, VM),
        scratch_shapes=[pltpu.VMEM((128, C), F32)],
        name="turn_input",
        compiler_params=params(12),
        cost_estimate=cost(10 * 768 * 768, 3200000),
    )(xp)


def slope_kernel(
    core, parts, skip, slope, extra, pre, send, keep, pool, skip_v, slope_v, pre_v, pool_v, in_sems, out_sems, pool_sem, extra_sem
):
    chunks = range(0, ROWS, 256)
    loads = []
    for r in chunks:
        rows = pl.ds(r, 256)
        loads.append(pltpu.make_async_copy(skip.at[rows], skip_v.at[rows], in_sems.at[0, r // 256]))
        loads.append(pltpu.make_async_copy(slope.at[rows], slope_v.at[rows], in_sems.at[1, r // 256]))
    for load in loads:
        load.start()
    joined = pltpu.make_async_copy(extra, send.at[pl.ds(ROWS, BLK)], extra_sem)
    joined.start()
    total = jnp.sum(parts[:, 0:ATT, :].astype(F32), axis=0) * (1.0 / FACTOR)
    pool_v[...] = total
    stores = [pltpu.make_async_copy(pool_v, pool, pool_sem)]
    stores[0].start()
    for r in chunks:
        loads[r // 128].wait()
        loads[r // 128 + 1].wait()
        for p in range(r, r + 256, 128):
            j = p // FACTOR
            piece = jnp.broadcast_to(total[j : j + 8, None, :], (8, FACTOR, C)).reshape(128, C)
            rows = slice(p, p + 128)
            grad = (skip_v[rows, :].astype(F32) + piece) * slope_v[rows, :].astype(F32)
            pre_v[rows, :] = grad.astype(BF)
        rows = pl.ds(r, 256)
        stores.append(pltpu.make_async_copy(pre_v.at[rows], pre.at[rows], out_sems.at[r // 256]))
        stores[-1].start()

    @pl.when(core[0] == 0)
    def _():
        keep[...] = pre_v[:, 0:HALF]
        send[0:ROWS, :] = pre_v[:, HALF:]

    @pl.when(core[0] != 0)
    def _():
        keep[...] = pre_v[:, HALF:]
        send[0:ROWS, :] = pre_v[:, 0:HALF]

    joined.wait()
    for store in stores:
        store.wait()


def pre_grads(core, parts, skip, slope, extra):
    near = pl.BlockSpec(memory_space=pltpu.HBM)
    return pl.pallas_call(
        slope_kernel,
        out_shape=(
            far((ROWS, C), BF),
            sds((ROWS + BLK, HALF), BF),
            sds((ROWS, HALF), BF),
            far((ATT, C), F32),
        ),
        in_specs=[SM, VM, near, near, near],
        out_specs=(near, VM, VM, near),
        scratch_shapes=[
            pltpu.VMEM((ROWS, C), BF),
            pltpu.VMEM((ROWS, C), BF),
            pltpu.VMEM((ROWS, C), BF),
            pltpu.VMEM((ATT, C), F32),
            pltpu.SemaphoreType.DMA((2, 3)),
            pltpu.SemaphoreType.DMA((3,)),
            pltpu.SemaphoreType.DMA,
            pltpu.SemaphoreType.DMA,
        ],
        name="pre_grads",
        compiler_params=params(12),
        cost_estimate=cost(5 * 768 * 768, 6000000),
    )(core, parts, hbm(skip), hbm(slope), hbm(extra))


def weights_kernel(xt0, al0, xt1, al1, y0, y1, p0, p1, s0, out, yf, wide, rest, made, sems):
    def copy(t):
        cols = pl.ds(t * HALF, HALF)
        return pltpu.make_async_copy(made.at[t], out.at[:, cols], sems.at[t])

    def pooled(ref):
        return jnp.concatenate([ref[h, ATT : 2 * ATT, :] for h in range(HEADS)], axis=0)

    part = jnp.concatenate([pooled(p0), pooled(p1)], axis=0)
    made[TAPS, :, 0:QH] = tn(part, jnp.concatenate([s0[...], y1[ROWS:, 0:QH]], axis=0)).astype(BF)
    made[TAPS, :, QH:HALF] = jnp.zeros((C, HALF - QH), BF)
    copy(TAPS).start()
    for i, ref in enumerate((y0, y1)):
        got = ref[0:ROWS, :].astype(F32)
        yf[i, 8 : 8 + ROWS, :] = got
        yf[i, 0:8, :] = got[ROWS - 8 :]
        yf[i, 8 + ROWS : 16 + ROWS, :] = got[0:8]
    chunks = range(0, C, 256)
    for r in chunks:
        rows = slice(r, r + 256)
        left = jnp.concatenate([xt0[rows, :], xt1[rows, :]], axis=1)
        made[2, rows, :] = mm(left, jnp.concatenate([y0[...], y1[0:ROWS, :]], axis=0)).astype(BF)
    copy(2).start()
    for g, taps in enumerate(((0, 1), (3, 4))):
        base, spot = (0, 2 * 256) if g == 0 else (256, 0)
        for k, t in enumerate(taps):
            cols = slice(k * HALF, (k + 1) * HALF)
            for i in range(2):
                at = 10 - t + base
                wide[g, i * 512 : (i + 1) * 512, cols] = yf[i, at : at + 512, :].astype(BF)
                at = 10 - t + spot
                rest[2 * g + k, i * 256 : (i + 1) * 256, :] = yf[i, at : at + 256, :].astype(BF)
        for r in chunks:
            rows = slice(r, r + 256)
            left = jnp.concatenate([xt0[rows, base : base + 512], xt1[rows, base : base + 512]], axis=1)
            both = mm(left, wide[g])
            for k, t in enumerate(taps):
                tiles = []
                for xt, al in ((xt0, al0), (xt1, al1)):
                    if g == 0:
                        tiles += [xt[rows, 512:640], al[rows, t * 128 : t * 128 + 128]]
                    else:
                        tiles += [al[rows, (t - 1) * 128 : t * 128], xt[rows, 128:256]]
                edge = mm(jnp.concatenate(tiles, axis=1), rest[2 * g + k])
                made[t, rows, :] = (both[:, k * HALF : (k + 1) * HALF] + edge).astype(BF)
        for t in taps:
            copy(t).start()
    for t in range(TAPS + 1):
        copy(t).wait()


def weight_grads(xt0, al0, xt1, al1, y0, y1, p0, p1, s0):
    return pl.pallas_call(
        weights_kernel,
        out_shape=far((C, 2304), BF),
        in_specs=[VM] * 9,
        out_specs=pl.BlockSpec(memory_space=pltpu.HBM),
        scratch_shapes=[
            pltpu.VMEM((2, ROWS + 16, HALF), F32),
            pltpu.VMEM((2, 1024, 2 * HALF), BF),
            pltpu.VMEM((4, 512, HALF), BF),
            pltpu.VMEM((TAPS + 1, C, HALF), BF),
            pltpu.SemaphoreType.DMA((TAPS + 1,)),
        ],
        name="weight_grads",
        compiler_params=params(32),
        cost_estimate=cost(2 * 5 * 768 * 1536 * 384, 10000000),
    )(xt0, al0, xt1, al1, y0, y1, p0, p1, s0)


def adjoint_kernel(par, pre, w, skip, pool, out, near, far_, first, last, yf, acc):
    tap = pl.program_id(0)

    @pl.when(tap == 0)
    def _():
        yf[0:16, :] = jnp.zeros((16, C), F32)
        yf[16 : 16 + ROWS, :] = pre[...].astype(F32)
        yf[16 + ROWS :, :] = jnp.zeros((16, C), F32)
        acc[0:8, :] = jnp.zeros((8, C), F32)
        acc[8 + ROWS :, :] = jnp.zeros((8, C), F32)
        for r in range(0, ATT, 8):
            piece = jnp.broadcast_to(pool[r : r + 8, :][:, None, :], (8, FACTOR, C)).reshape(128, C)
            rows = slice(r * FACTOR, r * FACTOR + 128)
            acc[8 + r * FACTOR : 136 + r * FACTOR, :] = skip[rows, :].astype(F32) + piece

    for t in range(TAPS):

        @pl.when(tap == t)
        def _(t=t):
            for r, n in ((0, 256), (256, 256), (512, 272)):
                rows = yf[10 - t + r : 10 - t + r + n, :].astype(BF)
                acc[r : r + n, :] += nt(rows, w[0])

    @pl.when(tap == TAPS - 1)
    def _():
        out[...] = acc[8 : 8 + ROWS, :].astype(BF)
        first[...] = acc[8:16, :]
        last[...] = acc[ROWS : ROWS + 8, :]
        even = par[0] == 0
        before, after = acc[0:8, :], acc[ROWS + 8 :, :]
        near[...] = jnp.where(even, after, before)
        far_[...] = jnp.where(even, before, after)


def conv_adjoint(par, pre, w, skip, pool):
    whole = lambda a, b: pl.BlockSpec((a, b), lambda t: (0, 0))
    return pl.pallas_call(
        adjoint_kernel,
        grid=(TAPS,),
        out_shape=(far((ROWS, C), BF),) + (sds((8, C), F32),) * 4,
        in_specs=[
            SM,
            whole(ROWS, C),
            pl.BlockSpec((1, C, C), lambda t: (t, 0, 0)),
            whole(ROWS, C),
            whole(ATT, C),
        ],
        out_specs=(whole(ROWS, C),) + (whole(8, C),) * 4,
        scratch_shapes=[pltpu.VMEM((ROWS + 32, C), F32), pltpu.VMEM((ROWS + 16, C), F32)],
        name="conv_adjoint",
        compiler_params=params(24),
        cost_estimate=cost(2 * 5 * 768**3, 9500000),
    )(par, hbm(pre), hbm(w), hbm(skip), hbm(pool))


def edge_kernel(par, rows, first, last, got1, got2, out):
    step = pl.program_id(0)
    held = rows[...].astype(F32)
    even = par[0] == 0

    @pl.when(step == 0)
    def _():
        top = jnp.where(even, got2[...], got1[...])
        out[...] = jnp.concatenate([first[...] + top, held[8:16]], axis=0).astype(BF)

    @pl.when(step != 0)
    def _():
        bottom = jnp.where(even, got1[...], got2[...])
        out[...] = jnp.concatenate([held[0:8], last[...] + bottom], axis=0).astype(BF)


def add_edges(par, rows, first, last, got1, got2):
    block = pl.BlockSpec((16, C), lambda i: (i * (ROWS // 16 - 1), 0))
    whole = pl.BlockSpec((8, C), lambda i: (0, 0))
    return pl.pallas_call(
        edge_kernel,
        grid=(2,),
        out_shape=far((ROWS, C), BF),
        in_specs=[SM, block, whole, whole, whole, whole],
        out_specs=block,
        input_output_aliases={1: 0},
        name="add_edges",
        compiler_params=params(8),
        cost_estimate=cost(30000, 150000),
    )(par, hbm(rows), first, last, got1, got2)


def sum_kernel(parts, after, after2, out):
    step = pl.program_id(0)

    @pl.when(step < TAPS)
    def _():
        total = parts[0].astype(F32)
        for s in range(1, 32):
            total = total + parts[s].astype(F32)
        out[:, pl.ds(pl.multiple_of(step * HALF, HALF), HALF)] = total.astype(BF)

    @pl.when(step == TAPS)
    def _():
        for h in range(HEADS):
            total = parts[4 * h].astype(F32)
            for s in range(4 * h + 1, 4 * h + 4):
                total = total + parts[s].astype(F32)
            at = TAPS * HALF + h * QH
            out[:, at : at + QH] = total[:, 0:QH].astype(BF)


def sum_partials(parts, after, after2):
    return pl.pallas_call(
        sum_kernel,
        grid=(TAPS + 1,),
        out_shape=sds((24, WIDE), BF),
        in_specs=[pl.BlockSpec((32, 24, HALF), lambda t: (0, 0, t)), ANY, ANY],
        out_specs=pl.BlockSpec((24, WIDE), lambda t: (0, 0)),
        name="sum_partials",
        compiler_params=params(8),
        cost_estimate=cost(32 * 24 * 2304, 3700000),
    )(parts, hbm(after), hbm(after2))


def add_kernel(a, b, after, out):
    out[...] = (a[...].astype(F32) + b[...].astype(F32)) * (1.0 / LOSS_SCALE)


def add_pair(a, b, after):
    return pl.pallas_call(
        add_kernel,
        out_shape=sds((24, WIDE), F32),
        in_specs=[VM] * 2 + [ANY],
        out_specs=VM,
        name="add_pair",
        compiler_params=params(8),
        cost_estimate=cost(300000, 1500000),
    )(a, b, hbm(after))


def place_kernel(core, mine, other, conv, proj):
    def put(low, high):
        for t in range(TAPS):
            conv[t, :, 0:HALF] = low[:, t * HALF : (t + 1) * HALF]
            conv[t, :, HALF:] = high[:, t * HALF : (t + 1) * HALF]
        for h in range(HEADS):
            at = h * HD
            got = TAPS * HALF + h * QH
            proj[:, at : at + HD] = low[:, got : got + HD]
            proj[:, 1536 + at : 1536 + at + HD] = jnp.concatenate(
                [low[:, got + HD : got + QH], high[:, got : got + HD // 2]], axis=1
            )
            proj[:, 3072 + at : 3072 + at + HD] = high[:, got + HD // 2 : got + QH]

    @pl.when(core[0] == 0)
    def _():
        put(mine, other)

    @pl.when(core[0] != 0)
    def _():
        put(other, mine)


def place(core, mine, other):
    return pl.pallas_call(
        place_kernel,
        out_shape=(far((TAPS, 24, C), F32), far((24, 4608), F32)),
        in_specs=[SM, VM, VM],
        out_specs=(VM, VM),
        name="place",
        compiler_params=params(8),
        cost_estimate=cost(0, 2500000),
    )(core, mine, other)


NEAR = [(i, i ^ 1) for i in range(32)]
NEXT = [pair for i in range(1, 31, 2) for pair in ((i, i + 1), (i + 1, i))]


def local(conv_input, skip_grad, conv_weight, proj_weight, query, key, value, grad):
    core = lax.axis_index("core").astype(jnp.int32).reshape(1)
    head = lax.axis_index(HAX).astype(jnp.int32)
    pair, odd = (head // 2).reshape(1), (head % 2).reshape(1)
    x, skip = conv_input[0], skip_grad[0]

    packed = pack_heads(query[0], key[0], value[0], grad[0])
    own = lax.all_to_all(packed, HAX, 0, 0, tiled=True).reshape(BLK, 4 * HD)
    wh = head_weights(pair, odd, proj_weight, packed)
    qg_own, kv_own = split_own(own, wh)
    qg = lax.ppermute(qg_own, "z", A_PAIR)
    kv = lax.ppermute(kv_own, "z", B_PAIR)

    par = (lax.axis_index("z") % 2).astype(jnp.int32).reshape(1)
    head_rows, tail_rows = x[0:2], x[ROWS - 2 :]
    got1 = lax.ppermute(jnp.where(par[0] == 0, tail_rows, head_rows), SEQ, NEAR)
    got2 = lax.ppermute(jnp.where(par[0] == 0, head_rows, tail_rows), SEQ, NEXT)
    early, xp = conv_apply(par, x, got1, got2, conv_weight, qg_own)

    st = att_stats(own, qg, kv, early)
    st2 = lax.ppermute(st, "z", A_PAIR)
    dq_own, dq_send, dkv_own, dkv_send = att_grads(own, qg, kv, st, st2, wh)
    dq_in = lax.ppermute(dq_send, "z", A_PAIR)
    dkv_in = lax.ppermute(dkv_send, "z", B_PAIR)
    slope, pooled = gelu_pool(early, x, dq_send)
    pool_part, s0, s_send = att_join(core, dq_own, dkv_own, dq_in, dkv_in, wh, pooled)
    parts = lax.all_to_all(pool_part, HAX, 0, 0, tiled=True)
    parts, xp = lax.optimization_barrier((parts, xp))
    parts_sib = lax.ppermute(parts, "core", SWAP)
    xp_sib = lax.ppermute(xp, "core", SWAP)
    xt0, al0 = turn_input(xp)
    xt1, al1 = turn_input(xp_sib)

    pre, y_send, y0, pool = pre_grads(core, parts, skip, slope, s_send)
    y1 = lax.ppermute(y_send, "core", SWAP)
    terms = weight_grads(xt0, al0, xt1, al1, y0, y1, parts, parts_sib, s0)
    got = lax.all_to_all(terms.reshape(32, 24, 2304), SEQ, 0, 0, tiled=True)

    rows, near, next_, first, last = conv_adjoint(par, pre, conv_weight, skip, pool)
    rim1 = lax.ppermute(near, SEQ, NEAR)
    rim2 = lax.ppermute(next_, SEQ, NEXT)

    total = sum_partials(got, rim1, rim2)
    total_far = lax.ppermute(total, "yh", SWAP)
    input_grad = add_edges(par, rows, first, last, rim1, rim2)
    mine = add_pair(total, total_far, input_grad)
    other = lax.ppermute(mine, "core", SWAP)
    conv_grad, proj_grad = place(core, mine, other)
    return input_grad[None], conv_grad, proj_grad


def solution(mesh):
    fine = Mesh(mesh.devices.reshape(2, 2, 2, 4, 4), ("yh", "core", "yl", "x", "z"))
    rows = P(DP, SEQ, None)
    return jax.shard_map(
        local,
        mesh=fine,
        in_specs=(rows, rows, P(), P(), rows, rows, rows, rows),
        out_specs=(rows, P(None, SEQ, None), P(SEQ, None)),
        check_vma=False,
    )
```

```python
import jax
import jax.numpy as jnp
from jax import lax
from jax.experimental import pallas as pl
from jax.experimental.pallas import tpu as pltpu
from jax.sharding import Mesh, PartitionSpec as P

HEADS = 8
TAPS = 5
LOSS_SCALE = 32
HD = 192
C = 768
ROWS = 768
ATT = 48
BLK = 384
FACTOR = 16
HALF = 384
QH = 288
WIDE = 5 * HALF + 8 * QH
SCALE = HD ** (-0.5)
SQRT_HALF = 0.7071067811865476
INV_ROOT_TWO_PI = 0.3989422804014327

BF = jnp.bfloat16
F32 = jnp.float32
DP = ("yh", "core")
SEQ = ("yl", "x", "z")
HAX = ("yl", "x")

NT = (((1,), (1,)), ((), ()))
TN = (((0,), (0,)), ((), ()))

A_PAIR = [(0, 1), (1, 0), (2, 3), (3, 2)]
B_PAIR = [(0, 3), (3, 0), (1, 2), (2, 1)]
SWAP = [(0, 1), (1, 0)]


def sds(shape, dtype):
    return jax.ShapeDtypeStruct(shape, dtype)


def far(shape, dtype):
    return pltpu.HBM(shape, dtype)


def hbm(x):
    return pltpu.with_memory_space_constraint(x, pltpu.HBM)


def params(mib):
    return pltpu.CompilerParams(vmem_limit_bytes=mib * 1024 * 1024)


def cost(flops, nbytes, trans=0):
    return pl.CostEstimate(flops=flops, bytes_accessed=nbytes, transcendentals=trans)


VM = pl.BlockSpec()
ANY = pl.BlockSpec(memory_space=pl.ANY)
SM = pl.BlockSpec(memory_space=pltpu.SMEM)


def nt(a, b):
    return lax.dot_general(a, b, NT, preferred_element_type=F32)


def tn(a, b):
    return lax.dot_general(a, b, TN, preferred_element_type=F32)


def mm(a, b):
    return jnp.dot(a, b, preferred_element_type=F32)


def pack_kernel(q, k, v, g, out, held, made, in_sems, out_sems):
    loads = [pltpu.make_async_copy(ref, held.at[i], in_sems.at[i]) for i, ref in enumerate((q, g, k, v))]
    for load in loads:
        load.start()
    stores = []
    for half in range(2):
        for i in (2 * half, 2 * half + 1):
            loads[i].wait()
            for h in range(HEADS):
                made[h, :, i * HD : (i + 1) * HD] = held[i, :, h * HD : (h + 1) * HD]
        cols = pl.ds(half * 2 * HD, 2 * HD)
        stores.append(pltpu.make_async_copy(made.at[:, :, cols], out.at[:, :, cols], out_sems.at[half]))
        stores[-1].start()
    for store in stores:
        store.wait()


def pack_heads(q, k, v, g):
    near = pl.BlockSpec(memory_space=pltpu.HBM)
    return pl.pallas_call(
        pack_kernel,
        out_shape=far((HEADS, ATT, 4 * HD), BF),
        in_specs=[near] * 4,
        out_specs=near,
        scratch_shapes=[
            pltpu.VMEM((4, ATT, HEADS * HD), BF),
            pltpu.VMEM((HEADS, ATT, 4 * HD), BF),
            pltpu.SemaphoreType.DMA((4,)),
            pltpu.SemaphoreType.DMA((2,)),
        ],
        name="pack_heads",
        compiler_params=params(8),
        cost_estimate=cost(0, 1200000),
    )(hbm(q), hbm(k), hbm(v), hbm(g))


def att_parts(own, qg, kv):
    query = jnp.concatenate([own[:, 0:HD], qg[:, 0:HD]], axis=0)
    grads = jnp.concatenate([own[:, HD : 2 * HD], qg[:, HD : 2 * HD]], axis=0)
    keys = jnp.concatenate([own[:, 2 * HD : 3 * HD], kv[:, 0:HD]], axis=0)
    values = jnp.concatenate([own[:, 3 * HD : 4 * HD], kv[:, HD : 2 * HD]], axis=0)
    return query, grads, keys, values


def stats_kernel(own, qg, kv, after, out):
    query, grads, keys, values = att_parts(own, qg, kv)
    out[...] = jnp.zeros_like(out)
    for i in range(2):
        rows = slice(i * BLK, (i + 1) * BLK)
        scores = nt(keys, query[rows]) * SCALE
        top = jnp.max(scores, axis=0, keepdims=True)
        powers = jnp.exp(scores - top)
        pgrad = nt(values, grads[rows])
        out[0:1, rows] = top
        out[1:2, rows] = jnp.sum(powers, axis=0, keepdims=True)
        out[2:3, rows] = jnp.sum(powers * pgrad, axis=0, keepdims=True)


def att_stats(own, qg, kv, after):
    return pl.pallas_call(
        stats_kernel,
        out_shape=sds((8, 2 * BLK), F32),
        in_specs=[VM] * 3 + [ANY],
        out_specs=VM,
        name="att_stats",
        compiler_params=params(16),
        cost_estimate=cost(8000000000, 1200000, 768 * 768),
    )(own, qg, kv, hbm(after))


def grads_kernel(own, qg, kv, st, st2, after, dq_own, dq_send, dkv_own, dkv_send):
    query, grads, keys, values = att_parts(own, qg, kv)
    dk = jnp.zeros((2 * BLK, HD), F32)
    dv = jnp.zeros((2 * BLK, HD), F32)
    for i in range(2):
        rows = slice(i * BLK, (i + 1) * BLK)
        other = slice((1 - i) * BLK, (2 - i) * BLK)
        m0, m1 = st[0:1, rows], st2[0:1, other]
        top = jnp.maximum(m0, m1)
        e0, e1 = jnp.exp(m0 - top), jnp.exp(m1 - top)
        inv = 1.0 / (st[1:2, rows] * e0 + st2[1:2, other] * e1)
        delta = (st[2:3, rows] * e0 + st2[2:3, other] * e1) * inv
        scores = nt(keys, query[rows]) * SCALE
        probs = jnp.exp(scores - top) * inv
        pgrad = nt(values, grads[rows])
        sgrad = (probs * (pgrad - delta)).astype(BF)
        dq = tn(sgrad, keys) * SCALE
        dk = dk + mm(sgrad, query[rows])
        dv = dv + mm(probs.astype(BF), grads[rows])
        if i == 0:
            dq_own[...] = dq.astype(BF)
        else:
            dq_send[:, 0:HD] = dq[0 : BLK // 2].astype(BF)
            dq_send[:, HD : 2 * HD] = dq[BLK // 2 : BLK].astype(BF)
    dk = dk * SCALE
    dkv_own[:, 0:HD] = dk[0:BLK].astype(BF)
    dkv_own[:, HD : 2 * HD] = dv[0:BLK].astype(BF)
    dkv_send[:, 0:HD] = dk[BLK:].astype(BF)
    dkv_send[:, HD : 2 * HD] = dv[BLK:].astype(BF)


def att_grads(own, qg, kv, st, st2, after):
    return pl.pallas_call(
        grads_kernel,
        out_shape=(
            far((BLK, HD), BF),
            sds((BLK // 2, 2 * HD), BF),
            far((BLK, 2 * HD), BF),
            sds((BLK, 2 * HD), BF),
        ),
        in_specs=[VM] * 5 + [ANY],
        out_specs=(VM,) * 4,
        name="att_grads",
        compiler_params=params(20),
        cost_estimate=cost(20000000000, 3000000, 768 * 768),
    )(own, qg, kv, st, st2, hbm(after))


def split_kernel(own, after, qg, kv):
    qg[...] = own[:, 0 : 2 * HD]
    kv[...] = own[:, 2 * HD : 4 * HD]


def split_own(own, after):
    return pl.pallas_call(
        split_kernel,
        out_shape=(sds((BLK, 2 * HD), BF), sds((BLK, 2 * HD), BF)),
        in_specs=[VM, ANY],
        out_specs=(VM, VM),
        name="split_own",
        compiler_params=params(8),
        cost_estimate=cost(0, 1200000),
    )(own, hbm(after))


def head_kernel(pair, odd, wq, wk, wv, after, out):
    @pl.when(odd[0] == 0)
    def _():
        for p, ref in enumerate((wq, wk, wv)):
            out[p * HD : (p + 1) * HD, :] = ref[:, 0:HD].T

    @pl.when(odd[0] != 0)
    def _():
        for p, ref in enumerate((wq, wk, wv)):
            out[p * HD : (p + 1) * HD, :] = ref[:, HD : 2 * HD].T


def head_weights(pair, odd, weight, after):
    part = lambda p: pl.BlockSpec((C, 2 * HD), lambda i, pair, odd, p=p: (0, 4 * p + pair[0]))
    return pl.pallas_call(
        head_kernel,
        out_shape=far((3 * HD, C), BF),
        grid_spec=pltpu.PrefetchScalarGridSpec(
            num_scalar_prefetch=2,
            grid=(1,),
            in_specs=[part(0), part(1), part(2), ANY],
            out_specs=pl.BlockSpec((3 * HD, C), lambda i, pair, odd: (0, 0)),
        ),
        name="head_weights",
        compiler_params=params(12),
        cost_estimate=cost(0, 3000000),
    )(pair, odd, hbm(weight), hbm(weight), hbm(weight), after)


def join_kernel(core, dq_own, dkv_own, dq_in, dkv_in, wh, pooled, pool, keep, send, made, sems, sem2):
    others = [
        pltpu.make_async_copy(pooled, pool.at[h, pl.ds(ATT, ATT)], sem2.at[h]) for h in range(HEADS)
    ]
    for other in others:
        other.start()
    dq_got = jnp.concatenate([dq_in[:, 0:HD], dq_in[:, HD : 2 * HD]], axis=0).astype(F32)
    dq = (dq_own[...].astype(F32) + dq_got).astype(BF)
    dkv = (dkv_own[...].astype(F32) + dkv_in[...].astype(F32)).astype(BF)
    qkv = jnp.concatenate([dq, dkv], axis=1)
    stores = []
    for r in range(0, BLK, 2 * ATT):
        made[r : r + 2 * ATT, :] = mm(qkv[r : r + 2 * ATT], wh[...]).astype(BF)
        for h in (r // ATT, r // ATT + 1):
            rows = pl.ds(h * ATT, ATT)
            stores.append(pltpu.make_async_copy(made.at[rows], pool.at[h, pl.ds(0, ATT)], sems.at[h]))
            stores[-1].start()

    @pl.when(core[0] == 0)
    def _():
        keep[...] = qkv[:, 0:QH]
        send[...] = qkv[:, QH : 2 * QH]

    @pl.when(core[0] != 0)
    def _():
        keep[...] = qkv[:, QH : 2 * QH]
        send[...] = qkv[:, 0:QH]

    for copy in others + stores:
        copy.wait()


def att_join(core, dq_own, dkv_own, dq_in, dkv_in, wh, pooled):
    return pl.pallas_call(
        join_kernel,
        out_shape=(far((HEADS, 2 * ATT, C), BF), sds((BLK, QH), BF), sds((BLK, QH), BF)),
        in_specs=[SM] + [VM] * 6,
        out_specs=(pl.BlockSpec(memory_space=pltpu.HBM), VM, VM),
        scratch_shapes=[
            pltpu.VMEM((BLK, C), BF),
            pltpu.SemaphoreType.DMA((HEADS,)),
            pltpu.SemaphoreType.DMA((HEADS,)),
        ],
        name="att_join",
        compiler_params=params(12),
        cost_estimate=cost(10000000000, 3500000),
    )(core, hbm(dq_own), hbm(dkv_own), dq_in, dkv_in, hbm(wh), hbm(pooled))


def conv_kernel(par, x, got1, got2, w, after, pre, xp, xb, xf, wv, pv, xsem, wsems, psems):
    chunks = range(0, ROWS, 256)
    load = pltpu.make_async_copy(x, xb, xsem)
    loads = [pltpu.make_async_copy(w.at[t], wv.at[t], wsems.at[t]) for t in range(TAPS)]
    stores = [
        pltpu.make_async_copy(pv.at[pl.ds(r, 256)], pre.at[pl.ds(r, 256)], psems.at[r // 256])
        for r in chunks
    ]
    load.start()
    loads[0].start()
    xf[0:8, :] = jnp.zeros((8, C), F32)
    xf[8 + ROWS :, :] = jnp.zeros((8, C), F32)
    even = par[0] == 0
    one, two = got1[...].astype(F32), got2[...].astype(F32)
    xf[6:8, :] = jnp.where(even, two, one)
    xf[8 + ROWS : 10 + ROWS, :] = jnp.where(even, one, two)
    load.wait()
    loads[1].start()
    xf[8 : 8 + ROWS, :] = xb[...].astype(F32)
    for t in range(TAPS):
        loads[t].wait()
        if t + 2 < TAPS:
            loads[t + 2].start()
        for r in chunks:
            got = mm(xf[6 + t + r : 6 + t + r + 256, :].astype(BF), wv[t])
            if t == 0:
                pv[r : r + 256, :] = got
            else:
                pv[r : r + 256, :] += got
            if t == TAPS - 1:
                stores[r // 256].start()
    xp[...] = xf[...].astype(BF)
    for store in stores:
        store.wait()


def conv_apply(par, x, got1, got2, w, after):
    near = pl.BlockSpec(memory_space=pltpu.HBM)
    return pl.pallas_call(
        conv_kernel,
        out_shape=(far((ROWS, C), F32), sds((ROWS + 16, C), BF)),
        in_specs=[SM, near, VM, VM, near, ANY],
        out_specs=(near, VM),
        scratch_shapes=[
            pltpu.VMEM((ROWS, C), BF),
            pltpu.VMEM((ROWS + 16, C), F32),
            pltpu.VMEM((TAPS, C, C), BF),
            pltpu.VMEM((ROWS, C), F32),
            pltpu.SemaphoreType.DMA,
            pltpu.SemaphoreType.DMA((TAPS,)),
            pltpu.SemaphoreType.DMA((3,)),
        ],
        name="conv_apply",
        compiler_params=params(24),
        cost_estimate=cost(2 * 5 * 768**3, 9500000),
    )(par, hbm(x), got1, got2, hbm(w), after)


def gelu_kernel(pre, x, after, slope, pooled, means):
    for p in range(0, ROWS, 64):
        value = pre[p : p + 64, :]
        cumul = 0.5 * (1.0 + lax.erf(value * SQRT_HALF))
        bell = value * INV_ROOT_TWO_PI * jnp.exp(-0.5 * value * value)
        slope[p : p + 64, :] = (cumul + bell).astype(BF)
        block = (x[p : p + 64, :].astype(F32) + value * cumul).astype(BF).astype(F32)
        means[p // FACTOR : p // FACTOR + 4, :] = jnp.mean(block.reshape(4, FACTOR, C), axis=1)
    pooled[...] = means[...].astype(BF)


def gelu_pool(pre, x, after):
    return pl.pallas_call(
        gelu_kernel,
        out_shape=(far((ROWS, C), BF), far((ATT, C), BF)),
        in_specs=[VM, VM, ANY],
        out_specs=(VM, VM),
        scratch_shapes=[pltpu.VMEM((ATT, C), F32)],
        name="gelu_pool",
        compiler_params=params(16),
        cost_estimate=cost(3000000000, 5000000, 2 * 768 * 768),
    )(hbm(pre), hbm(x), after)


def turn_kernel(xp, xt, alts, edge):
    for r in range(0, ROWS, 128):
        xt[:, r : r + 128] = xp[8 + r : 8 + r + 128, :].T
    last = xp[8 + ROWS - 128 : 8 + ROWS, :].astype(F32)
    first = xp[8 : 8 + 128, :].astype(F32)
    top = xp[0:16, :].astype(F32)[0:8]
    bottom = xp[ROWS : ROWS + 16, :].astype(F32)[8:16]
    edge[...] = last
    edge[126:128, :] = top[6:8]
    alts[:, 0:128] = edge[...].astype(BF).T
    edge[126:127, :] = last[126:127]
    alts[:, 128:256] = edge[...].astype(BF).T
    edge[...] = first
    edge[0:1, :] = bottom[0:1]
    alts[:, 256:384] = edge[...].astype(BF).T
    edge[1:2, :] = bottom[1:2]
    alts[:, 384:512] = edge[...].astype(BF).T


def turn_input(xp):
    return pl.pallas_call(
        turn_kernel,
        out_shape=(sds((C, ROWS), BF), sds((C, 512), BF)),
        in_specs=[VM],
        out_specs=(VM, VM),
        scratch_shapes=[pltpu.VMEM((128, C), F32)],
        name="turn_input",
        compiler_params=params(12),
        cost_estimate=cost(10 * 768 * 768, 3200000),
    )(xp)


def slope_kernel(
    core, parts, skip, slope, pre, send, keep, pool, skip_v, slope_v, pre_v, pool_v, in_sems, out_sems, pool_sem
):
    chunks = range(0, ROWS, 256)
    loads = []
    for r in chunks:
        rows = pl.ds(r, 256)
        loads.append(pltpu.make_async_copy(skip.at[rows], skip_v.at[rows], in_sems.at[0, r // 256]))
        loads.append(pltpu.make_async_copy(slope.at[rows], slope_v.at[rows], in_sems.at[1, r // 256]))
    for load in loads:
        load.start()
    total = jnp.sum(parts[:, 0:ATT, :].astype(F32), axis=0) * (1.0 / FACTOR)
    pool_v[...] = total
    stores = [pltpu.make_async_copy(pool_v, pool, pool_sem)]
    stores[0].start()
    for r in chunks:
        loads[r // 128].wait()
        loads[r // 128 + 1].wait()
        for p in range(r, r + 256, 128):
            j = p // FACTOR
            piece = jnp.broadcast_to(total[j : j + 8, None, :], (8, FACTOR, C)).reshape(128, C)
            rows = slice(p, p + 128)
            grad = (skip_v[rows, :].astype(F32) + piece) * slope_v[rows, :].astype(F32)
            pre_v[rows, :] = grad.astype(BF)
        rows = pl.ds(r, 256)
        stores.append(pltpu.make_async_copy(pre_v.at[rows], pre.at[rows], out_sems.at[r // 256]))
        stores[-1].start()

    @pl.when(core[0] == 0)
    def _():
        keep[...] = pre_v[:, 0:HALF]
        send[...] = pre_v[:, HALF:]

    @pl.when(core[0] != 0)
    def _():
        keep[...] = pre_v[:, HALF:]
        send[...] = pre_v[:, 0:HALF]

    for store in stores:
        store.wait()


def pre_grads(core, parts, skip, slope):
    near = pl.BlockSpec(memory_space=pltpu.HBM)
    return pl.pallas_call(
        slope_kernel,
        out_shape=(
            far((ROWS, C), BF),
            sds((ROWS, HALF), BF),
            sds((ROWS, HALF), BF),
            far((ATT, C), F32),
        ),
        in_specs=[SM, VM, near, near],
        out_specs=(near, VM, VM, near),
        scratch_shapes=[
            pltpu.VMEM((ROWS, C), BF),
            pltpu.VMEM((ROWS, C), BF),
            pltpu.VMEM((ROWS, C), BF),
            pltpu.VMEM((ATT, C), F32),
            pltpu.SemaphoreType.DMA((2, 3)),
            pltpu.SemaphoreType.DMA((3,)),
            pltpu.SemaphoreType.DMA,
        ],
        name="pre_grads",
        compiler_params=params(12),
        cost_estimate=cost(5 * 768 * 768, 6000000),
    )(core, parts, hbm(skip), hbm(slope))


def weights_kernel(xt0, al0, xt1, al1, y0, y1, p0, p1, s0, s1, out, yf, wide, rest, made, sems):
    def copy(t):
        cols = pl.ds(t * HALF, HALF)
        return pltpu.make_async_copy(made.at[t], out.at[:, cols], sems.at[t])

    def pooled(ref):
        return jnp.concatenate([ref[h, ATT : 2 * ATT, :] for h in range(HEADS)], axis=0)

    part = jnp.concatenate([pooled(p0), pooled(p1)], axis=0)
    made[TAPS, :, 0:QH] = tn(part, jnp.concatenate([s0[...], s1[...]], axis=0)).astype(BF)
    made[TAPS, :, QH:HALF] = jnp.zeros((C, HALF - QH), BF)
    copy(TAPS).start()
    for i, ref in enumerate((y0, y1)):
        got = ref[...].astype(F32)
        yf[i, 8 : 8 + ROWS, :] = got
        yf[i, 0:8, :] = got[ROWS - 8 :]
        yf[i, 8 + ROWS : 16 + ROWS, :] = got[0:8]
    chunks = range(0, C, 256)
    for r in chunks:
        rows = slice(r, r + 256)
        left = jnp.concatenate([xt0[rows, :], xt1[rows, :]], axis=1)
        made[2, rows, :] = mm(left, jnp.concatenate([y0[...], y1[...]], axis=0)).astype(BF)
    copy(2).start()
    for g, taps in enumerate(((0, 1), (3, 4))):
        base, spot = (0, 2 * 256) if g == 0 else (256, 0)
        for k, t in enumerate(taps):
            cols = slice(k * HALF, (k + 1) * HALF)
            for i in range(2):
                at = 10 - t + base
                wide[g, i * 512 : (i + 1) * 512, cols] = yf[i, at : at + 512, :].astype(BF)
                at = 10 - t + spot
                rest[2 * g + k, i * 256 : (i + 1) * 256, :] = yf[i, at : at + 256, :].astype(BF)
        for r in chunks:
            rows = slice(r, r + 256)
            left = jnp.concatenate([xt0[rows, base : base + 512], xt1[rows, base : base + 512]], axis=1)
            both = mm(left, wide[g])
            for k, t in enumerate(taps):
                tiles = []
                for xt, al in ((xt0, al0), (xt1, al1)):
                    if g == 0:
                        tiles += [xt[rows, 512:640], al[rows, t * 128 : t * 128 + 128]]
                    else:
                        tiles += [al[rows, (t - 1) * 128 : t * 128], xt[rows, 128:256]]
                edge = mm(jnp.concatenate(tiles, axis=1), rest[2 * g + k])
                made[t, rows, :] = (both[:, k * HALF : (k + 1) * HALF] + edge).astype(BF)
        for t in taps:
            copy(t).start()
    for t in range(TAPS + 1):
        copy(t).wait()


def weight_grads(xt0, al0, xt1, al1, y0, y1, p0, p1, s0, s1):
    return pl.pallas_call(
        weights_kernel,
        out_shape=far((C, 2304), BF),
        in_specs=[VM] * 10,
        out_specs=pl.BlockSpec(memory_space=pltpu.HBM),
        scratch_shapes=[
            pltpu.VMEM((2, ROWS + 16, HALF), F32),
            pltpu.VMEM((2, 1024, 2 * HALF), BF),
            pltpu.VMEM((4, 512, HALF), BF),
            pltpu.VMEM((TAPS + 1, C, HALF), BF),
            pltpu.SemaphoreType.DMA((TAPS + 1,)),
        ],
        name="weight_grads",
        compiler_params=params(32),
        cost_estimate=cost(2 * 5 * 768 * 1536 * 384, 10000000),
    )(xt0, al0, xt1, al1, y0, y1, p0, p1, s0, s1)


def adjoint_kernel(par, pre, w, skip, pool, out, near, far_, first, last, yf, acc):
    tap = pl.program_id(0)

    @pl.when(tap == 0)
    def _():
        yf[0:16, :] = jnp.zeros((16, C), F32)
        yf[16 : 16 + ROWS, :] = pre[...].astype(F32)
        yf[16 + ROWS :, :] = jnp.zeros((16, C), F32)
        acc[0:8, :] = jnp.zeros((8, C), F32)
        acc[8 + ROWS :, :] = jnp.zeros((8, C), F32)
        for r in range(0, ATT, 8):
            piece = jnp.broadcast_to(pool[r : r + 8, :][:, None, :], (8, FACTOR, C)).reshape(128, C)
            rows = slice(r * FACTOR, r * FACTOR + 128)
            acc[8 + r * FACTOR : 136 + r * FACTOR, :] = skip[rows, :].astype(F32) + piece

    for t in range(TAPS):

        @pl.when(tap == t)
        def _(t=t):
            for r, n in ((0, 256), (256, 256), (512, 272)):
                rows = yf[10 - t + r : 10 - t + r + n, :].astype(BF)
                acc[r : r + n, :] += nt(rows, w[0])

    @pl.when(tap == TAPS - 1)
    def _():
        out[...] = acc[8 : 8 + ROWS, :].astype(BF)
        first[...] = acc[8:16, :]
        last[...] = acc[ROWS : ROWS + 8, :]
        even = par[0] == 0
        before, after = acc[0:8, :], acc[ROWS + 8 :, :]
        near[...] = jnp.where(even, after, before)
        far_[...] = jnp.where(even, before, after)


def conv_adjoint(par, pre, w, skip, pool):
    whole = lambda a, b: pl.BlockSpec((a, b), lambda t: (0, 0))
    return pl.pallas_call(
        adjoint_kernel,
        grid=(TAPS,),
        out_shape=(far((ROWS, C), BF),) + (sds((8, C), F32),) * 4,
        in_specs=[
            SM,
            whole(ROWS, C),
            pl.BlockSpec((1, C, C), lambda t: (t, 0, 0)),
            whole(ROWS, C),
            whole(ATT, C),
        ],
        out_specs=(whole(ROWS, C),) + (whole(8, C),) * 4,
        scratch_shapes=[pltpu.VMEM((ROWS + 32, C), F32), pltpu.VMEM((ROWS + 16, C), F32)],
        name="conv_adjoint",
        compiler_params=params(24),
        cost_estimate=cost(2 * 5 * 768**3, 9500000),
    )(par, hbm(pre), hbm(w), hbm(skip), hbm(pool))


def edge_kernel(par, rows, first, last, got1, got2, out):
    step = pl.program_id(0)
    held = rows[...].astype(F32)
    even = par[0] == 0

    @pl.when(step == 0)
    def _():
        top = jnp.where(even, got2[...], got1[...])
        out[...] = jnp.concatenate([first[...] + top, held[8:16]], axis=0).astype(BF)

    @pl.when(step != 0)
    def _():
        bottom = jnp.where(even, got1[...], got2[...])
        out[...] = jnp.concatenate([held[0:8], last[...] + bottom], axis=0).astype(BF)


def add_edges(par, rows, first, last, got1, got2):
    block = pl.BlockSpec((16, C), lambda i: (i * (ROWS // 16 - 1), 0))
    whole = pl.BlockSpec((8, C), lambda i: (0, 0))
    return pl.pallas_call(
        edge_kernel,
        grid=(2,),
        out_shape=far((ROWS, C), BF),
        in_specs=[SM, block, whole, whole, whole, whole],
        out_specs=block,
        input_output_aliases={1: 0},
        name="add_edges",
        compiler_params=params(8),
        cost_estimate=cost(30000, 150000),
    )(par, hbm(rows), first, last, got1, got2)


def sum_kernel(parts, after, after2, out):
    step = pl.program_id(0)

    @pl.when(step < TAPS)
    def _():
        total = parts[0].astype(F32)
        for s in range(1, 32):
            total = total + parts[s].astype(F32)
        out[:, pl.ds(pl.multiple_of(step * HALF, HALF), HALF)] = total.astype(BF)

    @pl.when(step == TAPS)
    def _():
        for h in range(HEADS):
            total = parts[4 * h].astype(F32)
            for s in range(4 * h + 1, 4 * h + 4):
                total = total + parts[s].astype(F32)
            at = TAPS * HALF + h * QH
            out[:, at : at + QH] = total[:, 0:QH].astype(BF)


def sum_partials(parts, after, after2):
    return pl.pallas_call(
        sum_kernel,
        grid=(TAPS + 1,),
        out_shape=sds((24, WIDE), BF),
        in_specs=[pl.BlockSpec((32, 24, HALF), lambda t: (0, 0, t)), ANY, ANY],
        out_specs=pl.BlockSpec((24, WIDE), lambda t: (0, 0)),
        name="sum_partials",
        compiler_params=params(8),
        cost_estimate=cost(32 * 24 * 2304, 3700000),
    )(parts, hbm(after), hbm(after2))


def add_kernel(a, b, after, out):
    out[...] = (a[...].astype(F32) + b[...].astype(F32)) * (1.0 / LOSS_SCALE)


def add_pair(a, b, after):
    return pl.pallas_call(
        add_kernel,
        out_shape=sds((24, WIDE), F32),
        in_specs=[VM] * 2 + [ANY],
        out_specs=VM,
        name="add_pair",
        compiler_params=params(8),
        cost_estimate=cost(300000, 1500000),
    )(a, b, hbm(after))


def place_kernel(core, mine, other, conv, proj):
    def put(low, high):
        for t in range(TAPS):
            conv[t, :, 0:HALF] = low[:, t * HALF : (t + 1) * HALF]
            conv[t, :, HALF:] = high[:, t * HALF : (t + 1) * HALF]
        for h in range(HEADS):
            at = h * HD
            got = TAPS * HALF + h * QH
            proj[:, at : at + HD] = low[:, got : got + HD]
            proj[:, 1536 + at : 1536 + at + HD] = jnp.concatenate(
                [low[:, got + HD : got + QH], high[:, got : got + HD // 2]], axis=1
            )
            proj[:, 3072 + at : 3072 + at + HD] = high[:, got + HD // 2 : got + QH]

    @pl.when(core[0] == 0)
    def _():
        put(mine, other)

    @pl.when(core[0] != 0)
    def _():
        put(other, mine)


def place(core, mine, other):
    return pl.pallas_call(
        place_kernel,
        out_shape=(far((TAPS, 24, C), F32), far((24, 4608), F32)),
        in_specs=[SM, VM, VM],
        out_specs=(VM, VM),
        name="place",
        compiler_params=params(8),
        cost_estimate=cost(0, 2500000),
    )(core, mine, other)


NEAR = [(i, i ^ 1) for i in range(32)]
NEXT = [pair for i in range(1, 31, 2) for pair in ((i, i + 1), (i + 1, i))]


def local(conv_input, skip_grad, conv_weight, proj_weight, query, key, value, grad):
    core = lax.axis_index("core").astype(jnp.int32).reshape(1)
    head = lax.axis_index(HAX).astype(jnp.int32)
    pair, odd = (head // 2).reshape(1), (head % 2).reshape(1)
    x, skip = conv_input[0], skip_grad[0]

    packed = pack_heads(query[0], key[0], value[0], grad[0])
    own = lax.all_to_all(packed, HAX, 0, 0, tiled=True).reshape(BLK, 4 * HD)
    wh = head_weights(pair, odd, proj_weight, packed)
    qg_own, kv_own = split_own(own, wh)
    qg = lax.ppermute(qg_own, "z", A_PAIR)
    kv = lax.ppermute(kv_own, "z", B_PAIR)

    par = (lax.axis_index("z") % 2).astype(jnp.int32).reshape(1)
    head_rows, tail_rows = x[0:2], x[ROWS - 2 :]
    got1 = lax.ppermute(jnp.where(par[0] == 0, tail_rows, head_rows), SEQ, NEAR)
    got2 = lax.ppermute(jnp.where(par[0] == 0, head_rows, tail_rows), SEQ, NEXT)
    early, xp = conv_apply(par, x, got1, got2, conv_weight, qg_own)

    st = att_stats(own, qg, kv, early)
    st2 = lax.ppermute(st, "z", A_PAIR)
    dq_own, dq_send, dkv_own, dkv_send = att_grads(own, qg, kv, st, st2, wh)
    dq_in = lax.ppermute(dq_send, "z", A_PAIR)
    dkv_in = lax.ppermute(dkv_send, "z", B_PAIR)
    slope, pooled = gelu_pool(early, x, dq_send)
    pool_part, s0, s_send = att_join(core, dq_own, dkv_own, dq_in, dkv_in, wh, pooled)
    parts = lax.all_to_all(pool_part, HAX, 0, 0, tiled=True)
    parts, xp = lax.optimization_barrier((parts, xp))
    parts_sib = lax.ppermute(parts, "core", SWAP)
    xp_sib = lax.ppermute(xp, "core", SWAP)
    s1 = lax.ppermute(s_send, "core", SWAP)
    xt0, al0 = turn_input(xp)
    xt1, al1 = turn_input(xp_sib)

    pre, y_send, y0, pool = pre_grads(core, parts, skip, slope)
    y1 = lax.ppermute(y_send, "core", SWAP)
    terms = weight_grads(xt0, al0, xt1, al1, y0, y1, parts, parts_sib, s0, s1)
    got = lax.all_to_all(terms.reshape(32, 24, 2304), SEQ, 0, 0, tiled=True)

    rows, near, next_, first, last = conv_adjoint(par, pre, conv_weight, skip, pool)
    rim1 = lax.ppermute(near, SEQ, NEAR)
    rim2 = lax.ppermute(next_, SEQ, NEXT)

    total = sum_partials(got, rim1, rim2)
    total_far = lax.ppermute(total, "yh", SWAP)
    input_grad = add_edges(par, rows, first, last, rim1, rim2)
    mine = add_pair(total, total_far, input_grad)
    other = lax.ppermute(mine, "core", SWAP)
    conv_grad, proj_grad = place(core, mine, other)
    return input_grad[None], conv_grad, proj_grad


def solution(mesh):
    fine = Mesh(mesh.devices.reshape(2, 2, 2, 4, 4), ("yh", "core", "yl", "x", "z"))
    rows = P(DP, SEQ, None)
    return jax.shard_map(
        local,
        mesh=fine,
        in_specs=(rows, rows, P(), P(), rows, rows, rows, rows),
        out_specs=(rows, P(None, SEQ, None), P(SEQ, None)),
        check_vma=False,
    )
```

```python
import jax
import jax.numpy as jnp
from jax import lax
from jax.experimental import pallas as pl
from jax.experimental.pallas import tpu as pltpu
from jax.sharding import Mesh, PartitionSpec as P

HEADS = 8
TAPS = 5
LOSS_SCALE = 32
HD = 192
C = 768
ROWS = 768
ATT = 48
BLK = 384
FACTOR = 16
HALF = 384
QH = 288
WIDE = 5 * HALF + 8 * QH
SCALE = HD ** (-0.5)
SQRT_HALF = 0.7071067811865476
INV_ROOT_TWO_PI = 0.3989422804014327

BF = jnp.bfloat16
F32 = jnp.float32
DP = ("yh", "core")
SEQ = ("yl", "x", "z")
HAX = ("yl", "x")

NT = (((1,), (1,)), ((), ()))
TN = (((0,), (0,)), ((), ()))

A_PAIR = [(0, 1), (1, 0), (2, 3), (3, 2)]
B_PAIR = [(0, 3), (3, 0), (1, 2), (2, 1)]
SWAP = [(0, 1), (1, 0)]


def sds(shape, dtype):
    return jax.ShapeDtypeStruct(shape, dtype)


def far(shape, dtype):
    return pltpu.HBM(shape, dtype)


def hbm(x):
    return pltpu.with_memory_space_constraint(x, pltpu.HBM)


def params(mib):
    return pltpu.CompilerParams(vmem_limit_bytes=mib * 1024 * 1024)


def cost(flops, nbytes, trans=0):
    return pl.CostEstimate(flops=flops, bytes_accessed=nbytes, transcendentals=trans)


VM = pl.BlockSpec()
ANY = pl.BlockSpec(memory_space=pl.ANY)
SM = pl.BlockSpec(memory_space=pltpu.SMEM)


def nt(a, b):
    return lax.dot_general(a, b, NT, preferred_element_type=F32)


def tn(a, b):
    return lax.dot_general(a, b, TN, preferred_element_type=F32)


def mm(a, b):
    return jnp.dot(a, b, preferred_element_type=F32)


def pack_kernel(q, k, v, g, out, held, made, in_sems, out_sems):
    loads = [pltpu.make_async_copy(ref, held.at[i], in_sems.at[i]) for i, ref in enumerate((q, g, k, v))]
    for load in loads:
        load.start()
    stores = []
    for half in range(2):
        for i in (2 * half, 2 * half + 1):
            loads[i].wait()
            for h in range(HEADS):
                made[h, :, i * HD : (i + 1) * HD] = held[i, :, h * HD : (h + 1) * HD]
        cols = pl.ds(half * 2 * HD, 2 * HD)
        stores.append(pltpu.make_async_copy(made.at[:, :, cols], out.at[:, :, cols], out_sems.at[half]))
        stores[-1].start()
    for store in stores:
        store.wait()


def pack_heads(q, k, v, g):
    near = pl.BlockSpec(memory_space=pltpu.HBM)
    return pl.pallas_call(
        pack_kernel,
        out_shape=far((HEADS, ATT, 4 * HD), BF),
        in_specs=[near] * 4,
        out_specs=near,
        scratch_shapes=[
            pltpu.VMEM((4, ATT, HEADS * HD), BF),
            pltpu.VMEM((HEADS, ATT, 4 * HD), BF),
            pltpu.SemaphoreType.DMA((4,)),
            pltpu.SemaphoreType.DMA((2,)),
        ],
        name="pack_heads",
        compiler_params=params(8),
        cost_estimate=cost(0, 1200000),
    )(hbm(q), hbm(k), hbm(v), hbm(g))


def att_parts(own, qg, kv):
    query = jnp.concatenate([own[:, 0:HD], qg[:, 0:HD]], axis=0)
    grads = jnp.concatenate([own[:, HD : 2 * HD], qg[:, HD : 2 * HD]], axis=0)
    keys = jnp.concatenate([own[:, 2 * HD : 3 * HD], kv[:, 0:HD]], axis=0)
    values = jnp.concatenate([own[:, 3 * HD : 4 * HD], kv[:, HD : 2 * HD]], axis=0)
    return query, grads, keys, values


def stats_kernel(own, qg, kv, after, out):
    query, grads, keys, values = att_parts(own, qg, kv)
    out[...] = jnp.zeros_like(out)
    for i in range(2):
        rows = slice(i * BLK, (i + 1) * BLK)
        scores = nt(keys, query[rows]) * SCALE
        top = jnp.max(scores, axis=0, keepdims=True)
        powers = jnp.exp(scores - top)
        pgrad = nt(values, grads[rows])
        out[0:1, rows] = top
        out[1:2, rows] = jnp.sum(powers, axis=0, keepdims=True)
        out[2:3, rows] = jnp.sum(powers * pgrad, axis=0, keepdims=True)


def att_stats(own, qg, kv, after):
    return pl.pallas_call(
        stats_kernel,
        out_shape=sds((8, 2 * BLK), F32),
        in_specs=[VM] * 3 + [ANY],
        out_specs=VM,
        name="att_stats",
        compiler_params=params(16),
        cost_estimate=cost(8000000000, 1200000, 768 * 768),
    )(own, qg, kv, hbm(after))


def grads_kernel(own, qg, kv, st, st2, after, dq_own, dq_send, dkv_own, dkv_send):
    query, grads, keys, values = att_parts(own, qg, kv)
    dk = jnp.zeros((2 * BLK, HD), F32)
    dv = jnp.zeros((2 * BLK, HD), F32)
    for i in range(2):
        rows = slice(i * BLK, (i + 1) * BLK)
        other = slice((1 - i) * BLK, (2 - i) * BLK)
        m0, m1 = st[0:1, rows], st2[0:1, other]
        top = jnp.maximum(m0, m1)
        e0, e1 = jnp.exp(m0 - top), jnp.exp(m1 - top)
        inv = 1.0 / (st[1:2, rows] * e0 + st2[1:2, other] * e1)
        delta = (st[2:3, rows] * e0 + st2[2:3, other] * e1) * inv
        scores = nt(keys, query[rows]) * SCALE
        probs = jnp.exp(scores - top) * inv
        pgrad = nt(values, grads[rows])
        sgrad = (probs * (pgrad - delta)).astype(BF)
        dq = tn(sgrad, keys) * SCALE
        dk = dk + mm(sgrad, query[rows])
        dv = dv + mm(probs.astype(BF), grads[rows])
        if i == 0:
            dq_own[...] = dq.astype(BF)
        else:
            dq_send[:, 0:HD] = dq[0 : BLK // 2].astype(BF)
            dq_send[:, HD : 2 * HD] = dq[BLK // 2 : BLK].astype(BF)
    dk = dk * SCALE
    dkv_own[:, 0:HD] = dk[0:BLK].astype(BF)
    dkv_own[:, HD : 2 * HD] = dv[0:BLK].astype(BF)
    dkv_send[:, 0:HD] = dk[BLK:].astype(BF)
    dkv_send[:, HD : 2 * HD] = dv[BLK:].astype(BF)


def att_grads(own, qg, kv, st, st2, after):
    return pl.pallas_call(
        grads_kernel,
        out_shape=(
            far((BLK, HD), BF),
            sds((BLK // 2, 2 * HD), BF),
            far((BLK, 2 * HD), BF),
            sds((BLK, 2 * HD), BF),
        ),
        in_specs=[VM] * 5 + [ANY],
        out_specs=(VM,) * 4,
        name="att_grads",
        compiler_params=params(20),
        cost_estimate=cost(20000000000, 3000000, 768 * 768),
    )(own, qg, kv, st, st2, hbm(after))


def split_kernel(own, after, qg, kv):
    qg[...] = own[:, 0 : 2 * HD]
    kv[...] = own[:, 2 * HD : 4 * HD]


def split_own(own, after):
    return pl.pallas_call(
        split_kernel,
        out_shape=(sds((BLK, 2 * HD), BF), sds((BLK, 2 * HD), BF)),
        in_specs=[VM, ANY],
        out_specs=(VM, VM),
        name="split_own",
        compiler_params=params(8),
        cost_estimate=cost(0, 1200000),
    )(own, hbm(after))


def head_kernel(pair, odd, wq, wk, wv, after, out):
    @pl.when(odd[0] == 0)
    def _():
        for p, ref in enumerate((wq, wk, wv)):
            out[p * HD : (p + 1) * HD, :] = ref[:, 0:HD].T

    @pl.when(odd[0] != 0)
    def _():
        for p, ref in enumerate((wq, wk, wv)):
            out[p * HD : (p + 1) * HD, :] = ref[:, HD : 2 * HD].T


def head_weights(pair, odd, weight, after):
    part = lambda p: pl.BlockSpec((C, 2 * HD), lambda i, pair, odd, p=p: (0, 4 * p + pair[0]))
    return pl.pallas_call(
        head_kernel,
        out_shape=far((3 * HD, C), BF),
        grid_spec=pltpu.PrefetchScalarGridSpec(
            num_scalar_prefetch=2,
            grid=(1,),
            in_specs=[part(0), part(1), part(2), ANY],
            out_specs=pl.BlockSpec((3 * HD, C), lambda i, pair, odd: (0, 0)),
        ),
        name="head_weights",
        compiler_params=params(12),
        cost_estimate=cost(0, 3000000),
    )(pair, odd, hbm(weight), hbm(weight), hbm(weight), after)


def join_kernel(core, dq_own, dkv_own, dq_in, dkv_in, wh, pooled, pool, keep, send, made, sems, sem2):
    others = [
        pltpu.make_async_copy(pooled, pool.at[h, pl.ds(ATT, ATT)], sem2.at[h]) for h in range(HEADS)
    ]
    for other in others:
        other.start()
    dq_got = jnp.concatenate([dq_in[:, 0:HD], dq_in[:, HD : 2 * HD]], axis=0).astype(F32)
    dq = (dq_own[...].astype(F32) + dq_got).astype(BF)
    dkv = (dkv_own[...].astype(F32) + dkv_in[...].astype(F32)).astype(BF)
    qkv = jnp.concatenate([dq, dkv], axis=1)
    stores = []
    for r in range(0, BLK, 4 * ATT):
        made[r : r + 4 * ATT, :] = mm(qkv[r : r + 4 * ATT], wh[...]).astype(BF)
        for h in range(r // ATT, r // ATT + 4):
            rows = pl.ds(h * ATT, ATT)
            stores.append(pltpu.make_async_copy(made.at[rows], pool.at[h, pl.ds(0, ATT)], sems.at[h]))
            stores[-1].start()

    @pl.when(core[0] == 0)
    def _():
        keep[...] = qkv[:, 0:QH]
        send[...] = qkv[:, QH : 2 * QH]

    @pl.when(core[0] != 0)
    def _():
        keep[...] = qkv[:, QH : 2 * QH]
        send[...] = qkv[:, 0:QH]

    for copy in others + stores:
        copy.wait()


def att_join(core, dq_own, dkv_own, dq_in, dkv_in, wh, pooled):
    return pl.pallas_call(
        join_kernel,
        out_shape=(far((HEADS, 2 * ATT, C), BF), sds((BLK, QH), BF), sds((BLK, QH), BF)),
        in_specs=[SM] + [VM] * 6,
        out_specs=(pl.BlockSpec(memory_space=pltpu.HBM), VM, VM),
        scratch_shapes=[
            pltpu.VMEM((BLK, C), BF),
            pltpu.SemaphoreType.DMA((HEADS,)),
            pltpu.SemaphoreType.DMA((HEADS,)),
        ],
        name="att_join",
        compiler_params=params(12),
        cost_estimate=cost(10000000000, 3500000),
    )(core, hbm(dq_own), hbm(dkv_own), dq_in, dkv_in, hbm(wh), hbm(pooled))


def conv_kernel(par, x, got1, got2, w, after, pre, xp, xb, xf, wv, pv, xsem, wsems, psems):
    chunks = range(0, ROWS, 256)
    load = pltpu.make_async_copy(x, xb, xsem)
    loads = [pltpu.make_async_copy(w.at[t], wv.at[t], wsems.at[t]) for t in range(TAPS)]
    stores = [
        pltpu.make_async_copy(pv.at[pl.ds(r, 256)], pre.at[pl.ds(r, 256)], psems.at[r // 256])
        for r in chunks
    ]
    load.start()
    loads[0].start()
    xf[0:8, :] = jnp.zeros((8, C), F32)
    xf[8 + ROWS :, :] = jnp.zeros((8, C), F32)
    even = par[0] == 0
    one, two = got1[...].astype(F32), got2[...].astype(F32)
    xf[6:8, :] = jnp.where(even, two, one)
    xf[8 + ROWS : 10 + ROWS, :] = jnp.where(even, one, two)
    load.wait()
    loads[1].start()
    xf[8 : 8 + ROWS, :] = xb[...].astype(F32)
    for t in range(TAPS):
        loads[t].wait()
        if t + 2 < TAPS:
            loads[t + 2].start()
        for r in chunks:
            got = mm(xf[6 + t + r : 6 + t + r + 256, :].astype(BF), wv[t])
            if t == 0:
                pv[r : r + 256, :] = got
            else:
                pv[r : r + 256, :] += got
            if t == TAPS - 1:
                stores[r // 256].start()
    xp[...] = xf[...].astype(BF)
    for store in stores:
        store.wait()


def conv_apply(par, x, got1, got2, w, after):
    near = pl.BlockSpec(memory_space=pltpu.HBM)
    return pl.pallas_call(
        conv_kernel,
        out_shape=(far((ROWS, C), F32), sds((ROWS + 16, C), BF)),
        in_specs=[SM, near, VM, VM, near, ANY],
        out_specs=(near, VM),
        scratch_shapes=[
            pltpu.VMEM((ROWS, C), BF),
            pltpu.VMEM((ROWS + 16, C), F32),
            pltpu.VMEM((TAPS, C, C), BF),
            pltpu.VMEM((ROWS, C), F32),
            pltpu.SemaphoreType.DMA,
            pltpu.SemaphoreType.DMA((TAPS,)),
            pltpu.SemaphoreType.DMA((3,)),
        ],
        name="conv_apply",
        compiler_params=params(24),
        cost_estimate=cost(2 * 5 * 768**3, 9500000),
    )(par, hbm(x), got1, got2, hbm(w), after)


def gelu_kernel(pre, x, after, slope, pooled, means):
    for p in range(0, ROWS, 64):
        value = pre[p : p + 64, :]
        cumul = 0.5 * (1.0 + lax.erf(value * SQRT_HALF))
        bell = value * INV_ROOT_TWO_PI * jnp.exp(-0.5 * value * value)
        slope[p : p + 64, :] = (cumul + bell).astype(BF)
        block = (x[p : p + 64, :].astype(F32) + value * cumul).astype(BF).astype(F32)
        means[p // FACTOR : p // FACTOR + 4, :] = jnp.mean(block.reshape(4, FACTOR, C), axis=1)
    pooled[...] = means[...].astype(BF)


def gelu_pool(pre, x, after):
    return pl.pallas_call(
        gelu_kernel,
        out_shape=(far((ROWS, C), BF), far((ATT, C), BF)),
        in_specs=[VM, VM, ANY],
        out_specs=(VM, VM),
        scratch_shapes=[pltpu.VMEM((ATT, C), F32)],
        name="gelu_pool",
        compiler_params=params(16),
        cost_estimate=cost(3000000000, 5000000, 2 * 768 * 768),
    )(hbm(pre), hbm(x), after)


def turn_kernel(xp, xt, alts, edge):
    for r in range(0, ROWS, 128):
        xt[:, r : r + 128] = xp[8 + r : 8 + r + 128, :].T
    last = xp[8 + ROWS - 128 : 8 + ROWS, :].astype(F32)
    first = xp[8 : 8 + 128, :].astype(F32)
    top = xp[0:16, :].astype(F32)[0:8]
    bottom = xp[ROWS : ROWS + 16, :].astype(F32)[8:16]
    edge[...] = last
    edge[126:128, :] = top[6:8]
    alts[:, 0:128] = edge[...].astype(BF).T
    edge[126:127, :] = last[126:127]
    alts[:, 128:256] = edge[...].astype(BF).T
    edge[...] = first
    edge[0:1, :] = bottom[0:1]
    alts[:, 256:384] = edge[...].astype(BF).T
    edge[1:2, :] = bottom[1:2]
    alts[:, 384:512] = edge[...].astype(BF).T


def turn_input(xp):
    return pl.pallas_call(
        turn_kernel,
        out_shape=(sds((C, ROWS), BF), sds((C, 512), BF)),
        in_specs=[VM],
        out_specs=(VM, VM),
        scratch_shapes=[pltpu.VMEM((128, C), F32)],
        name="turn_input",
        compiler_params=params(12),
        cost_estimate=cost(10 * 768 * 768, 3200000),
    )(xp)


def slope_kernel(
    core, parts, skip, slope, pre, send, keep, pool, skip_v, slope_v, pre_v, pool_v, in_sems, out_sems, pool_sem
):
    chunks = range(0, ROWS, 256)
    loads = []
    for r in chunks:
        rows = pl.ds(r, 256)
        loads.append(pltpu.make_async_copy(skip.at[rows], skip_v.at[rows], in_sems.at[0, r // 256]))
        loads.append(pltpu.make_async_copy(slope.at[rows], slope_v.at[rows], in_sems.at[1, r // 256]))
    for load in loads:
        load.start()
    total = jnp.sum(parts[:, 0:ATT, :].astype(F32), axis=0) * (1.0 / FACTOR)
    pool_v[...] = total
    stores = [pltpu.make_async_copy(pool_v, pool, pool_sem)]
    stores[0].start()
    for r in chunks:
        loads[r // 128].wait()
        loads[r // 128 + 1].wait()
        for p in range(r, r + 256, 128):
            j = p // FACTOR
            piece = jnp.broadcast_to(total[j : j + 8, None, :], (8, FACTOR, C)).reshape(128, C)
            rows = slice(p, p + 128)
            grad = (skip_v[rows, :].astype(F32) + piece) * slope_v[rows, :].astype(F32)
            pre_v[rows, :] = grad.astype(BF)
        rows = pl.ds(r, 256)
        stores.append(pltpu.make_async_copy(pre_v.at[rows], pre.at[rows], out_sems.at[r // 256]))
        stores[-1].start()

    @pl.when(core[0] == 0)
    def _():
        keep[...] = pre_v[:, 0:HALF]
        send[...] = pre_v[:, HALF:]

    @pl.when(core[0] != 0)
    def _():
        keep[...] = pre_v[:, HALF:]
        send[...] = pre_v[:, 0:HALF]

    for store in stores:
        store.wait()


def pre_grads(core, parts, skip, slope):
    near = pl.BlockSpec(memory_space=pltpu.HBM)
    return pl.pallas_call(
        slope_kernel,
        out_shape=(
            far((ROWS, C), BF),
            sds((ROWS, HALF), BF),
            sds((ROWS, HALF), BF),
            far((ATT, C), F32),
        ),
        in_specs=[SM, VM, near, near],
        out_specs=(near, VM, VM, near),
        scratch_shapes=[
            pltpu.VMEM((ROWS, C), BF),
            pltpu.VMEM((ROWS, C), BF),
            pltpu.VMEM((ROWS, C), BF),
            pltpu.VMEM((ATT, C), F32),
            pltpu.SemaphoreType.DMA((2, 3)),
            pltpu.SemaphoreType.DMA((3,)),
            pltpu.SemaphoreType.DMA,
        ],
        name="pre_grads",
        compiler_params=params(12),
        cost_estimate=cost(5 * 768 * 768, 6000000),
    )(core, parts, hbm(skip), hbm(slope))


def weights_kernel(xt0, al0, xt1, al1, y0, y1, p0, p1, s0, s1, out, yf, wide, rest, made, sems):
    def copy(t):
        cols = pl.ds(t * HALF, HALF)
        return pltpu.make_async_copy(made.at[t], out.at[:, cols], sems.at[t])

    def pooled(ref):
        return jnp.concatenate([ref[h, ATT : 2 * ATT, :] for h in range(HEADS)], axis=0)

    part = jnp.concatenate([pooled(p0), pooled(p1)], axis=0)
    made[TAPS, :, 0:QH] = tn(part, jnp.concatenate([s0[...], s1[...]], axis=0)).astype(BF)
    made[TAPS, :, QH:HALF] = jnp.zeros((C, HALF - QH), BF)
    copy(TAPS).start()
    for i, ref in enumerate((y0, y1)):
        got = ref[...].astype(F32)
        yf[i, 8 : 8 + ROWS, :] = got
        yf[i, 0:8, :] = got[ROWS - 8 :]
        yf[i, 8 + ROWS : 16 + ROWS, :] = got[0:8]
    chunks = range(0, C, 256)
    for r in chunks:
        rows = slice(r, r + 256)
        left = jnp.concatenate([xt0[rows, :], xt1[rows, :]], axis=1)
        made[2, rows, :] = mm(left, jnp.concatenate([y0[...], y1[...]], axis=0)).astype(BF)
    copy(2).start()
    for g, taps in enumerate(((0, 1), (3, 4))):
        base, spot = (0, 2 * 256) if g == 0 else (256, 0)
        for k, t in enumerate(taps):
            cols = slice(k * HALF, (k + 1) * HALF)
            for i in range(2):
                at = 10 - t + base
                wide[g, i * 512 : (i + 1) * 512, cols] = yf[i, at : at + 512, :].astype(BF)
                at = 10 - t + spot
                rest[2 * g + k, i * 256 : (i + 1) * 256, :] = yf[i, at : at + 256, :].astype(BF)
        for r in chunks:
            rows = slice(r, r + 256)
            left = jnp.concatenate([xt0[rows, base : base + 512], xt1[rows, base : base + 512]], axis=1)
            both = mm(left, wide[g])
            for k, t in enumerate(taps):
                tiles = []
                for xt, al in ((xt0, al0), (xt1, al1)):
                    if g == 0:
                        tiles += [xt[rows, 512:640], al[rows, t * 128 : t * 128 + 128]]
                    else:
                        tiles += [al[rows, (t - 1) * 128 : t * 128], xt[rows, 128:256]]
                edge = mm(jnp.concatenate(tiles, axis=1), rest[2 * g + k])
                made[t, rows, :] = (both[:, k * HALF : (k + 1) * HALF] + edge).astype(BF)
        for t in taps:
            copy(t).start()
    for t in range(TAPS + 1):
        copy(t).wait()


def weight_grads(xt0, al0, xt1, al1, y0, y1, p0, p1, s0, s1):
    return pl.pallas_call(
        weights_kernel,
        out_shape=far((C, 2304), BF),
        in_specs=[VM] * 10,
        out_specs=pl.BlockSpec(memory_space=pltpu.HBM),
        scratch_shapes=[
            pltpu.VMEM((2, ROWS + 16, HALF), F32),
            pltpu.VMEM((2, 1024, 2 * HALF), BF),
            pltpu.VMEM((4, 512, HALF), BF),
            pltpu.VMEM((TAPS + 1, C, HALF), BF),
            pltpu.SemaphoreType.DMA((TAPS + 1,)),
        ],
        name="weight_grads",
        compiler_params=params(32),
        cost_estimate=cost(2 * 5 * 768 * 1536 * 384, 10000000),
    )(xt0, al0, xt1, al1, y0, y1, p0, p1, s0, s1)


def adjoint_kernel(par, pre, w, skip, pool, out, near, far_, first, last, yf, acc):
    tap = pl.program_id(0)

    @pl.when(tap == 0)
    def _():
        yf[0:16, :] = jnp.zeros((16, C), F32)
        yf[16 : 16 + ROWS, :] = pre[...].astype(F32)
        yf[16 + ROWS :, :] = jnp.zeros((16, C), F32)
        acc[0:8, :] = jnp.zeros((8, C), F32)
        acc[8 + ROWS :, :] = jnp.zeros((8, C), F32)
        for r in range(0, ATT, 8):
            piece = jnp.broadcast_to(pool[r : r + 8, :][:, None, :], (8, FACTOR, C)).reshape(128, C)
            rows = slice(r * FACTOR, r * FACTOR + 128)
            acc[8 + r * FACTOR : 136 + r * FACTOR, :] = skip[rows, :].astype(F32) + piece

    for t in range(TAPS):

        @pl.when(tap == t)
        def _(t=t):
            for r, n in ((0, 256), (256, 256), (512, 272)):
                rows = yf[10 - t + r : 10 - t + r + n, :].astype(BF)
                acc[r : r + n, :] += nt(rows, w[0])

    @pl.when(tap == TAPS - 1)
    def _():
        out[...] = acc[8 : 8 + ROWS, :].astype(BF)
        first[...] = acc[8:16, :]
        last[...] = acc[ROWS : ROWS + 8, :]
        even = par[0] == 0
        before, after = acc[0:8, :], acc[ROWS + 8 :, :]
        near[...] = jnp.where(even, after, before)
        far_[...] = jnp.where(even, before, after)


def conv_adjoint(par, pre, w, skip, pool):
    whole = lambda a, b: pl.BlockSpec((a, b), lambda t: (0, 0))
    return pl.pallas_call(
        adjoint_kernel,
        grid=(TAPS,),
        out_shape=(far((ROWS, C), BF),) + (sds((8, C), F32),) * 4,
        in_specs=[
            SM,
            whole(ROWS, C),
            pl.BlockSpec((1, C, C), lambda t: (t, 0, 0)),
            whole(ROWS, C),
            whole(ATT, C),
        ],
        out_specs=(whole(ROWS, C),) + (whole(8, C),) * 4,
        scratch_shapes=[pltpu.VMEM((ROWS + 32, C), F32), pltpu.VMEM((ROWS + 16, C), F32)],
        name="conv_adjoint",
        compiler_params=params(24),
        cost_estimate=cost(2 * 5 * 768**3, 9500000),
    )(par, hbm(pre), hbm(w), hbm(skip), hbm(pool))


def edge_kernel(par, rows, first, last, got1, got2, out):
    step = pl.program_id(0)
    held = rows[...].astype(F32)
    even = par[0] == 0

    @pl.when(step == 0)
    def _():
        top = jnp.where(even, got2[...], got1[...])
        out[...] = jnp.concatenate([first[...] + top, held[8:16]], axis=0).astype(BF)

    @pl.when(step != 0)
    def _():
        bottom = jnp.where(even, got1[...], got2[...])
        out[...] = jnp.concatenate([held[0:8], last[...] + bottom], axis=0).astype(BF)


def add_edges(par, rows, first, last, got1, got2):
    block = pl.BlockSpec((16, C), lambda i: (i * (ROWS // 16 - 1), 0))
    whole = pl.BlockSpec((8, C), lambda i: (0, 0))
    return pl.pallas_call(
        edge_kernel,
        grid=(2,),
        out_shape=far((ROWS, C), BF),
        in_specs=[SM, block, whole, whole, whole, whole],
        out_specs=block,
        input_output_aliases={1: 0},
        name="add_edges",
        compiler_params=params(8),
        cost_estimate=cost(30000, 150000),
    )(par, hbm(rows), first, last, got1, got2)


def sum_kernel(parts, after, after2, out):
    step = pl.program_id(0)

    @pl.when(step < TAPS)
    def _():
        total = parts[0].astype(F32)
        for s in range(1, 32):
            total = total + parts[s].astype(F32)
        out[:, pl.ds(pl.multiple_of(step * HALF, HALF), HALF)] = total.astype(BF)

    @pl.when(step == TAPS)
    def _():
        for h in range(HEADS):
            total = parts[4 * h].astype(F32)
            for s in range(4 * h + 1, 4 * h + 4):
                total = total + parts[s].astype(F32)
            at = TAPS * HALF + h * QH
            out[:, at : at + QH] = total[:, 0:QH].astype(BF)


def sum_partials(parts, after, after2):
    return pl.pallas_call(
        sum_kernel,
        grid=(TAPS + 1,),
        out_shape=sds((24, WIDE), BF),
        in_specs=[pl.BlockSpec((32, 24, HALF), lambda t: (0, 0, t)), ANY, ANY],
        out_specs=pl.BlockSpec((24, WIDE), lambda t: (0, 0)),
        name="sum_partials",
        compiler_params=params(8),
        cost_estimate=cost(32 * 24 * 2304, 3700000),
    )(parts, hbm(after), hbm(after2))


def add_kernel(a, b, after, out):
    out[...] = (a[...].astype(F32) + b[...].astype(F32)) * (1.0 / LOSS_SCALE)


def add_pair(a, b, after):
    return pl.pallas_call(
        add_kernel,
        out_shape=sds((24, WIDE), F32),
        in_specs=[VM] * 2 + [ANY],
        out_specs=VM,
        name="add_pair",
        compiler_params=params(8),
        cost_estimate=cost(300000, 1500000),
    )(a, b, hbm(after))


def place_kernel(core, mine, other, conv, proj):
    def put(low, high):
        for t in range(TAPS):
            conv[t, :, 0:HALF] = low[:, t * HALF : (t + 1) * HALF]
            conv[t, :, HALF:] = high[:, t * HALF : (t + 1) * HALF]
        for h in range(HEADS):
            at = h * HD
            got = TAPS * HALF + h * QH
            proj[:, at : at + HD] = low[:, got : got + HD]
            proj[:, 1536 + at : 1536 + at + HD] = jnp.concatenate(
                [low[:, got + HD : got + QH], high[:, got : got + HD // 2]], axis=1
            )
            proj[:, 3072 + at : 3072 + at + HD] = high[:, got + HD // 2 : got + QH]

    @pl.when(core[0] == 0)
    def _():
        put(mine, other)

    @pl.when(core[0] != 0)
    def _():
        put(other, mine)


def place(core, mine, other):
    return pl.pallas_call(
        place_kernel,
        out_shape=(far((TAPS, 24, C), F32), far((24, 4608), F32)),
        in_specs=[SM, VM, VM],
        out_specs=(VM, VM),
        name="place",
        compiler_params=params(8),
        cost_estimate=cost(0, 2500000),
    )(core, mine, other)


NEAR = [(i, i ^ 1) for i in range(32)]
NEXT = [pair for i in range(1, 31, 2) for pair in ((i, i + 1), (i + 1, i))]


def local(conv_input, skip_grad, conv_weight, proj_weight, query, key, value, grad):
    core = lax.axis_index("core").astype(jnp.int32).reshape(1)
    head = lax.axis_index(HAX).astype(jnp.int32)
    pair, odd = (head // 2).reshape(1), (head % 2).reshape(1)
    x, skip = conv_input[0], skip_grad[0]

    packed = pack_heads(query[0], key[0], value[0], grad[0])
    own = lax.all_to_all(packed, HAX, 0, 0, tiled=True).reshape(BLK, 4 * HD)
    wh = head_weights(pair, odd, proj_weight, packed)
    qg_own, kv_own = split_own(own, wh)
    qg = lax.ppermute(qg_own, "z", A_PAIR)
    kv = lax.ppermute(kv_own, "z", B_PAIR)

    par = (lax.axis_index("z") % 2).astype(jnp.int32).reshape(1)
    head_rows, tail_rows = x[0:2], x[ROWS - 2 :]
    got1 = lax.ppermute(jnp.where(par[0] == 0, tail_rows, head_rows), SEQ, NEAR)
    got2 = lax.ppermute(jnp.where(par[0] == 0, head_rows, tail_rows), SEQ, NEXT)
    early, xp = conv_apply(par, x, got1, got2, conv_weight, qg_own)

    st = att_stats(own, qg, kv, early)
    st2 = lax.ppermute(st, "z", A_PAIR)
    dq_own, dq_send, dkv_own, dkv_send = att_grads(own, qg, kv, st, st2, wh)
    dq_in = lax.ppermute(dq_send, "z", A_PAIR)
    dkv_in = lax.ppermute(dkv_send, "z", B_PAIR)
    slope, pooled = gelu_pool(early, x, dq_send)
    pool_part, s0, s_send = att_join(core, dq_own, dkv_own, dq_in, dkv_in, wh, pooled)
    parts = lax.all_to_all(pool_part, HAX, 0, 0, tiled=True)
    parts, xp = lax.optimization_barrier((parts, xp))
    parts_sib = lax.ppermute(parts, "core", SWAP)
    xp_sib = lax.ppermute(xp, "core", SWAP)
    s1 = lax.ppermute(s_send, "core", SWAP)
    xt0, al0 = turn_input(xp)
    xt1, al1 = turn_input(xp_sib)

    pre, y_send, y0, pool = pre_grads(core, parts, skip, slope)
    y1 = lax.ppermute(y_send, "core", SWAP)
    terms = weight_grads(xt0, al0, xt1, al1, y0, y1, parts, parts_sib, s0, s1)
    got = lax.all_to_all(terms.reshape(32, 24, 2304), SEQ, 0, 0, tiled=True)

    rows, near, next_, first, last = conv_adjoint(par, pre, conv_weight, skip, pool)
    rim1 = lax.ppermute(near, SEQ, NEAR)
    rim2 = lax.ppermute(next_, SEQ, NEXT)

    total = sum_partials(got, rim1, rim2)
    total_far = lax.ppermute(total, "yh", SWAP)
    input_grad = add_edges(par, rows, first, last, rim1, rim2)
    mine = add_pair(total, total_far, input_grad)
    other = lax.ppermute(mine, "core", SWAP)
    conv_grad, proj_grad = place(core, mine, other)
    return input_grad[None], conv_grad, proj_grad


def solution(mesh):
    fine = Mesh(mesh.devices.reshape(2, 2, 2, 4, 4), ("yh", "core", "yl", "x", "z"))
    rows = P(DP, SEQ, None)
    return jax.shard_map(
        local,
        mesh=fine,
        in_specs=(rows, rows, P(), P(), rows, rows, rows, rows),
        out_specs=(rows, P(None, SEQ, None), P(SEQ, None)),
        check_vma=False,
    )
```
